256 devices in a mesh: seq: 64 (over x, z_hi, y, core), dp: 4 (over z_lo).
Axes of the slice: x: 4, y: 4, z: 8 (z_hi: 2, z_lo: 4; z = z_hi * 4 + z_lo), core: 2. Of those that a mesh axis runs over, the one named last changes fastest.
Arguments:
- queries: bfloat16 [4, 8192, 512], P('dp', 'seq'), may hold values from -6 to 6
- keys: bfloat16 [4, 8192, 512], P('dp', 'seq'), may hold values from -6 to 6
- values: bfloat16 [4, 8192, 512], P('dp', 'seq'), may hold values from -6 to 6
- out_weight: bfloat16 [512, 1024], replicated, may hold values from -0.1875 to 0.1875
- ffn_input: bfloat16 [4, 8192, 1024], P('dp', 'seq'), may hold values from -6 to 6
- routes: int32 [4, 8192, 2], P('dp', 'seq'), may hold values from 0 to 63, all different within a row; in each aligned block of 128 rows (0 to 127, 128 to 255, ..., all dimensions but the last counted through in order) at most 8 rows name the same one
- gates: bfloat16 [4, 8192, 2], P('dp', 'seq'), may hold values from 0.19921875 to 1
- up_weight: bfloat16 [64, 1024, 2048], P('seq', 'dp'), may hold values from -0.1875 to 0.1875
- down_weight: bfloat16 [64, 2048, 1024], P('seq', 'dp'), may hold values from -0.125 to 0.125
- out_grad: bfloat16 [4, 8192, 1024], P('dp', 'seq'), may hold values from -6 to 6
Outputs:
- input_grad: bfloat16 [4, 8192, 1024], P('dp', 'seq')
- query_grad: bfloat16 [4, 8192, 512], P('dp', 'seq')
- key_grad: bfloat16 [4, 8192, 512], P('dp', 'seq')
- value_grad: bfloat16 [4, 8192, 512], P('dp', 'seq')
- out_weight_grad: bfloat16 [512, 1024], replicated
- up_grad: bfloat16 [64, 1024, 2048], P('seq', 'dp')
- down_grad: bfloat16 [64, 2048, 1024], P('seq', 'dp')
- gate_grad: float32 [4, 8192, 2], P('dp', 'seq')
The draws below stay inside these ranges and needn't reach their ends.
Inputs may be any that keep to these rules, and one draw needn't show every extreme that they name: `routes`: among the 128 frames of one device (an aligned block), no expert is named more than 8 times, a bound that some block reaches; the two experts of a frame differ.
All inputs are finite; a program needn't handle non-finite values.
Results may differ from the reference program's by a relative error of at most 0.022.
Values may be sent and summed in bfloat16 or wider, within the bound.
No kernel may reach another device: no remote copies, remote signals or barrier semaphores. Data moves between devices by JAX's collectives and lax.ppermute only.
A program may use at most 128 MiB of HBM per device.

```python
import math
import jax
import jax.numpy as jnp
import numpy as np
from jax import lax

D = 1024
INNER = 2048
LOCAL_HEADS = 8
HEAD_SIZE = 64
TOK_DEV = 128
EXPERTS = 64
WINDOWS = 4
WINDOW_FRAMES = 8192
CONTEXT_REACH = 384
SLOT = 8
N_SEQ = 64


def draw_queries(key, part):
    key = jax.random.fold_in(key, 1)
    shape = (WINDOWS, WINDOW_FRAMES, LOCAL_HEADS * HEAD_SIZE)
    field = jnp.clip(jax.random.normal(key, shape, jnp.float32), -6.0, 6.0)
    return field.astype(jnp.bfloat16)


def draw_keys(key, part):
    key = jax.random.fold_in(key, 2)
    shape = (WINDOWS, WINDOW_FRAMES, LOCAL_HEADS * HEAD_SIZE)
    field = jnp.clip(jax.random.normal(key, shape, jnp.float32), -6.0, 6.0)
    return field.astype(jnp.bfloat16)


def levels(rng, dims, shards, smallest, high):
    factor_of = 1.0
    for dim, blocks in shards:
        heights = jax.random.uniform(jax.random.fold_in(jax.random.fold_in(rng, 6), dim), (blocks,), jnp.float32, smallest / len(shards), high / len(shards))
        factor_of = factor_of * jnp.repeat(jnp.exp(heights), dims[dim] // blocks).reshape((-1,) + (1,) * (len(dims) - 1 - dim))
    return factor_of


def routed_block(own_key, own, number, rows, amount, top, reach, slope):
    ranking = jax.random.permutation(own_key, amount)
    crowded, common = shares(amount, rows * top, reach, slope, True), shares(amount, rows * top, reach, slope, False)
    places = jnp.arange(amount)

    def named(sizes, offset_by):
        used = int((sizes > 0).sum())
        fixed = max(1, used // 4)
        moved = fixed + (places - fixed + offset_by * (used - fixed)) % max(1, amount - fixed)
        return jnp.zeros((amount,), jnp.int32).at[ranking[jnp.where(places < fixed, places, moved)]].set(jnp.asarray(sizes, jnp.int32))

    sizes = jnp.where(number % 4 == 0, named(crowded, number // 4), named(common, number - number // 4 - 1))
    mixed = jax.random.permutation(jax.random.fold_in(own, 3), amount)
    giver, sink = mixed[0:amount // 2 * 2:2], mixed[1:amount // 2 * 2:2]
    slack = jnp.minimum(sizes[giver] - 1, reach - sizes[sink]) // 2
    slack = jnp.where((giver == ranking[0]) | (sink == ranking[0]) | (sizes[sink] == 0), 0, jnp.maximum(slack, 0))
    moved = jax.random.randint(jax.random.fold_in(own, 4), (amount // 2,), 0, 1 << 20) % (slack + 1)
    sizes = sizes.at[giver].add(-moved).at[sink].add(moved)
    labels = jnp.searchsorted(jnp.cumsum(sizes), jnp.arange(rows * top), side="right").astype(jnp.int32)
    listing = labels.reshape(top, rows).T
    listing = listing[jax.random.permutation(jax.random.fold_in(own, 1), rows)]
    offset_by = jax.random.randint(jax.random.fold_in(own, 2), (rows, 1), 0, top)
    return jnp.take_along_axis(listing, (jnp.arange(top)[None, :] + offset_by) % top, axis=1)


def shares(number_of, total, bound, lean, full):
    portions = [(1 << 20) // math.isqrt(standing ** lean) + 1 for standing in range(1, number_of + 1)]
    largest = bound if full else min(bound, max(-(-total // number_of), total * portions[0] // sum(portions)))
    least = 1 if total - largest >= number_of - 1 else 0
    counts, rest = [largest] + [least] * (number_of - 1), total - largest - least * (number_of - 1)
    while rest > 0:
        movable = [i for i in range(1, number_of) if counts[i] < largest] or [i for i in range(1, number_of) if counts[i] < bound]
        mass, remaining = sum([portions[i] for i in movable]), rest
        for i in movable:
            addition = min(bound - counts[i], max(1, remaining * portions[i] // mass), rest)
            counts[i] = counts[i] + addition
            rest = rest - addition
    return np.array(counts)


def noise(stream_key, shape, scale, reach, pieces=(), held_as=jnp.bfloat16):
    values = scale * jax.random.normal(stream_key, shape, jnp.float32)
    if pieces:
        values = values * levels(stream_key, shape, pieces, -0.22, 0.18)
    return jnp.clip(values, -reach, reach).astype(held_as)


def setup_inputs(seed: int = 0) -> dict:
    arg_keys = jax.random.split(jax.random.key(seed), 11)
    queries = draw_queries(jax.random.fold_in(arg_keys[10], 71), 0)
    keys = draw_keys(jax.random.fold_in(arg_keys[10], 71), 0)
    values = noise(arg_keys[2], (WINDOWS, WINDOW_FRAMES, LOCAL_HEADS * HEAD_SIZE), 1.0, 6.0, ((0, 4), (1, 64)))
    out_weight = noise(arg_keys[3], (LOCAL_HEADS * HEAD_SIZE, D), D ** -0.5, 0.1875)
    ffn_input = noise(arg_keys[4], (WINDOWS, WINDOW_FRAMES, D), 1.0, 6.0, ((0, 4), (1, 64)))
    routes_keys = jax.random.split(jax.random.fold_in(arg_keys[5], 1), WINDOWS * WINDOW_FRAMES // TOK_DEV)
    routes_turns = jax.random.permutation(jax.random.fold_in(arg_keys[5], 3), WINDOWS * WINDOW_FRAMES // TOK_DEV)
    routes = jax.vmap(lambda own, number: routed_block(jax.random.fold_in(arg_keys[5], 2), own, number, TOK_DEV, EXPERTS, 2, SLOT, 2))(routes_keys, routes_turns).reshape((WINDOWS, WINDOW_FRAMES, 2))
    gates = jnp.clip(0.19921875 + 0.80078125 * jax.random.uniform(arg_keys[6], (WINDOWS, WINDOW_FRAMES, 2), jnp.float32) ** levels(arg_keys[6], (WINDOWS, WINDOW_FRAMES, 2), ((0, 4), (1, 64)), -0.2, 0.2), 0.19921875, 1.0).astype(jnp.bfloat16)
    up_weight = noise(arg_keys[7], (EXPERTS, D, INNER), D ** -0.5, 0.1875, ((0, 64), (1, 4)))
    down_weight = noise(arg_keys[8], (EXPERTS, INNER, D), INNER ** -0.5, 0.125, ((0, 64), (1, 4)))
    out_grad = noise(arg_keys[9], (WINDOWS, WINDOW_FRAMES, D), 1.0, 6.0, ((0, 4), (1, 64)))
    return {"queries": queries, "keys": keys, "values": values, "out_weight": out_weight, "ffn_input": ffn_input, "routes": routes, "gates": gates, "up_weight": up_weight, "down_weight": down_weight, "out_grad": out_grad}


def silu_slope(pre):
    sig = jax.nn.sigmoid(pre)
    return sig * (1.0 + pre * (1.0 - sig))


def attention_window(q_rows, k_rows, value_rows, grad_rows):
    scale = HEAD_SIZE ** -0.5
    block = math.gcd(WINDOW_FRAMES, 512)
    count = WINDOW_FRAMES // block
    reach_rows = block + 2 * CONTEXT_REACH
    qh = q_rows.reshape(WINDOW_FRAMES, LOCAL_HEADS, HEAD_SIZE)
    doh = grad_rows.reshape(WINDOW_FRAMES, LOCAL_HEADS, HEAD_SIZE)
    kpad = jnp.pad(k_rows, ((CONTEXT_REACH, CONTEXT_REACH), (0, 0))).reshape(WINDOW_FRAMES + 2 * CONTEXT_REACH, LOCAL_HEADS, HEAD_SIZE)
    value_padded = jnp.pad(value_rows, ((CONTEXT_REACH, CONTEXT_REACH), (0, 0))).reshape(WINDOW_FRAMES + 2 * CONTEXT_REACH, LOCAL_HEADS, HEAD_SIZE)

    def probs(start_offset):
        qs = lax.dynamic_slice_in_dim(qh, start_offset, block, 0)
        ks = lax.dynamic_slice_in_dim(kpad, start_offset, reach_rows, 0)
        value_slices = lax.dynamic_slice_in_dim(value_padded, start_offset, reach_rows, 0)
        qpos = start_offset + jnp.arange(block, dtype=jnp.int32)
        kpos = start_offset - CONTEXT_REACH + jnp.arange(reach_rows, dtype=jnp.int32)
        mask = (jnp.abs(qpos[:, None] - kpos[None, :]) <= CONTEXT_REACH) & (kpos >= 0)[None, :] & (kpos < WINDOW_FRAMES)[None, :]
        scores = jnp.einsum('qhd,khd->hqk', qs.astype(jnp.float32), ks.astype(jnp.float32)) * scale
        masked = jnp.where(mask[None], scores, -1e30)
        top = jnp.max(masked, axis=2, keepdims=True)
        lse = top + jnp.log(jnp.sum(jnp.exp(masked - top), axis=2, keepdims=True))
        prob = jnp.where(mask[None], jnp.exp(masked - lse), 0.0)
        return qs, ks, value_slices, prob

    def forward(index):
        start_offset = (index * block).astype(jnp.int32)
        qs, ks, value_slices, prob = probs(start_offset)
        prob_b = prob.astype(jnp.bfloat16)
        out = jnp.einsum('hqk,khd->qhd', prob_b.astype(jnp.float32), value_slices.astype(jnp.float32))
        return out.astype(jnp.bfloat16)

    attn_out = lax.map(forward, jnp.arange(count, dtype=jnp.int32)).reshape(WINDOW_FRAMES, LOCAL_HEADS, HEAD_SIZE)

    def backward(carry, index):
        key_acc, value_acc = carry
        start_offset = (index * block).astype(jnp.int32)
        qs, ks, value_slices, prob = probs(start_offset)
        prob_b = prob.astype(jnp.bfloat16)
        dos = lax.dynamic_slice_in_dim(doh, start_offset, block, 0)
        outs = lax.dynamic_slice_in_dim(attn_out, start_offset, block, 0)
        delta = jnp.einsum('qhd,qhd->hq', dos.astype(jnp.float32), outs.astype(jnp.float32))
        dprob = jnp.einsum('qhd,khd->hqk', dos.astype(jnp.float32), value_slices.astype(jnp.float32))
        dscore = (prob * (dprob - delta[:, :, None]) * scale).astype(jnp.bfloat16)
        dq = jnp.einsum('hqk,khd->qhd', dscore.astype(jnp.float32), ks.astype(jnp.float32))
        dk = jnp.einsum('hqk,qhd->khd', dscore.astype(jnp.float32), qs.astype(jnp.float32))
        dv = jnp.einsum('hqk,qhd->khd', prob_b.astype(jnp.float32), dos.astype(jnp.float32))
        key_acc = lax.dynamic_update_slice_in_dim(key_acc, lax.dynamic_slice_in_dim(key_acc, start_offset, reach_rows, 0) + dk, start_offset, 0)
        value_acc = lax.dynamic_update_slice_in_dim(value_acc, lax.dynamic_slice_in_dim(value_acc, start_offset, reach_rows, 0) + dv, start_offset, 0)
        return (key_acc, value_acc), dq.astype(jnp.bfloat16)

    zeros = jnp.zeros((WINDOW_FRAMES + 2 * CONTEXT_REACH, LOCAL_HEADS, HEAD_SIZE), jnp.float32)
    (key_acc, value_acc), dq = lax.scan(backward, (zeros, zeros), jnp.arange(count, dtype=jnp.int32))
    width = LOCAL_HEADS * HEAD_SIZE
    key_grad = key_acc[CONTEXT_REACH:CONTEXT_REACH + WINDOW_FRAMES].reshape(WINDOW_FRAMES, width).astype(jnp.bfloat16)
    value_grad = value_acc[CONTEXT_REACH:CONTEXT_REACH + WINDOW_FRAMES].reshape(WINDOW_FRAMES, width).astype(jnp.bfloat16)
    return attn_out.reshape(WINDOW_FRAMES, width), dq.reshape(WINDOW_FRAMES, width), key_grad, value_grad


def reference(queries, keys, values, out_weight, ffn_input, routes, gates, up_weight, down_weight, out_grad):
    cap = N_SEQ * SLOT
    flat_rows = ffn_input.reshape(WINDOWS * WINDOW_FRAMES, D)
    flat_grad = out_grad.reshape(WINDOWS * WINDOW_FRAMES, D)
    flat_routes = routes.reshape(WINDOWS, WINDOW_FRAMES * 2)
    flat_gates = gates.reshape(WINDOWS * WINDOW_FRAMES * 2)
    slots = jnp.arange(cap, dtype=jnp.int32)

    def per_expert(carry, expert):
        contrib_acc, gate_acc = carry
        w_up = up_weight[expert]
        w_down = down_weight[expert]
        up_total = jnp.zeros((D, INNER), jnp.float32)
        down_total = jnp.zeros((INNER, D), jnp.float32)
        for window in range(WINDOWS):
            hits = flat_routes[window] == expert
            spots = jnp.nonzero(hits, size=cap, fill_value=0)[0].astype(jnp.int32)
            valid = slots < jnp.sum(hits.astype(jnp.int32))
            assign = (window * WINDOW_FRAMES * 2 + spots).astype(jnp.int32)
            frame = assign // 2
            rows = jnp.where(valid[:, None], flat_rows[frame], 0)
            grads = jnp.where(valid[:, None], flat_grad[frame], 0)
            gate = jnp.where(valid, flat_gates[assign], 0)
            pre = jnp.dot(rows, w_up, preferred_element_type=jnp.float32)
            act = jax.nn.silu(pre).astype(jnp.bfloat16)
            expert_out = jnp.dot(act, w_down, preferred_element_type=jnp.float32)
            slot_gate = jnp.sum(grads.astype(jnp.float32) * expert_out, axis=1)
            scaled = (gate.astype(jnp.float32)[:, None] * grads.astype(jnp.float32)).astype(jnp.bfloat16)
            act_grad = jnp.dot(scaled, w_down.T, preferred_element_type=jnp.float32)
            pre_grad = (act_grad * silu_slope(pre)).astype(jnp.bfloat16)
            contrib = jnp.dot(pre_grad, w_up.T, preferred_element_type=jnp.float32)
            up_part = jnp.dot(rows.T, pre_grad, preferred_element_type=jnp.float32).astype(jnp.bfloat16)
            down_part = jnp.dot(act.T, scaled, preferred_element_type=jnp.float32).astype(jnp.bfloat16)
            up_part = lax.optimization_barrier(up_part)
            down_part = lax.optimization_barrier(down_part)
            up_total = up_total + up_part.astype(jnp.float32)
            down_total = down_total + down_part.astype(jnp.float32)
            contrib_acc = contrib_acc.at[frame].add(jnp.where(valid[:, None], contrib, 0.0))
            gate_acc = gate_acc.at[assign].add(jnp.where(valid, slot_gate, 0.0))
        return (contrib_acc, gate_acc), (up_total.astype(jnp.bfloat16), down_total.astype(jnp.bfloat16))

    init = (jnp.zeros((WINDOWS * WINDOW_FRAMES, D), jnp.float32), jnp.zeros((WINDOWS * WINDOW_FRAMES * 2,), jnp.float32))
    (contrib_acc, gate_acc), (up_grad, down_grad) = lax.scan(per_expert, init, jnp.arange(EXPERTS, dtype=jnp.int32))
    input_grad = (flat_grad.astype(jnp.float32) + contrib_acc).astype(jnp.bfloat16).reshape(WINDOWS, WINDOW_FRAMES, D)
    gate_grad = gate_acc.reshape(WINDOWS, WINDOW_FRAMES, 2)
    width = LOCAL_HEADS * HEAD_SIZE
    weight_acc = jnp.zeros((width, D), jnp.float32)
    query_list, key_list, value_list = [], [], []
    for window in range(WINDOWS):
        attn_grad = jnp.dot(input_grad[window], out_weight.T, preferred_element_type=jnp.float32).astype(jnp.bfloat16)
        attn_out, dq, dk, dv = attention_window(queries[window], keys[window], values[window], attn_grad)
        weight_acc = weight_acc + jnp.dot(attn_out.T, input_grad[window], preferred_element_type=jnp.float32)
        query_list.append(dq)
        key_list.append(dk)
        value_list.append(dv)
    return (input_grad, jnp.stack(query_list), jnp.stack(key_list), jnp.stack(value_list),
            weight_acc.astype(jnp.bfloat16), up_grad, down_grad, gate_grad)
```

```python
import functools

import jax
import jax.numpy as jnp
from jax import lax
from jax.experimental import pallas as pl
from jax.experimental.pallas import tpu as pltpu
from jax.sharding import PartitionSpec as P

HEADS = 8
HEAD = 64
SLOT = 8
TOK = 128
WIDTH = HEADS * HEAD
MODEL = 1024
SCALE = HEAD ** (-0.5)
LOW = -1e30
BOTH = ("seq", "dp")
BF = jnp.bfloat16
F32 = jnp.float32


def seq_of(x, zh, y, c):
    return ((x % 4 * 2 + zh) * 4 + y % 4) * 2 + c


PLANES = [[seq_of(x, zh, y, c) for x in range(4) for y in range(4) for c in range(2)] for zh in range(2)]


def along_z(array, move):
    pairs = []
    for x in range(4):
        for y in range(4):
            for c in range(2):
                for z in range(8):
                    to = move(z) % 8
                    pairs.append(
                        (seq_of(x, z // 4, y, c) * 4 + z % 4, seq_of(x, to // 4, y, c) * 4 + to % 4)
                    )
    return lax.ppermute(array, BOTH, pairs)


def seq_permute(array, move):
    size = lax.axis_size("seq")
    pairs = [(i, move(i)) for i in range(size) if 0 <= move(i) < size]
    return lax.ppermute(array, "seq", pairs)


def plane_exchange(array):
    return lax.all_to_all(
        array, "seq", split_axis=0, concat_axis=0, tiled=True, axis_index_groups=PLANES
    )


def after(value, *others):
    return lax.optimization_barrier((value, *others))[0]


def halo(array):
    swap = seq_permute(array, lambda i: i ^ 1)
    left = seq_permute(array, lambda i: i + 2)
    right = seq_permute(array, lambda i: i - 2)
    far = seq_permute(array, lambda i: i + 3 if i % 2 else i - 3)
    rows = array.shape[0]
    swapped = seq_permute(jnp.concatenate([left, right], axis=0), lambda i: i ^ 1)
    return [array, swap, left, swapped[:rows], right, swapped[rows:], far]


def halo_steps(seq):
    core = seq % 2
    steps = jnp.stack(
        [
            jnp.int32(0),
            1 - 2 * core,
            jnp.int32(-2),
            -1 - 2 * core,
            jnp.int32(2),
            3 - 2 * core,
            6 * core - 3,
        ]
    ).astype(jnp.int32)
    there = seq + steps
    real = ((there >= 0) & (there < lax.axis_size("seq"))).astype(jnp.int32)
    return jnp.stack([steps, real])


def dot(left, right, dims=((1,), (0,))):
    return lax.dot_general(left, right, (dims, ((), ())), preferred_element_type=F32)


def dot_nt(left, right):
    return dot(left, right, ((1,), (1,)))


def head_lanes(half):
    lane = lax.broadcasted_iota(jnp.int32, (TOK, 2 * HEAD), 1)
    return (lane < HEAD) if half == 0 else (lane >= HEAD)


def within(steps_ref, b, far_axis):
    own = lax.broadcasted_iota(jnp.int32, (TOK, TOK), 1 - far_axis)
    other = lax.broadcasted_iota(jnp.int32, (TOK, TOK), far_axis)
    gap = other + steps_ref[0, b] * TOK - own
    return (jnp.abs(gap) <= 3 * TOK) & (steps_ref[1, b] == 1)


def fwd_kernel(steps_ref, q_ref, *refs):
    kv = refs[:7]
    shared_ref, lse_ref = refs[7:9]
    lane = lax.broadcasted_iota(jnp.int32, (TOK, TOK), 1)
    lse_all = jnp.zeros((TOK, TOK), F32)
    masks = [within(steps_ref, b, 1) for b in range(7)]
    shared_ref[0:TOK, 0:WIDTH] = q_ref[...]
    for pair in range(HEADS // 2):
        cols = slice(pair * 128, pair * 128 + 128)
        vcols = slice(WIDTH + pair * 128, WIDTH + pair * 128 + 128)
        q_pair = q_ref[:, cols]
        outs = []
        for half in range(2):
            q_head = jnp.where(head_lanes(half), q_pair, jnp.zeros((), BF))
            scores = [
                jnp.where(masks[b], dot_nt(q_head, kv[b][:, cols]) * SCALE, LOW) for b in range(7)
            ]
            top = functools.reduce(jnp.maximum, scores)
            top = jnp.max(top, axis=1, keepdims=True)
            exps = [jnp.exp(s - top) for s in scores]
            total = jnp.sum(functools.reduce(jnp.add, exps), axis=1, keepdims=True)
            inv = 1.0 / total
            acc = jnp.zeros((TOK, 128), F32)
            for b in range(7):
                acc = acc + dot((exps[b] * inv).astype(BF), kv[b][:, vcols])
            outs.append(acc)
            lse_all = jnp.where(lane == 2 * pair + half, top + jnp.log(total), lse_all)
        shared_ref[0:TOK, vcols] = jnp.where(head_lanes(0), outs[0], outs[1]).astype(BF)
    lse_ref[...] = lse_all
    rows = jnp.transpose(lse_all)[0:16]
    high = rows.astype(BF)
    rows = rows - high.astype(F32)
    mid = rows.astype(BF)
    low = (rows - mid.astype(F32)).astype(BF)
    shared_ref[TOK : TOK + 16, :] = jnp.concatenate(
        [high, mid, low, jnp.zeros((16, MODEL - 3 * TOK), BF)], axis=1
    )


def query_kernel(steps_ref, shared_ref, lse_ref, do_ref, *refs):
    kv = refs[:7]
    dq_ref = refs[7]
    masks = [within(steps_ref, b, 1) for b in range(7)]
    lse_all = lse_ref[...]
    for pair in range(HEADS // 2):
        cols = slice(pair * 128, pair * 128 + 128)
        vcols = slice(WIDTH + pair * 128, WIDTH + pair * 128 + 128)
        q_pair = shared_ref[0:TOK, cols]
        do_pair = do_ref[:, cols]
        prod = do_pair.astype(F32) * shared_ref[0:TOK, vcols].astype(F32)
        outs = []
        for half in range(2):
            lanes = head_lanes(half)
            q_head = jnp.where(lanes, q_pair, jnp.zeros((), BF))
            do_head = jnp.where(lanes, do_pair, jnp.zeros((), BF))
            delta = jnp.sum(jnp.where(lanes, prod, 0.0), axis=1, keepdims=True)
            lse = lse_all[:, 2 * pair + half : 2 * pair + half + 1]
            acc = jnp.zeros((TOK, 128), F32)
            for b in range(7):
                score = dot_nt(q_head, kv[b][:, cols]) * SCALE - lse
                prob = jnp.exp(jnp.where(masks[b], score, LOW))
                dprob = dot_nt(do_head, kv[b][:, vcols])
                dscore = (prob * (dprob - delta) * SCALE).astype(BF)
                acc = acc + dot(dscore, kv[b][:, cols])
            outs.append(acc)
        dq_ref[:, cols] = jnp.where(head_lanes(0), outs[0], outs[1]).astype(BF)


def key_kernel(steps_ref, kv_ref, *refs):
    shared = refs[:7]
    do = refs[7:14]
    dk_ref, dv_ref, lse_scr, delta_scr = refs[14:18]
    masks = [within(steps_ref, b, 1) for b in range(7)]
    row = lax.broadcasted_iota(jnp.int32, (16, WIDTH), 0)
    col = lax.broadcasted_iota(jnp.int32, (16, WIDTH), 1)
    pick = ((col >= row * HEAD) & (col < row * HEAD + HEAD)).astype(BF)
    for b in range(7):
        tail = shared[b][TOK : TOK + 16, 0 : 3 * TOK].astype(F32)
        lse_scr[b] = tail[:, 0:TOK] + tail[:, TOK : 2 * TOK] + tail[:, 2 * TOK :]
        prod = do[b][...].astype(F32) * shared[b][0:TOK, WIDTH:].astype(F32)
        high = prod.astype(BF)
        prod = prod - high.astype(F32)
        mid = prod.astype(BF)
        low = (prod - mid.astype(F32)).astype(BF)
        delta_scr[b] = dot_nt(pick, high) + dot_nt(pick, mid) + dot_nt(pick, low)
    for pair in range(HEADS // 2):
        cols = slice(pair * 128, pair * 128 + 128)
        vcols = slice(WIDTH + pair * 128, WIDTH + pair * 128 + 128)
        k_pair = kv_ref[:, cols]
        v_pair = kv_ref[:, vcols]
        dks, dvs = [], []
        for half in range(2):
            head = 2 * pair + half
            lanes = head_lanes(half)
            k_head = jnp.where(lanes, k_pair, jnp.zeros((), BF))
            v_head = jnp.where(lanes, v_pair, jnp.zeros((), BF))
            dk = jnp.zeros((TOK, 128), F32)
            dv = jnp.zeros((TOK, 128), F32)
            for b in range(7):
                q_b = shared[b][0:TOK, cols]
                do_b = do[b][:, cols]
                score = dot_nt(k_head, q_b) * SCALE - lse_scr[b, head : head + 1, :]
                prob = jnp.exp(jnp.where(masks[b], score, LOW))
                dprob = dot_nt(v_head, do_b)
                dscore = (prob * (dprob - delta_scr[b, head : head + 1, :]) * SCALE).astype(BF)
                dk = dk + dot(dscore, q_b)
                dv = dv + dot(prob.astype(BF), do_b)
            dks.append(dk)
            dvs.append(dv)
        dk_ref[:, cols] = jnp.where(head_lanes(0), dks[0], dks[1]).astype(BF)
        dv_ref[:, cols] = jnp.where(head_lanes(0), dvs[0], dvs[1]).astype(BF)


def on_chip(body, outs, n_in, scratch=()):
    return pl.pallas_call(
        body,
        out_shape=outs,
        in_specs=[pl.BlockSpec(memory_space=pltpu.SMEM)]
        + [pl.BlockSpec(memory_space=pltpu.VMEM)] * (n_in - 1),
        out_specs=[pl.BlockSpec(memory_space=pltpu.VMEM)] * len(outs),
        scratch_shapes=list(scratch),
        compiler_params=pltpu.CompilerParams(vmem_limit_bytes=24 * 1024 * 1024),
        cost_estimate=pl.CostEstimate(flops=10**9, bytes_accessed=6 * 10**6, transcendentals=10**6),
    )


def attn_forward(steps, q, kv):
    outs = [
        jax.ShapeDtypeStruct((TOK + 16, MODEL), BF),
        jax.ShapeDtypeStruct((TOK, TOK), F32),
    ]
    return on_chip(fwd_kernel, outs, 9)(steps, q, *kv)


def attn_queries(steps, shared, lse, do, kv):
    outs = [jax.ShapeDtypeStruct((TOK, WIDTH), BF)]
    return on_chip(query_kernel, outs, 11)(steps, shared, lse, do, *kv)[0]


def attn_keys(steps, kv, shared, do):
    outs = [jax.ShapeDtypeStruct((TOK, WIDTH), BF)] * 2
    scratch = [pltpu.VMEM((7, 16, TOK), F32), pltpu.VMEM((7, 16, TOK), F32)]
    return on_chip(key_kernel, outs, 16, scratch)(steps, kv, *shared, *do)


def silu_slope(pre):
    sig = jax.nn.sigmoid(pre)
    return sig * (1.0 + pre * (1.0 - sig))


def per_device(
    queries, keys, values, out_weight, ffn_input, routes, gates, up_weight, down_weight, out_grad
):
    seq = lax.axis_index("seq")
    dp = lax.axis_index("dp")
    z_hi = (seq // 8) % 2
    tok, model = ffn_input.shape[1:]
    n_seq = lax.axis_size("seq")
    plane = n_seq // 2
    frames = ffn_input[0]
    cotan = out_grad[0]

    with jax.named_scope("meta"):
        chosen = routes[0].T.reshape(1, 2 * tok)
        named = chosen == jnp.arange(n_seq, dtype=jnp.int32)[:, None]
        order = jnp.arange(2 * tok)
        before = (order[:, None] < order[None, :]).astype(BF)
        counts = dot(named.astype(BF), before)
        rank = jnp.sum(jnp.where(named, counts, 0.0), axis=0, keepdims=True)
        note = jnp.concatenate(
            [
                chosen.astype(BF),
                rank.astype(BF),
                gates[0].T.reshape(1, 2 * tok),
                jnp.zeros((1, 2 * tok), BF),
            ],
            axis=1,
        )
        payload = jnp.concatenate([frames, note, jnp.zeros((15, model), BF), cotan], axis=0)
    n_x = tok + 16
    with jax.named_scope("tokens_z"):
        above = along_z(payload, lambda z: z - 2)
        below = along_z(payload, lambda z: z + 2)
        across_x = along_z(above[:n_x], lambda z: z - 2)
        across_g = along_z(below[n_x:], lambda z: z + 2)

    with jax.named_scope("weights_z"):
        half = dp // 2
        up_mine = lax.dynamic_slice(up_weight[0], (0, half * 1024), (256, 1024))
        up_other = lax.dynamic_slice(up_weight[0], (0, (1 - half) * 1024), (256, 1024))
        pack = jnp.concatenate([up_mine, down_weight[0]], axis=0)
        pack, up_other, _, _ = lax.optimization_barrier((pack, up_other, above, below))
        pack1 = along_z(pack, lambda z: z ^ 1)
        up_3 = along_z(up_other, lambda z: z ^ 3)
        up_2 = along_z(up_other, lambda z: z ^ 2)
        up_parts = [up_mine, pack1[:256], up_2, up_3]
        down_parts = [down_weight[0], pack1[256:]]

    def rows_of(note_row, stride, offset):
        expert = note_row[0, : 2 * tok].astype(jnp.int32)
        place = (expert // 16) * 8 + expert % 8
        here = (expert // 8) % 2 == z_hi
        row = place * stride + offset + note_row[0, 2 * tok : 4 * tok].astype(jnp.int32)
        row = jnp.where(here, row, -1).reshape(2, tok)
        return row, note_row[0, 4 * tok : 6 * tok].reshape(2, tok)

    def placing(row, total):
        spots = jnp.arange(total, dtype=jnp.int32)[:, None]
        return [spots == row[t][None, :] for t in range(2)]

    def merged(hits, gate=None):
        if gate is None:
            return (hits[0] | hits[1]).astype(BF)
        zero = jnp.zeros((), BF)
        return jnp.where(hits[0], gate[0][None, :], jnp.where(hits[1], gate[1][None, :], zero))

    class Sets:
        def __init__(self, notes, xs, gs):
            n = len(notes)
            self.n = n
            found = [rows_of(note_row, n * SLOT, k * SLOT) for k, note_row in enumerate(notes)]
            self.hits = placing(jnp.concatenate([f[0] for f in found], axis=1), plane * n * SLOT)
            self.gate = jnp.concatenate([f[1] for f in found], axis=1)
            self.place = merged(self.hits)
            self.x = xs[0] if n == 1 else jnp.concatenate(xs, axis=0)
            self.g = gs[0] if n == 1 else jnp.concatenate(gs, axis=0)

        def packed(self):
            shape = (plane, self.n * SLOT, model)
            send_x = dot(self.place, self.x).astype(BF).reshape(shape)
            send_g = dot(merged(self.hits, self.gate), self.g).astype(BF).reshape(shape)
            return jnp.concatenate([send_x, send_g], axis=1)

        def split(self, got):
            cut = self.n * SLOT
            return got[:, :cut].reshape(-1, model), got[:, cut:].reshape(-1, model)

        def unpacked(self, returned):
            return dot(self.place, returned.reshape(-1, model), ((0,), (0,)))

        def gate_values(self, values):
            column = values.reshape(-1, 1)
            return jnp.stack([jnp.sum(jnp.where(h, column, 0.0), axis=0) for h in self.hits])

    with jax.named_scope("out_own"):
        own = Sets([note], [frames], [cotan])
        got_own = plane_exchange(own.packed())
    with jax.named_scope("out_near"):
        near = Sets(
            [above[tok : tok + 1], below[tok : tok + 1]],
            [above[:tok], below[:tok]],
            [above[n_x:], below[n_x:]],
        )
        got_near = plane_exchange(after(near.packed(), got_own))
    with jax.named_scope("out_across"):
        across = Sets([across_x[tok : tok + 1]], [across_x[:tok]], [across_g])
        got_across = plane_exchange(after(across.packed(), got_near))

    with jax.named_scope("attn_fwd"):
        steps = halo_steps(seq)
        kv_own = jnp.concatenate([keys[0], values[0]], axis=1)
        kv = halo(after(kv_own, across_x, across_g, pack1))
        shared_own, lse = attn_forward(steps, queries[0], kv)
        shared = halo(shared_own)

    with jax.named_scope("experts"):
        w_up = jnp.zeros((1024, 1024), BF)
        for j, part in enumerate(up_parts):
            w_up = lax.dynamic_update_slice(w_up, part, ((dp ^ j) * 256, 0))
        w_down = jnp.zeros((1024, 1024), BF)
        for j, part in enumerate(down_parts):
            w_down = lax.dynamic_update_slice(w_down, part, (((dp ^ j) % 2) * 512, 0))
        sets = [near, across, own]
        pieces = [s.split(got) for s, got in zip(sets, [got_near, got_across, got_own])]
        x_rows = jnp.concatenate([p[0] for p in pieces], axis=0)
        g_rows = jnp.concatenate([p[1] for p in pieces], axis=0)
        pre = dot(x_rows, w_up)
        act = jax.nn.silu(pre).astype(BF)
        act_grad = dot_nt(g_rows, w_down)
        slot_gate = jnp.sum(act.astype(F32) * act_grad, axis=1)
        pre_grad = (act_grad * silu_slope(pre)).astype(BF)
        back = dot_nt(pre_grad, w_up).astype(BF)
    size = plane * SLOT
    with jax.named_scope("back"):
        ret_near = plane_exchange(back[: 2 * size].reshape(plane, 2 * SLOT, model))
        ret_across = plane_exchange(
            after(back[2 * size : 3 * size].reshape(plane, SLOT, model), ret_near)
        )
        ret_own = plane_exchange(after(back[3 * size :].reshape(plane, SLOT, model), ret_across))
        near_sum = near.unpacked(ret_near).astype(BF)
        from_below = along_z(near_sum[:tok], lambda z: z + 2)
        from_above = along_z(near_sum[tok:], lambda z: z - 2)
        from_across = along_z(across.unpacked(ret_across).astype(BF), lambda z: z + 4)
        total = cotan.astype(F32) + own.unpacked(ret_own)
        total = total + from_below.astype(F32) + from_above.astype(F32) + from_across.astype(F32)
        input_grad = total.astype(BF)

    with jax.named_scope("weight_grads"):
        down_term = dot(act, g_rows, ((0,), (0,))).astype(BF)

        def down_part(j):
            return lax.dynamic_slice(down_term, (((dp ^ j) % 2) * 512, 0), (512, model))

        down_grad = down_part(0).astype(F32) + along_z(down_part(1), lambda z: z ^ 1).astype(F32)
        down_grad = down_grad.astype(BF)
        up_term = dot(x_rows, pre_grad, ((0,), (0,))).astype(BF)
        up_term = after(up_term, from_across)

        def up_part(j):
            return lax.dynamic_slice(up_term, ((dp ^ j) * 256, 0), (256, 1024))

        same = up_part(0).astype(F32) + along_z(up_part(1), lambda z: z ^ 1).astype(F32)
        opposite = along_z(up_part(2), lambda z: z ^ 2).astype(F32) + along_z(
            up_part(3), lambda z: z ^ 3
        ).astype(F32)
        first = jnp.where(half == 0, same, opposite).astype(BF)
        second = jnp.where(half == 0, opposite, same).astype(BF)
        up_grad = jnp.concatenate([first, second], axis=1)

    with jax.named_scope("attn_bwd"):
        attn_grad = dot_nt(input_grad, out_weight).astype(BF)
        do = halo(attn_grad)
        weight_term = dot(shared_own[:tok, WIDTH:], input_grad, ((0,), (0,))).astype(BF)

    with jax.named_scope("out_weight"):
        rows = WIDTH // plane
        parts = plane_exchange(weight_term.reshape(plane, rows, model))
        part = jnp.sum(parts.astype(F32), axis=0)
        part_b = part.astype(BF)
        for k in (1, 2, 3):
            part = part + along_z(part_b, lambda z, k=k: z ^ k).astype(F32)
        part_b = part.astype(BF)
        part = part_b.astype(F32) + along_z(part_b, lambda z: z + 4).astype(F32)
        whole = jnp.broadcast_to(part.astype(BF)[None], (plane, rows, model))
        out_weight_grad = plane_exchange(whole).reshape(WIDTH, model)

    with jax.named_scope("gate_back"):
        gate_pack = jnp.concatenate(
            [
                slot_gate[: 2 * size].reshape(plane, 2 * SLOT),
                slot_gate[2 * size : 3 * size].reshape(plane, SLOT),
                slot_gate[3 * size :].reshape(plane, SLOT),
            ],
            axis=1,
        ).astype(BF)
        ret_gate = plane_exchange(after(gate_pack, parts)).astype(F32)
        near_gate = near.gate_values(ret_gate[:, : 2 * SLOT]).astype(BF)
        across_gate = across.gate_values(ret_gate[:, 2 * SLOT : 3 * SLOT]).astype(BF)
        gate_sum = own.gate_values(ret_gate[:, 3 * SLOT :])
        gate_sum = gate_sum + along_z(near_gate[:, :tok], lambda z: z + 2).astype(F32)
        gate_sum = gate_sum + along_z(near_gate[:, tok:], lambda z: z - 2).astype(F32)
        gate_sum = gate_sum + along_z(across_gate, lambda z: z + 4).astype(F32)
        gate_grad = gate_sum.T / gates[0].astype(F32)

    with jax.named_scope("attn_bwd"):
        query_grad = attn_queries(steps, shared_own, lse, attn_grad, kv)
        key_grad, value_grad = attn_keys(steps, kv_own, shared, do)

    return (
        input_grad[None],
        query_grad[None],
        key_grad[None],
        value_grad[None],
        out_weight_grad,
        up_grad[None],
        down_grad[None],
        gate_grad[None],
    )


def solution(mesh):
    rows = P("dp", "seq", None)
    weights = P("seq", "dp", None)
    return jax.shard_map(
        per_device,
        mesh=mesh,
        in_specs=(rows, rows, rows, P(), rows, rows, rows, weights, weights, rows),
        out_specs=(rows, rows, rows, rows, P(), weights, weights, rows),
        check_vma=False,
    )
```

```python
import functools

import jax
import jax.numpy as jnp
from jax import lax
from jax.experimental import pallas as pl
from jax.experimental.pallas import tpu as pltpu
from jax.sharding import PartitionSpec as P

HEADS = 8
HEAD = 64
SLOT = 8
TOK = 128
WIDTH = HEADS * HEAD
MODEL = 1024
SCALE = HEAD ** (-0.5)
LOW = -1e30
BOTH = ("seq", "dp")
BF = jnp.bfloat16
F32 = jnp.float32


def seq_of(x, zh, y, c):
    return ((x % 4 * 2 + zh) * 4 + y % 4) * 2 + c


PLANES = [[seq_of(x, zh, y, c) for x in range(4) for y in range(4) for c in range(2)] for zh in range(2)]


def along_z(array, move):
    pairs = []
    for x in range(4):
        for y in range(4):
            for c in range(2):
                for z in range(8):
                    to = move(z) % 8
                    pairs.append(
                        (seq_of(x, z // 4, y, c) * 4 + z % 4, seq_of(x, to // 4, y, c) * 4 + to % 4)
                    )
    return lax.ppermute(array, BOTH, pairs)


def seq_permute(array, move):
    size = lax.axis_size("seq")
    pairs = [(i, move(i)) for i in range(size) if 0 <= move(i) < size]
    return lax.ppermute(array, "seq", pairs)


def plane_exchange(array):
    return lax.all_to_all(
        array, "seq", split_axis=0, concat_axis=0, tiled=True, axis_index_groups=PLANES
    )


def after(value, *others):
    return lax.optimization_barrier((value, *others))[0]


def halo(array):
    swap = seq_permute(array, lambda i: i ^ 1)
    left = seq_permute(array, lambda i: i + 2)
    right = seq_permute(array, lambda i: i - 2)
    far = seq_permute(array, lambda i: i + 3 if i % 2 else i - 3)
    rows = array.shape[0]
    swapped = seq_permute(jnp.concatenate([left, right], axis=0), lambda i: i ^ 1)
    return [array, swap, left, swapped[:rows], right, swapped[rows:], far]


def halo_steps(seq):
    core = seq % 2
    steps = jnp.stack(
        [
            jnp.int32(0),
            1 - 2 * core,
            jnp.int32(-2),
            -1 - 2 * core,
            jnp.int32(2),
            3 - 2 * core,
            6 * core - 3,
        ]
    ).astype(jnp.int32)
    there = seq + steps
    real = ((there >= 0) & (there < lax.axis_size("seq"))).astype(jnp.int32)
    return jnp.stack([steps, real])


def dot(left, right, dims=((1,), (0,))):
    return lax.dot_general(left, right, (dims, ((), ())), preferred_element_type=F32)


def dot_nt(left, right):
    return dot(left, right, ((1,), (1,)))


def head_lanes(half):
    lane = lax.broadcasted_iota(jnp.int32, (TOK, 2 * HEAD), 1)
    return (lane < HEAD) if half == 0 else (lane >= HEAD)


def within(steps_ref, b, far_axis):
    own = lax.broadcasted_iota(jnp.int32, (TOK, TOK), 1 - far_axis)
    other = lax.broadcasted_iota(jnp.int32, (TOK, TOK), far_axis)
    gap = other + steps_ref[0, b] * TOK - own
    return (jnp.abs(gap) <= 3 * TOK) & (steps_ref[1, b] == 1)


def fwd_kernel(steps_ref, q_ref, *refs):
    kv = refs[:7]
    shared_ref, lse_ref = refs[7:9]
    lane = lax.broadcasted_iota(jnp.int32, (TOK, TOK), 1)
    lse_all = jnp.zeros((TOK, TOK), F32)
    masks = [within(steps_ref, b, 1) for b in range(7)]
    shared_ref[0:TOK, 0:WIDTH] = q_ref[...]
    for pair in range(HEADS // 2):
        cols = slice(pair * 128, pair * 128 + 128)
        vcols = slice(WIDTH + pair * 128, WIDTH + pair * 128 + 128)
        q_pair = q_ref[:, cols]
        outs = []
        for half in range(2):
            q_head = jnp.where(head_lanes(half), q_pair, jnp.zeros((), BF))
            scores = [
                jnp.where(masks[b], dot_nt(q_head, kv[b][:, cols]) * SCALE, LOW) for b in range(7)
            ]
            top = functools.reduce(jnp.maximum, scores)
            top = jnp.max(top, axis=1, keepdims=True)
            exps = [jnp.exp(s - top) for s in scores]
            total = jnp.sum(functools.reduce(jnp.add, exps), axis=1, keepdims=True)
            inv = 1.0 / total
            acc = jnp.zeros((TOK, 128), F32)
            for b in range(7):
                acc = acc + dot((exps[b] * inv).astype(BF), kv[b][:, vcols])
            outs.append(acc)
            lse_all = jnp.where(lane == 2 * pair + half, top + jnp.log(total), lse_all)
        shared_ref[0:TOK, vcols] = jnp.where(head_lanes(0), outs[0], outs[1]).astype(BF)
    lse_ref[...] = lse_all
    rows = jnp.transpose(lse_all)[0:16]
    high = rows.astype(BF)
    rows = rows - high.astype(F32)
    mid = rows.astype(BF)
    low = (rows - mid.astype(F32)).astype(BF)
    shared_ref[TOK : TOK + 16, :] = jnp.concatenate(
        [high, mid, low, jnp.zeros((16, MODEL - 3 * TOK), BF)], axis=1
    )


def query_kernel(steps_ref, shared_ref, lse_ref, do_ref, *refs):
    kv = refs[:7]
    dq_ref = refs[7]
    masks = [within(steps_ref, b, 1) for b in range(7)]
    lse_all = lse_ref[...]
    for pair in range(HEADS // 2):
        cols = slice(pair * 128, pair * 128 + 128)
        vcols = slice(WIDTH + pair * 128, WIDTH + pair * 128 + 128)
        q_pair = shared_ref[0:TOK, cols]
        do_pair = do_ref[:, cols]
        prod = do_pair.astype(F32) * shared_ref[0:TOK, vcols].astype(F32)
        outs = []
        for half in range(2):
            lanes = head_lanes(half)
            q_head = jnp.where(lanes, q_pair, jnp.zeros((), BF))
            do_head = jnp.where(lanes, do_pair, jnp.zeros((), BF))
            delta = jnp.sum(jnp.where(lanes, prod, 0.0), axis=1, keepdims=True)
            lse = lse_all[:, 2 * pair + half : 2 * pair + half + 1]
            acc = jnp.zeros((TOK, 128), F32)
            for b in range(7):
                score = dot_nt(q_head, kv[b][:, cols]) * SCALE - lse
                prob = jnp.exp(jnp.where(masks[b], score, LOW))
                dprob = dot_nt(do_head, kv[b][:, vcols])
                dscore = (prob * (dprob - delta) * SCALE).astype(BF)
                acc = acc + dot(dscore, kv[b][:, cols])
            outs.append(acc)
        dq_ref[:, cols] = jnp.where(head_lanes(0), outs[0], outs[1]).astype(BF)


def key_kernel(steps_ref, kv_ref, *refs):
    shared = refs[:7]
    do = refs[7:14]
    dk_ref, dv_ref, lse_scr, delta_scr = refs[14:18]
    masks = [within(steps_ref, b, 1) for b in range(7)]
    row = lax.broadcasted_iota(jnp.int32, (16, WIDTH), 0)
    col = lax.broadcasted_iota(jnp.int32, (16, WIDTH), 1)
    pick = ((col >= row * HEAD) & (col < row * HEAD + HEAD)).astype(BF)
    for b in range(7):
        tail = shared[b][TOK : TOK + 16, 0 : 3 * TOK].astype(F32)
        lse_scr[b] = tail[:, 0:TOK] + tail[:, TOK : 2 * TOK] + tail[:, 2 * TOK :]
        prod = do[b][...].astype(F32) * shared[b][0:TOK, WIDTH:].astype(F32)
        high = prod.astype(BF)
        prod = prod - high.astype(F32)
        mid = prod.astype(BF)
        low = (prod - mid.astype(F32)).astype(BF)
        delta_scr[b] = dot_nt(pick, high) + dot_nt(pick, mid) + dot_nt(pick, low)
    for pair in range(HEADS // 2):
        cols = slice(pair * 128, pair * 128 + 128)
        vcols = slice(WIDTH + pair * 128, WIDTH + pair * 128 + 128)
        k_pair = kv_ref[:, cols]
        v_pair = kv_ref[:, vcols]
        dks, dvs = [], []
        for half in range(2):
            head = 2 * pair + half
            lanes = head_lanes(half)
            k_head = jnp.where(lanes, k_pair, jnp.zeros((), BF))
            v_head = jnp.where(lanes, v_pair, jnp.zeros((), BF))
            dk = jnp.zeros((TOK, 128), F32)
            dv = jnp.zeros((TOK, 128), F32)
            for b in range(7):
                q_b = shared[b][0:TOK, cols]
                do_b = do[b][:, cols]
                score = dot_nt(k_head, q_b) * SCALE - lse_scr[b, head : head + 1, :]
                prob = jnp.exp(jnp.where(masks[b], score, LOW))
                dprob = dot_nt(v_head, do_b)
                dscore = (prob * (dprob - delta_scr[b, head : head + 1, :]) * SCALE).astype(BF)
                dk = dk + dot(dscore, q_b)
                dv = dv + dot(prob.astype(BF), do_b)
            dks.append(dk)
            dvs.append(dv)
        dk_ref[:, cols] = jnp.where(head_lanes(0), dks[0], dks[1]).astype(BF)
        dv_ref[:, cols] = jnp.where(head_lanes(0), dvs[0], dvs[1]).astype(BF)


def on_chip(body, outs, n_in, scratch=()):
    return pl.pallas_call(
        body,
        out_shape=outs,
        in_specs=[pl.BlockSpec(memory_space=pltpu.SMEM)]
        + [pl.BlockSpec(memory_space=pltpu.VMEM)] * (n_in - 1),
        out_specs=[pl.BlockSpec(memory_space=pltpu.VMEM)] * len(outs),
        scratch_shapes=list(scratch),
        compiler_params=pltpu.CompilerParams(vmem_limit_bytes=24 * 1024 * 1024),
        cost_estimate=pl.CostEstimate(flops=10**9, bytes_accessed=6 * 10**6, transcendentals=10**6),
    )


def attn_forward(steps, q, kv):
    outs = [
        jax.ShapeDtypeStruct((TOK + 16, MODEL), BF),
        jax.ShapeDtypeStruct((TOK, TOK), F32),
    ]
    return on_chip(fwd_kernel, outs, 9)(steps, q, *kv)


def attn_queries(steps, shared, lse, do, kv):
    outs = [jax.ShapeDtypeStruct((TOK, WIDTH), BF)]
    return on_chip(query_kernel, outs, 11)(steps, shared, lse, do, *kv)[0]


def attn_keys(steps, kv, shared, do):
    outs = [jax.ShapeDtypeStruct((TOK, WIDTH), BF)] * 2
    scratch = [pltpu.VMEM((7, 16, TOK), F32), pltpu.VMEM((7, 16, TOK), F32)]
    return on_chip(key_kernel, outs, 16, scratch)(steps, kv, *shared, *do)


def silu_slope(pre):
    sig = jax.nn.sigmoid(pre)
    return sig * (1.0 + pre * (1.0 - sig))


def per_device(
    queries, keys, values, out_weight, ffn_input, routes, gates, up_weight, down_weight, out_grad
):
    seq = lax.axis_index("seq")
    dp = lax.axis_index("dp")
    z_hi = (seq // 8) % 2
    tok, model = ffn_input.shape[1:]
    n_seq = lax.axis_size("seq")
    plane = n_seq // 2
    frames = ffn_input[0]
    cotan = out_grad[0]

    with jax.named_scope("meta"):
        chosen = routes[0].T.reshape(1, 2 * tok)
        named = chosen == jnp.arange(n_seq, dtype=jnp.int32)[:, None]
        order = jnp.arange(2 * tok)
        before = (order[:, None] < order[None, :]).astype(BF)
        counts = dot(named.astype(BF), before)
        rank = jnp.sum(jnp.where(named, counts, 0.0), axis=0, keepdims=True)
        note = jnp.concatenate(
            [
                chosen.astype(BF),
                rank.astype(BF),
                gates[0].T.reshape(1, 2 * tok),
                jnp.zeros((1, 2 * tok), BF),
            ],
            axis=1,
        )
        payload = jnp.concatenate([frames, note, jnp.zeros((15, model), BF), cotan], axis=0)
    n_x = tok + 16
    with jax.named_scope("tokens_z"):
        above = along_z(payload, lambda z: z - 2)
        below = along_z(payload, lambda z: z + 2)
        across_x = along_z(above[:n_x], lambda z: z - 2)
        across_g = along_z(below[n_x:], lambda z: z + 2)

    with jax.named_scope("weights_z"):
        half = dp // 2
        up_mine = lax.dynamic_slice(up_weight[0], (0, half * 1024), (256, 1024))
        up_other = lax.dynamic_slice(up_weight[0], (0, (1 - half) * 1024), (256, 1024))
        pack = jnp.concatenate([up_mine, down_weight[0]], axis=0)
        pack, up_other, _, _ = lax.optimization_barrier((pack, up_other, across_x, across_g))
        pack1 = along_z(pack, lambda z: z ^ 1)
        up_first = [along_z(up_other[:128], lambda z, j=j: z ^ j) for j in (2, 3)]
        up_second = after(up_other[128:], *up_first)
        up_second = [along_z(up_second, lambda z, j=j: z ^ j) for j in (2, 3)]

    def rows_of(note_row, stride, offset):
        expert = note_row[0, : 2 * tok].astype(jnp.int32)
        place = (expert // 16) * 8 + expert % 8
        here = (expert // 8) % 2 == z_hi
        row = place * stride + offset + note_row[0, 2 * tok : 4 * tok].astype(jnp.int32)
        row = jnp.where(here, row, -1).reshape(2, tok)
        return row, note_row[0, 4 * tok : 6 * tok].reshape(2, tok)

    def placing(row, total):
        spots = jnp.arange(total, dtype=jnp.int32)[:, None]
        return [spots == row[t][None, :] for t in range(2)]

    def merged(hits, gate=None):
        if gate is None:
            return (hits[0] | hits[1]).astype(BF)
        zero = jnp.zeros((), BF)
        return jnp.where(hits[0], gate[0][None, :], jnp.where(hits[1], gate[1][None, :], zero))

    class Sets:
        def __init__(self, notes, xs, gs):
            n = len(notes)
            self.n = n
            found = [rows_of(note_row, n * SLOT, k * SLOT) for k, note_row in enumerate(notes)]
            self.hits = placing(jnp.concatenate([f[0] for f in found], axis=1), plane * n * SLOT)
            self.gate = jnp.concatenate([f[1] for f in found], axis=1)
            self.place = merged(self.hits)
            self.x = xs[0] if n == 1 else jnp.concatenate(xs, axis=0)
            self.g = gs[0] if n == 1 else jnp.concatenate(gs, axis=0)

        def packed(self):
            shape = (plane, self.n * SLOT, model)
            send_x = dot(self.place, self.x).astype(BF).reshape(shape)
            send_g = dot(merged(self.hits, self.gate), self.g).astype(BF).reshape(shape)
            return jnp.concatenate([send_x, send_g], axis=1)

        def split(self, got):
            cut = self.n * SLOT
            return got[:, :cut].reshape(-1, model), got[:, cut:].reshape(-1, model)

        def unpacked(self, returned):
            return dot(self.place, returned.reshape(-1, model), ((0,), (0,)))

        def gate_values(self, values):
            column = values.reshape(-1, 1)
            return jnp.stack([jnp.sum(jnp.where(h, column, 0.0), axis=0) for h in self.hits])

    with jax.named_scope("out_own"):
        own = Sets([note], [frames], [cotan])
        got_own = plane_exchange(own.packed())
    with jax.named_scope("out_near"):
        near = Sets(
            [above[tok : tok + 1], below[tok : tok + 1]],
            [above[:tok], below[:tok]],
            [above[n_x:], below[n_x:]],
        )
        got_near = plane_exchange(after(near.packed(), got_own, across_x, across_g))
    with jax.named_scope("out_across"):
        across = Sets([across_x[tok : tok + 1]], [across_x[:tok]], [across_g])
        got_across = plane_exchange(after(across.packed(), got_near, *up_first))

    with jax.named_scope("attn_fwd"):
        steps = halo_steps(seq)
        kv_own = jnp.concatenate([keys[0], values[0]], axis=1)
        pack1, *up_second = lax.optimization_barrier((pack1, *up_second, got_across))[:3]
        up_parts = [(up_mine, 0, 0), (pack1[:256], 1, 0)]
        up_parts += [(up_first[i], 2 + i, 0) for i in range(2)]
        up_parts += [(up_second[i], 2 + i, 128) for i in range(2)]
        down_parts = [down_weight[0], pack1[256:]]
        kv = halo(after(kv_own, pack1, *up_second))

    with jax.named_scope("experts"):
        w_up = jnp.zeros((1024, 1024), BF)
        for part, j, row in up_parts:
            w_up = lax.dynamic_update_slice(w_up, part, ((dp ^ j) * 256 + row, 0))
        w_down = jnp.zeros((1024, 1024), BF)
        for j, part in enumerate(down_parts):
            w_down = lax.dynamic_update_slice(w_down, part, (((dp ^ j) % 2) * 512, 0))
        sets = [near, across, own]
        pieces = [s.split(got) for s, got in zip(sets, [got_near, got_across, got_own])]
        x_rows = jnp.concatenate([p[0] for p in pieces], axis=0)
        g_rows = jnp.concatenate([p[1] for p in pieces], axis=0)
        pre = dot(x_rows, w_up)
        act = jax.nn.silu(pre).astype(BF)
        act_grad = dot_nt(g_rows, w_down)
        slot_gate = jnp.sum(act.astype(F32) * act_grad, axis=1)
        pre_grad = (act_grad * silu_slope(pre)).astype(BF)
        down_term = dot(act, g_rows, ((0,), (0,))).astype(BF)
        back = dot_nt(pre_grad, w_up).astype(BF)
        back = after(back, down_term)
    size = plane * SLOT
    with jax.named_scope("weight_grads"):

        def down_part(j):
            return lax.dynamic_slice(down_term, (((dp ^ j) % 2) * 512, 0), (512, model))

        down_far = along_z(down_part(1), lambda z: z ^ 1)
        down_grad = (down_part(0).astype(F32) + down_far.astype(F32)).astype(BF)

    with jax.named_scope("attn_fwd"):
        shared_own, lse = attn_forward(steps, after(queries[0], back), kv)
        shared = halo(shared_own)

    with jax.named_scope("back"):
        ret_near = plane_exchange(back[: 2 * size].reshape(plane, 2 * SLOT, model))
        ret_across = plane_exchange(
            after(back[2 * size : 3 * size].reshape(plane, SLOT, model), ret_near)
        )
        ret_own = plane_exchange(after(back[3 * size :].reshape(plane, SLOT, model), ret_across))
        near_sum = near.unpacked(ret_near).astype(BF)
        near_sum = after(near_sum, down_far)
        from_below = along_z(near_sum[:tok], lambda z: z + 2)
        from_above = along_z(near_sum[tok:], lambda z: z - 2)
        from_across = along_z(across.unpacked(ret_across).astype(BF), lambda z: z + 4)
        total = cotan.astype(F32) + own.unpacked(after(ret_own, *shared))
        total = total + from_below.astype(F32) + from_above.astype(F32) + from_across.astype(F32)
        input_grad = total.astype(BF)

    with jax.named_scope("weight_grads"):
        up_term = dot(x_rows, pre_grad, ((0,), (0,))).astype(BF)
        up_term = after(up_term, input_grad)

        def up_part(j):
            return lax.dynamic_slice(up_term, ((dp ^ j) * 256, 0), (256, 1024))

        up_far = [along_z(up_part(j), lambda z, j=j: z ^ j) for j in (1, 2, 3)]
        same = up_part(0).astype(F32) + up_far[0].astype(F32)
        opposite = up_far[1].astype(F32) + up_far[2].astype(F32)
        first = jnp.where(half == 0, same, opposite).astype(BF)
        second = jnp.where(half == 0, opposite, same).astype(BF)
        up_grad = jnp.concatenate([first, second], axis=1)

    with jax.named_scope("attn_bwd"):
        attn_grad = dot_nt(input_grad, out_weight).astype(BF)
        do = halo(attn_grad)
        weight_term = dot(shared_own[:tok, WIDTH:], input_grad, ((0,), (0,))).astype(BF)

    with jax.named_scope("out_weight"):
        rows = WIDTH // plane
        parts = plane_exchange(weight_term.reshape(plane, rows, model))
        part = jnp.sum(parts.astype(F32), axis=0)
        part_b = part.astype(BF)
        for k in (1, 2, 3):
            part = part + along_z(part_b, lambda z, k=k: z ^ k).astype(F32)
        part_b = part.astype(BF)
        part = part_b.astype(F32) + along_z(part_b, lambda z: z + 4).astype(F32)
        whole = jnp.broadcast_to(part.astype(BF)[None], (plane, rows, model))
        whole = after(whole, *up_far)
        out_weight_grad = plane_exchange(whole).reshape(WIDTH, model)

    with jax.named_scope("gate_back"):
        gate_pack = jnp.concatenate(
            [
                slot_gate[: 2 * size].reshape(plane, 2 * SLOT),
                slot_gate[2 * size : 3 * size].reshape(plane, SLOT),
                slot_gate[3 * size :].reshape(plane, SLOT),
            ],
            axis=1,
        ).astype(BF)
        ret_gate = plane_exchange(after(gate_pack, parts)).astype(F32)
        near_gate = near.gate_values(ret_gate[:, : 2 * SLOT]).astype(BF)
        across_gate = across.gate_values(ret_gate[:, 2 * SLOT : 3 * SLOT]).astype(BF)
        gate_sum = own.gate_values(ret_gate[:, 3 * SLOT :])
        gate_sum = gate_sum + along_z(near_gate[:, :tok], lambda z: z + 2).astype(F32)
        gate_sum = gate_sum + along_z(near_gate[:, tok:], lambda z: z - 2).astype(F32)
        gate_sum = gate_sum + along_z(across_gate, lambda z: z + 4).astype(F32)
        gate_grad = gate_sum.T / gates[0].astype(F32)

    with jax.named_scope("attn_bwd"):
        query_grad = attn_queries(steps, shared_own, lse, attn_grad, kv)
        key_grad, value_grad = attn_keys(steps, kv_own, shared, do)

    return (
        input_grad[None],
        query_grad[None],
        key_grad[None],
        value_grad[None],
        out_weight_grad,
        up_grad[None],
        down_grad[None],
        gate_grad[None],
    )


def solution(mesh):
    rows = P("dp", "seq", None)
    weights = P("seq", "dp", None)
    return jax.shard_map(
        per_device,
        mesh=mesh,
        in_specs=(rows, rows, rows, P(), rows, rows, rows, weights, weights, rows),
        out_specs=(rows, rows, rows, rows, P(), weights, weights, rows),
        check_vma=False,
    )
```

```python
import functools

import jax
import jax.numpy as jnp
from jax import lax
from jax.experimental import pallas as pl
from jax.experimental.pallas import tpu as pltpu
from jax.sharding import PartitionSpec as P

HEADS = 8
HEAD = 64
SLOT = 8
TOK = 128
WIDTH = HEADS * HEAD
MODEL = 1024
SCALE = HEAD ** (-0.5)
LOW = -1e30
BOTH = ("seq", "dp")
BF = jnp.bfloat16
F32 = jnp.float32


def seq_of(x, zh, y, c):
    return ((x % 4 * 2 + zh) * 4 + y % 4) * 2 + c


PLANES = [[seq_of(x, zh, y, c) for x in range(4) for y in range(4) for c in range(2)] for zh in range(2)]


def along_z(array, move):
    pairs = []
    for x in range(4):
        for y in range(4):
            for c in range(2):
                for z in range(8):
                    to = move(z) % 8
                    pairs.append(
                        (seq_of(x, z // 4, y, c) * 4 + z % 4, seq_of(x, to // 4, y, c) * 4 + to % 4)
                    )
    return lax.ppermute(array, BOTH, pairs)


def seq_permute(array, move):
    size = lax.axis_size("seq")
    pairs = [(i, move(i)) for i in range(size) if 0 <= move(i) < size]
    return lax.ppermute(array, "seq", pairs)


def plane_exchange(array):
    return lax.all_to_all(
        array, "seq", split_axis=0, concat_axis=0, tiled=True, axis_index_groups=PLANES
    )


def after(value, *others):
    return lax.optimization_barrier((value, *others))[0]


def halo(array):
    swap = seq_permute(array, lambda i: i ^ 1)
    left = seq_permute(array, lambda i: i + 2)
    right = seq_permute(array, lambda i: i - 2)
    far = seq_permute(array, lambda i: i + 3 if i % 2 else i - 3)
    rows = array.shape[0]
    swapped = seq_permute(jnp.concatenate([left, right], axis=0), lambda i: i ^ 1)
    return [array, swap, left, swapped[:rows], right, swapped[rows:], far]


def halo_steps(seq):
    core = seq % 2
    steps = jnp.stack(
        [
            jnp.int32(0),
            1 - 2 * core,
            jnp.int32(-2),
            -1 - 2 * core,
            jnp.int32(2),
            3 - 2 * core,
            6 * core - 3,
        ]
    ).astype(jnp.int32)
    there = seq + steps
    real = ((there >= 0) & (there < lax.axis_size("seq"))).astype(jnp.int32)
    return jnp.stack([steps, real])


def dot(left, right, dims=((1,), (0,))):
    return lax.dot_general(left, right, (dims, ((), ())), preferred_element_type=F32)


def dot_nt(left, right):
    return dot(left, right, ((1,), (1,)))


def head_lanes(half):
    lane = lax.broadcasted_iota(jnp.int32, (TOK, 2 * HEAD), 1)
    return (lane < HEAD) if half == 0 else (lane >= HEAD)


def within(steps_ref, b, far_axis):
    own = lax.broadcasted_iota(jnp.int32, (TOK, TOK), 1 - far_axis)
    other = lax.broadcasted_iota(jnp.int32, (TOK, TOK), far_axis)
    gap = other + steps_ref[0, b] * TOK - own
    return (jnp.abs(gap) <= 3 * TOK) & (steps_ref[1, b] == 1)


def fwd_kernel(steps_ref, q_ref, *refs):
    kv = refs[:7]
    shared_ref, lse_ref = refs[7:9]
    lane = lax.broadcasted_iota(jnp.int32, (TOK, TOK), 1)
    lse_all = jnp.zeros((TOK, TOK), F32)
    masks = [within(steps_ref, b, 1) for b in range(7)]
    shared_ref[0:TOK, 0:WIDTH] = q_ref[...]
    for pair in range(HEADS // 2):
        cols = slice(pair * 128, pair * 128 + 128)
        vcols = slice(WIDTH + pair * 128, WIDTH + pair * 128 + 128)
        q_pair = q_ref[:, cols]
        outs = []
        for half in range(2):
            q_head = jnp.where(head_lanes(half), q_pair, jnp.zeros((), BF))
            scores = [
                jnp.where(masks[b], dot_nt(q_head, kv[b][:, cols]) * SCALE, LOW) for b in range(7)
            ]
            top = functools.reduce(jnp.maximum, scores)
            top = jnp.max(top, axis=1, keepdims=True)
            exps = [jnp.exp(s - top) for s in scores]
            total = jnp.sum(functools.reduce(jnp.add, exps), axis=1, keepdims=True)
            inv = 1.0 / total
            acc = jnp.zeros((TOK, 128), F32)
            for b in range(7):
                acc = acc + dot((exps[b] * inv).astype(BF), kv[b][:, vcols])
            outs.append(acc)
            lse_all = jnp.where(lane == 2 * pair + half, top + jnp.log(total), lse_all)
        shared_ref[0:TOK, vcols] = jnp.where(head_lanes(0), outs[0], outs[1]).astype(BF)
    lse_ref[...] = lse_all
    rows = jnp.transpose(lse_all)[0:16]
    high = rows.astype(BF)
    rows = rows - high.astype(F32)
    mid = rows.astype(BF)
    low = (rows - mid.astype(F32)).astype(BF)
    shared_ref[TOK : TOK + 16, :] = jnp.concatenate(
        [high, mid, low, jnp.zeros((16, MODEL - 3 * TOK), BF)], axis=1
    )


def query_kernel(steps_ref, shared_ref, lse_ref, do_ref, *refs):
    kv = refs[:7]
    dq_ref = refs[7]
    masks = [within(steps_ref, b, 1) for b in range(7)]
    lse_all = lse_ref[...]
    for pair in range(HEADS // 2):
        cols = slice(pair * 128, pair * 128 + 128)
        vcols = slice(WIDTH + pair * 128, WIDTH + pair * 128 + 128)
        q_pair = shared_ref[0:TOK, cols]
        do_pair = do_ref[:, cols]
        prod = do_pair.astype(F32) * shared_ref[0:TOK, vcols].astype(F32)
        outs = []
        for half in range(2):
            lanes = head_lanes(half)
            q_head = jnp.where(lanes, q_pair, jnp.zeros((), BF))
            do_head = jnp.where(lanes, do_pair, jnp.zeros((), BF))
            delta = jnp.sum(jnp.where(lanes, prod, 0.0), axis=1, keepdims=True)
            lse = lse_all[:, 2 * pair + half : 2 * pair + half + 1]
            acc = jnp.zeros((TOK, 128), F32)
            for b in range(7):
                score = dot_nt(q_head, kv[b][:, cols]) * SCALE - lse
                prob = jnp.exp(jnp.where(masks[b], score, LOW))
                dprob = dot_nt(do_head, kv[b][:, vcols])
                dscore = (prob * (dprob - delta) * SCALE).astype(BF)
                acc = acc + dot(dscore, kv[b][:, cols])
            outs.append(acc)
        dq_ref[:, cols] = jnp.where(head_lanes(0), outs[0], outs[1]).astype(BF)


def key_kernel(steps_ref, kv_ref, *refs):
    shared = refs[:7]
    dk_ref, dv_ref, lse_scr, delta_scr = refs[7:11]
    masks = [within(steps_ref, b, 1) for b in range(7)]
    row = lax.broadcasted_iota(jnp.int32, (16, WIDTH), 0)
    col = lax.broadcasted_iota(jnp.int32, (16, WIDTH), 1)
    pick = ((col >= row * HEAD) & (col < row * HEAD + HEAD)).astype(BF)
    for b in range(7):
        tail = shared[b][TOK : TOK + 16, 0 : 3 * TOK].astype(F32)
        lse_scr[b] = tail[:, 0:TOK] + tail[:, TOK : 2 * TOK] + tail[:, 2 * TOK :]
        prod = shared[b][0:TOK, 2 * WIDTH :].astype(F32)
        prod = prod * shared[b][0:TOK, WIDTH : 2 * WIDTH].astype(F32)
        high = prod.astype(BF)
        prod = prod - high.astype(F32)
        mid = prod.astype(BF)
        low = (prod - mid.astype(F32)).astype(BF)
        delta_scr[b] = dot_nt(pick, high) + dot_nt(pick, mid) + dot_nt(pick, low)
    for pair in range(HEADS // 2):
        cols = slice(pair * 128, pair * 128 + 128)
        vcols = slice(WIDTH + pair * 128, WIDTH + pair * 128 + 128)
        dcols = slice(2 * WIDTH + pair * 128, 2 * WIDTH + pair * 128 + 128)
        k_pair = kv_ref[:, cols]
        v_pair = kv_ref[:, vcols]
        dks, dvs = [], []
        for half in range(2):
            head = 2 * pair + half
            lanes = head_lanes(half)
            k_head = jnp.where(lanes, k_pair, jnp.zeros((), BF))
            v_head = jnp.where(lanes, v_pair, jnp.zeros((), BF))
            dk = jnp.zeros((TOK, 128), F32)
            dv = jnp.zeros((TOK, 128), F32)
            for b in range(7):
                q_b = shared[b][0:TOK, cols]
                do_b = shared[b][0:TOK, dcols]
                score = dot_nt(k_head, q_b) * SCALE - lse_scr[b, head : head + 1, :]
                prob = jnp.exp(jnp.where(masks[b], score, LOW))
                dprob = dot_nt(v_head, do_b)
                dscore = (prob * (dprob - delta_scr[b, head : head + 1, :]) * SCALE).astype(BF)
                dk = dk + dot(dscore, q_b)
                dv = dv + dot(prob.astype(BF), do_b)
            dks.append(dk)
            dvs.append(dv)
        dk_ref[:, cols] = jnp.where(head_lanes(0), dks[0], dks[1]).astype(BF)
        dv_ref[:, cols] = jnp.where(head_lanes(0), dvs[0], dvs[1]).astype(BF)


def on_chip(body, outs, n_in, scratch=()):
    return pl.pallas_call(
        body,
        out_shape=outs,
        in_specs=[pl.BlockSpec(memory_space=pltpu.SMEM)]
        + [pl.BlockSpec(memory_space=pltpu.VMEM)] * (n_in - 1),
        out_specs=[pl.BlockSpec(memory_space=pltpu.VMEM)] * len(outs),
        scratch_shapes=list(scratch),
        compiler_params=pltpu.CompilerParams(vmem_limit_bytes=24 * 1024 * 1024),
        cost_estimate=pl.CostEstimate(flops=10**9, bytes_accessed=6 * 10**6, transcendentals=10**6),
    )


def attn_forward(steps, q, kv):
    outs = [
        jax.ShapeDtypeStruct((TOK + 16, MODEL), BF),
        jax.ShapeDtypeStruct((TOK, TOK), F32),
    ]
    return on_chip(fwd_kernel, outs, 9)(steps, q, *kv)


def attn_queries(steps, shared, lse, do, kv):
    outs = [jax.ShapeDtypeStruct((TOK, WIDTH), BF)]
    return on_chip(query_kernel, outs, 11)(steps, shared, lse, do, *kv)[0]


def attn_keys(steps, kv, shared):
    outs = [jax.ShapeDtypeStruct((TOK, WIDTH), BF)] * 2
    scratch = [pltpu.VMEM((7, 16, TOK), F32), pltpu.VMEM((7, 16, TOK), F32)]
    return on_chip(key_kernel, outs, 9, scratch)(steps, kv, *shared)


def experts_kernel(
    dp_ref, near_ref, across_ref, own_ref, mine_ref, pack_ref, u2_ref, u3_ref, u2b_ref, u3b_ref,
    down_ref, back_ref, x_ref, g_ref, act_ref, pg_ref, gate_ref, up_scr, down_scr,
):
    dp = dp_ref[0]

    def place(scr, block, rows, offset, value):
        start = pl.multiple_of(block * rows + offset, 128)
        scr[pl.ds(start, value.shape[0]), :] = value

    place(up_scr, dp, 256, 0, mine_ref[...])
    place(up_scr, dp ^ 1, 256, 0, pack_ref[0:256])
    place(up_scr, dp ^ 2, 256, 0, u2_ref[...])
    place(up_scr, dp ^ 2, 256, 128, u2b_ref[...])
    place(up_scr, dp ^ 3, 256, 0, u3_ref[...])
    place(up_scr, dp ^ 3, 256, 128, u3b_ref[...])
    place(down_scr, dp & 1, 512, 0, down_ref[...])
    place(down_scr, (dp & 1) ^ 1, 512, 0, pack_ref[256:768])

    def tile(i, carry):
        base = pl.multiple_of(i * 256, 256)
        for p in range(8):
            here = pl.ds(base + p * 32, 16)
            there = pl.ds(base + p * 32 + 16, 16)
            near = near_ref[i * 8 + p]
            x_ref[here, :] = near[0:16]
            g_ref[here, :] = near[16:32]
            across = across_ref[i * 8 + p].astype(F32)
            own = own_ref[i * 8 + p].astype(F32)
            x_ref[there, :] = jnp.concatenate([across[0:8], own[0:8]], axis=0).astype(BF)
            g_ref[there, :] = jnp.concatenate([across[8:16], own[8:16]], axis=0).astype(BF)
        rows = pl.ds(base, 256)
        pre = dot(x_ref[rows, :], up_scr[...])
        act_grad = dot_nt(g_ref[rows, :], down_scr[...])
        sig = 1.0 / (1.0 + jnp.exp(-pre))
        act = (pre * sig).astype(BF)
        act_ref[rows, :] = act
        gate = jnp.sum(act.astype(F32) * act_grad, axis=1, keepdims=True)
        gate_ref[rows, :] = jnp.broadcast_to(gate, (256, 128))
        pg_ref[rows, :] = (act_grad * (sig * (1.0 + pre * (1.0 - sig)))).astype(BF)
        back_ref[rows, :] = dot_nt(pg_ref[rows, :], up_scr[...]).astype(BF)
        return carry

    lax.fori_loop(0, 4, tile, 0)


def experts(dp, near, across, own, mine, pack, up_first, up_second, down):
    big = jax.ShapeDtypeStruct((1024, MODEL), BF)
    ins = [near, across, own, mine, pack, *up_first, *up_second, down]
    return pl.pallas_call(
        experts_kernel,
        out_shape=[big] * 5 + [jax.ShapeDtypeStruct((1024, 128), F32)],
        in_specs=[pl.BlockSpec(memory_space=pltpu.SMEM)]
        + [pl.BlockSpec(memory_space=pltpu.VMEM)] * len(ins),
        out_specs=[pl.BlockSpec(memory_space=pltpu.VMEM)] * 6,
        scratch_shapes=[pltpu.VMEM((1024, MODEL), BF)] * 2,
        compiler_params=pltpu.CompilerParams(vmem_limit_bytes=40 * 1024 * 1024),
        cost_estimate=pl.CostEstimate(
            flops=6 * 10**9, bytes_accessed=20 * 10**6, transcendentals=10**6
        ),
    )(dp.reshape(1), *ins)


def per_device(
    queries, keys, values, out_weight, ffn_input, routes, gates, up_weight, down_weight, out_grad
):
    seq = lax.axis_index("seq")
    dp = lax.axis_index("dp")
    z_hi = (seq // 8) % 2
    tok, model = ffn_input.shape[1:]
    n_seq = lax.axis_size("seq")
    plane = n_seq // 2
    frames = ffn_input[0]
    cotan = out_grad[0]

    with jax.named_scope("meta"):
        chosen = routes[0].T.reshape(1, 2 * tok)
        named = chosen == jnp.arange(n_seq, dtype=jnp.int32)[:, None]
        order = jnp.arange(2 * tok)
        before = (order[:, None] < order[None, :]).astype(BF)
        counts = dot(named.astype(BF), before)
        rank = jnp.sum(jnp.where(named, counts, 0.0), axis=0, keepdims=True)
        note = jnp.concatenate(
            [
                chosen.astype(BF),
                rank.astype(BF),
                gates[0].T.reshape(1, 2 * tok),
                jnp.zeros((1, 2 * tok), BF),
            ],
            axis=1,
        )
        payload = jnp.concatenate([frames, note, jnp.zeros((15, model), BF), cotan], axis=0)
    n_x = tok + 16
    with jax.named_scope("tokens_z"):
        above = along_z(payload, lambda z: z - 2)
        below = along_z(payload, lambda z: z + 2)
        across_x = along_z(above[:n_x], lambda z: z - 2)
        across_g = along_z(below[n_x:], lambda z: z + 2)

    with jax.named_scope("weights_z"):
        half = dp // 2
        up_mine = lax.dynamic_slice(up_weight[0], (0, half * 1024), (256, 1024))
        up_other = lax.dynamic_slice(up_weight[0], (0, (1 - half) * 1024), (256, 1024))
        pack = jnp.concatenate([up_mine, down_weight[0]], axis=0)
        up_other = after(up_other, above, below)
        pack1 = along_z(pack, lambda z: z ^ 1)
        up_first = [along_z(up_other[:128], lambda z, j=j: z ^ j) for j in (2, 3)]
        up_second = after(up_other[128:], *up_first)
        up_second = [along_z(up_second, lambda z, j=j: z ^ j) for j in (2, 3)]

    def rows_of(note_row, stride, offset):
        expert = note_row[0, : 2 * tok].astype(jnp.int32)
        place = (expert // 16) * 8 + expert % 8
        here = (expert // 8) % 2 == z_hi
        row = place * stride + offset + note_row[0, 2 * tok : 4 * tok].astype(jnp.int32)
        row = jnp.where(here, row, -1).reshape(2, tok)
        return row, note_row[0, 4 * tok : 6 * tok].reshape(2, tok)

    def placing(row, total):
        spots = jnp.arange(total, dtype=jnp.int32)[:, None]
        return [spots == row[t][None, :] for t in range(2)]

    def merged(hits, gate=None):
        if gate is None:
            return (hits[0] | hits[1]).astype(BF)
        zero = jnp.zeros((), BF)
        return jnp.where(hits[0], gate[0][None, :], jnp.where(hits[1], gate[1][None, :], zero))

    class Sets:
        def __init__(self, notes, xs, gs):
            n = len(notes)
            self.n = n
            found = [rows_of(note_row, n * SLOT, k * SLOT) for k, note_row in enumerate(notes)]
            self.hits = placing(jnp.concatenate([f[0] for f in found], axis=1), plane * n * SLOT)
            self.gate = jnp.concatenate([f[1] for f in found], axis=1)
            self.x = xs[0] if n == 1 else jnp.concatenate(xs, axis=0)
            self.g = gs[0] if n == 1 else jnp.concatenate(gs, axis=0)

        def packed(self):
            shape = (plane, self.n * SLOT, model)
            send_x = dot(merged(self.hits), self.x).astype(BF).reshape(shape)
            send_g = dot(merged(self.hits, self.gate), self.g).astype(BF).reshape(shape)
            return jnp.concatenate([send_x, send_g], axis=1)

    with jax.named_scope("out_own"):
        own = Sets([note], [frames], [cotan])
        got_own = plane_exchange(own.packed())
    with jax.named_scope("out_near"):
        near = Sets(
            [above[tok : tok + 1], below[tok : tok + 1]],
            [above[:tok], below[:tok]],
            [above[n_x:], below[n_x:]],
        )
        got_near = plane_exchange(after(near.packed(), got_own))
    with jax.named_scope("out_across"):
        across = Sets([across_x[tok : tok + 1]], [across_x[:tok]], [across_g])
        got_across = plane_exchange(after(across.packed(), got_near, *up_first))

    with jax.named_scope("attn_fwd"):
        steps = halo_steps(seq)
        kv_own = jnp.concatenate([keys[0], values[0]], axis=1)
        kv = halo(after(kv_own, up_second[0]))

    with jax.named_scope("experts"):
        pack1, late, _ = lax.optimization_barrier((pack1, up_second[1], got_across))
        back, x_rows, g_rows, act, pre_grad, gate_wide = experts(
            dp, got_near, got_across, got_own, up_mine, pack1, up_first, [up_second[0], late],
            down_weight[0],
        )
    with jax.named_scope("back"):
        returned = plane_exchange(back.reshape(plane, 4 * SLOT, model))

    with jax.named_scope("weight_grads"):
        down_term = dot(act, g_rows, ((0,), (0,))).astype(BF)
        up_term = dot(x_rows, pre_grad, ((0,), (0,))).astype(BF)

        def down_part(j):
            return lax.dynamic_slice(down_term, (((dp ^ j) % 2) * 512, 0), (512, model))

        def up_part(j):
            return lax.dynamic_slice(up_term, ((dp ^ j) * 256, 0), (256, 1024))

        up_far = [along_z(up_part(j), lambda z, j=j: z ^ j) for j in (2, 3)]
        down_far = along_z(down_part(1), lambda z: z ^ 1)

    with jax.named_scope("attn_fwd"):
        shared_own, lse = attn_forward(steps, after(queries[0], back), kv)

    with jax.named_scope("back"):
        found = [
            rows_of(note_row, 4 * SLOT, k * SLOT)
            for k, note_row in enumerate(
                [above[tok : tok + 1], below[tok : tok + 1], across_x[tok : tok + 1], note]
            )
        ]
        all_hits = placing(jnp.concatenate([f[0] for f in found], axis=1), plane * 4 * SLOT)
        all_place = after(merged(all_hits), back)
        sums = dot(all_place, returned.reshape(-1, model), ((0,), (0,)))
        far_sums = sums[: 3 * tok].astype(BF)
        gate_pack = gate_wide[:, 0].reshape(plane, 4 * SLOT).astype(BF)
        far_sums = [far_sums[k * tok : (k + 1) * tok] for k in range(3)]
        *far_sums, gate_pack = lax.optimization_barrier(
            (*far_sums, gate_pack, down_far, *up_far)
        )[:4]
        from_below = along_z(far_sums[0], lambda z: z + 2)
        from_above = along_z(far_sums[1], lambda z: z - 2)
        from_across = along_z(far_sums[2], lambda z: z + 4)
        total = cotan.astype(F32) + sums[3 * tok :]
        total = total + from_below.astype(F32) + from_above.astype(F32) + from_across.astype(F32)
        input_grad = total.astype(BF)

    with jax.named_scope("gate_back"):
        ret_gate = plane_exchange(gate_pack).astype(F32).reshape(-1, 1)
        gate_sums = jnp.stack([jnp.sum(jnp.where(h, ret_gate, 0.0), axis=0) for h in all_hits])

    with jax.named_scope("weight_grads"):
        up_near = along_z(after(up_part(1), input_grad), lambda z: z ^ 1)
        same = up_part(0).astype(F32) + up_near.astype(F32)
        opposite = up_far[0].astype(F32) + up_far[1].astype(F32)
        first = jnp.where(half == 0, same, opposite).astype(BF)
        second = jnp.where(half == 0, opposite, same).astype(BF)
        up_grad = jnp.concatenate([first, second], axis=1)
        down_grad = (down_part(0).astype(F32) + down_far.astype(F32)).astype(BF)

    with jax.named_scope("attn_bwd"):
        attn_grad = dot_nt(input_grad, out_weight).astype(BF)
        tail_rows = jnp.concatenate([attn_grad, jnp.zeros((16, WIDTH), BF)], axis=0)
        shared = halo(jnp.concatenate([shared_own, tail_rows], axis=1))
        weight_term = dot(shared_own[:tok, WIDTH:], input_grad, ((0,), (0,))).astype(BF)

    with jax.named_scope("out_weight"):
        rows = WIDTH // plane
        parts = plane_exchange(weight_term.reshape(plane, rows, model))
        part = jnp.sum(parts.astype(F32), axis=0)
        part_b = part.astype(BF)
        part_first = part_b
        for k in (1, 2, 3):
            part = part + along_z(part_b, lambda z, k=k: z ^ k).astype(F32)
        part_b = part.astype(BF)
        part = part_b.astype(F32) + along_z(part_b, lambda z: z + 4).astype(F32)
        whole = jnp.broadcast_to(part.astype(BF)[None], (plane, rows, model))
        whole = after(whole, up_near)
        out_weight_grad = plane_exchange(whole).reshape(WIDTH, model)

    with jax.named_scope("gate_back"):
        gate_far = after(gate_sums.astype(BF), *shared)
        gate_sum = gate_sums[:, 3 * tok :]
        gate_moves = [lambda z: z + 2, lambda z: z - 2, lambda z: z + 4]
        for k, move in enumerate(gate_moves):
            part = along_z(gate_far[:, k * tok : (k + 1) * tok], move)
            gate_sum = gate_sum + part.astype(F32)
        gate_grad = gate_sum.T / gates[0].astype(F32)

    with jax.named_scope("attn_bwd"):
        query_grad = attn_queries(steps, shared_own, lse, attn_grad, kv)
        key_grad, value_grad = attn_keys(steps, after(kv_own, part_first), shared)

    return (
        input_grad[None],
        query_grad[None],
        key_grad[None],
        value_grad[None],
        out_weight_grad,
        up_grad[None],
        down_grad[None],
        gate_grad[None],
    )


def solution(mesh):
    rows = P("dp", "seq", None)
    weights = P("seq", "dp", None)
    return jax.shard_map(
        per_device,
        mesh=mesh,
        in_specs=(rows, rows, rows, P(), rows, rows, rows, weights, weights, rows),
        out_specs=(rows, rows, rows, rows, P(), weights, weights, rows),
        check_vma=False,
    )
```

```python
import functools

import jax
import jax.numpy as jnp
from jax import lax
from jax.experimental import pallas as pl
from jax.experimental.pallas import tpu as pltpu
from jax.sharding import PartitionSpec as P

HEADS = 8
HEAD = 64
SLOT = 8
TOK = 128
WIDTH = HEADS * HEAD
MODEL = 1024
SCALE = HEAD ** (-0.5)
LOW = -1e30
CUT = 192
BOTH = ("seq", "dp")
BF = jnp.bfloat16
F32 = jnp.float32


def seq_of(x, zh, y, c):
    return ((x % 4 * 2 + zh) * 4 + y % 4) * 2 + c


PLANES = [[seq_of(x, zh, y, c) for x in range(4) for y in range(4) for c in range(2)] for zh in range(2)]


def along_z(array, move):
    pairs = []
    for x in range(4):
        for y in range(4):
            for c in range(2):
                for z in range(8):
                    to = move(z) % 8
                    pairs.append(
                        (seq_of(x, z // 4, y, c) * 4 + z % 4, seq_of(x, to // 4, y, c) * 4 + to % 4)
                    )
    return lax.ppermute(array, BOTH, pairs)


def seq_permute(array, move):
    size = lax.axis_size("seq")
    pairs = [(i, move(i)) for i in range(size) if 0 <= move(i) < size]
    return lax.ppermute(array, "seq", pairs)


def plane_exchange(array):
    return lax.all_to_all(
        array, "seq", split_axis=0, concat_axis=0, tiled=True, axis_index_groups=PLANES
    )


def after(value, *others):
    return lax.optimization_barrier((value, *others))[0]


def halo(array):
    swap = seq_permute(array, lambda i: i ^ 1)
    left = seq_permute(array, lambda i: i + 2)
    right = seq_permute(array, lambda i: i - 2)
    far = seq_permute(array, lambda i: i + 3 if i % 2 else i - 3)
    rows = array.shape[0]
    swapped = seq_permute(jnp.concatenate([left, right], axis=0), lambda i: i ^ 1)
    return [array, swap, left, swapped[:rows], right, swapped[rows:], far]


def halo_steps(seq):
    core = seq % 2
    steps = jnp.stack(
        [
            jnp.int32(0),
            1 - 2 * core,
            jnp.int32(-2),
            -1 - 2 * core,
            jnp.int32(2),
            3 - 2 * core,
            6 * core - 3,
        ]
    ).astype(jnp.int32)
    there = seq + steps
    real = ((there >= 0) & (there < lax.axis_size("seq"))).astype(jnp.int32)
    return jnp.stack([steps, real])


def dot(left, right, dims=((1,), (0,))):
    return lax.dot_general(left, right, (dims, ((), ())), preferred_element_type=F32)


def dot_nt(left, right):
    return dot(left, right, ((1,), (1,)))


def head_lanes(half):
    lane = lax.broadcasted_iota(jnp.int32, (TOK, 2 * HEAD), 1)
    return (lane < HEAD) if half == 0 else (lane >= HEAD)


def within(steps_ref, b, far_axis):
    own = lax.broadcasted_iota(jnp.int32, (TOK, TOK), 1 - far_axis)
    other = lax.broadcasted_iota(jnp.int32, (TOK, TOK), far_axis)
    gap = other + steps_ref[0, b] * TOK - own
    return (jnp.abs(gap) <= 3 * TOK) & (steps_ref[1, b] == 1)


def fwd_kernel(steps_ref, q_ref, *refs):
    kv = refs[:7]
    shared_ref, lse_ref = refs[7:9]
    lane = lax.broadcasted_iota(jnp.int32, (TOK, TOK), 1)
    lse_all = jnp.zeros((TOK, TOK), F32)
    masks = [within(steps_ref, b, 1) for b in range(7)]
    shared_ref[0:TOK, 0:WIDTH] = q_ref[...]
    for pair in range(HEADS // 2):
        cols = slice(pair * 128, pair * 128 + 128)
        vcols = slice(WIDTH + pair * 128, WIDTH + pair * 128 + 128)
        q_pair = q_ref[:, cols]
        outs = []
        for half in range(2):
            q_head = jnp.where(head_lanes(half), q_pair, jnp.zeros((), BF))
            scores = [
                jnp.where(masks[b], dot_nt(q_head, kv[b][:, cols]) * SCALE, LOW) for b in range(7)
            ]
            top = functools.reduce(jnp.maximum, scores)
            top = jnp.max(top, axis=1, keepdims=True)
            exps = [jnp.exp(s - top) for s in scores]
            total = jnp.sum(functools.reduce(jnp.add, exps), axis=1, keepdims=True)
            inv = 1.0 / total
            acc = jnp.zeros((TOK, 128), F32)
            for b in range(7):
                acc = acc + dot((exps[b] * inv).astype(BF), kv[b][:, vcols])
            outs.append(acc)
            lse_all = jnp.where(lane == 2 * pair + half, top + jnp.log(total), lse_all)
        shared_ref[0:TOK, vcols] = jnp.where(head_lanes(0), outs[0], outs[1]).astype(BF)
    lse_ref[...] = lse_all
    rows = jnp.transpose(lse_all)[0:16]
    high = rows.astype(BF)
    rows = rows - high.astype(F32)
    mid = rows.astype(BF)
    low = (rows - mid.astype(F32)).astype(BF)
    shared_ref[TOK : TOK + 16, :] = jnp.concatenate(
        [high, mid, low, jnp.zeros((16, MODEL - 3 * TOK), BF)], axis=1
    )


def query_kernel(steps_ref, shared_ref, lse_ref, do_ref, *refs):
    kv = refs[:7]
    dq_ref = refs[7]
    masks = [within(steps_ref, b, 1) for b in range(7)]
    lse_all = lse_ref[...]
    for pair in range(HEADS // 2):
        cols = slice(pair * 128, pair * 128 + 128)
        vcols = slice(WIDTH + pair * 128, WIDTH + pair * 128 + 128)
        q_pair = shared_ref[0:TOK, cols]
        do_pair = do_ref[:, cols]
        prod = do_pair.astype(F32) * shared_ref[0:TOK, vcols].astype(F32)
        outs = []
        for half in range(2):
            lanes = head_lanes(half)
            q_head = jnp.where(lanes, q_pair, jnp.zeros((), BF))
            do_head = jnp.where(lanes, do_pair, jnp.zeros((), BF))
            delta = jnp.sum(jnp.where(lanes, prod, 0.0), axis=1, keepdims=True)
            lse = lse_all[:, 2 * pair + half : 2 * pair + half + 1]
            acc = jnp.zeros((TOK, 128), F32)
            for b in range(7):
                score = dot_nt(q_head, kv[b][:, cols]) * SCALE - lse
                prob = jnp.exp(jnp.where(masks[b], score, LOW))
                dprob = dot_nt(do_head, kv[b][:, vcols])
                dscore = (prob * (dprob - delta) * SCALE).astype(BF)
                acc = acc + dot(dscore, kv[b][:, cols])
            outs.append(acc)
        dq_ref[:, cols] = jnp.where(head_lanes(0), outs[0], outs[1]).astype(BF)


def key_kernel(steps_ref, kv_ref, *refs):
    shared = refs[:7]
    do = refs[7:14]
    dk_ref, dv_ref, lse_scr, delta_scr = refs[14:18]
    masks = [within(steps_ref, b, 1) for b in range(7)]
    row = lax.broadcasted_iota(jnp.int32, (16, WIDTH), 0)
    col = lax.broadcasted_iota(jnp.int32, (16, WIDTH), 1)
    pick = ((col >= row * HEAD) & (col < row * HEAD + HEAD)).astype(BF)
    for b in range(7):
        tail = shared[b][TOK : TOK + 16, 0 : 3 * TOK].astype(F32)
        lse_scr[b] = tail[:, 0:TOK] + tail[:, TOK : 2 * TOK] + tail[:, 2 * TOK :]
        prod = do[b][...].astype(F32) * shared[b][0:TOK, WIDTH:].astype(F32)
        high = prod.astype(BF)
        prod = prod - high.astype(F32)
        mid = prod.astype(BF)
        low = (prod - mid.astype(F32)).astype(BF)
        delta_scr[b] = dot_nt(pick, high) + dot_nt(pick, mid) + dot_nt(pick, low)
    for pair in range(HEADS // 2):
        cols = slice(pair * 128, pair * 128 + 128)
        vcols = slice(WIDTH + pair * 128, WIDTH + pair * 128 + 128)
        k_pair = kv_ref[:, cols]
        v_pair = kv_ref[:, vcols]
        dks, dvs = [], []
        for half in range(2):
            head = 2 * pair + half
            lanes = head_lanes(half)
            k_head = jnp.where(lanes, k_pair, jnp.zeros((), BF))
            v_head = jnp.where(lanes, v_pair, jnp.zeros((), BF))
            dk = jnp.zeros((TOK, 128), F32)
            dv = jnp.zeros((TOK, 128), F32)
            for b in range(7):
                q_b = shared[b][0:TOK, cols]
                do_b = do[b][:, cols]
                score = dot_nt(k_head, q_b) * SCALE - lse_scr[b, head : head + 1, :]
                prob = jnp.exp(jnp.where(masks[b], score, LOW))
                dprob = dot_nt(v_head, do_b)
                dscore = (prob * (dprob - delta_scr[b, head : head + 1, :]) * SCALE).astype(BF)
                dk = dk + dot(dscore, q_b)
                dv = dv + dot(prob.astype(BF), do_b)
            dks.append(dk)
            dvs.append(dv)
        dk_ref[:, cols] = jnp.where(head_lanes(0), dks[0], dks[1]).astype(BF)
        dv_ref[:, cols] = jnp.where(head_lanes(0), dvs[0], dvs[1]).astype(BF)


def on_chip(body, outs, n_in, scratch=()):
    return pl.pallas_call(
        body,
        out_shape=outs,
        in_specs=[pl.BlockSpec(memory_space=pltpu.SMEM)]
        + [pl.BlockSpec(memory_space=pltpu.VMEM)] * (n_in - 1),
        out_specs=[pl.BlockSpec(memory_space=pltpu.VMEM)] * len(outs),
        scratch_shapes=list(scratch),
        compiler_params=pltpu.CompilerParams(vmem_limit_bytes=24 * 1024 * 1024),
        cost_estimate=pl.CostEstimate(flops=10**6, bytes_accessed=10**5, transcendentals=10**3),
    )


def attn_forward(steps, q, kv):
    outs = [
        jax.ShapeDtypeStruct((TOK + 16, MODEL), BF),
        jax.ShapeDtypeStruct((TOK, TOK), F32),
    ]
    return on_chip(fwd_kernel, outs, 9)(steps, q, *kv)


def attn_queries(steps, shared, lse, do, kv):
    outs = [jax.ShapeDtypeStruct((TOK, WIDTH), BF)]
    return on_chip(query_kernel, outs, 11)(steps, shared, lse, do, *kv)[0]


def attn_keys(steps, kv, shared, do):
    outs = [jax.ShapeDtypeStruct((TOK, WIDTH), BF)] * 2
    scratch = [pltpu.VMEM((7, 16, TOK), F32), pltpu.VMEM((7, 16, TOK), F32)]
    return on_chip(key_kernel, outs, 16, scratch)(steps, kv, *shared, *do)


def experts_kernel(
    dp_ref, near_ref, across_ref, own_ref, mine_ref, pack_ref, u2_ref, u3_ref, u2b_ref, u3b_ref,
    down_ref, back_ref, x_ref, g_ref, act_ref, pg_ref, gate_ref, up_scr, down_scr,
):
    dp = dp_ref[0]

    def place(scr, block, rows, offset, value):
        start = pl.multiple_of(block * rows + offset, 64)
        scr[pl.ds(start, value.shape[0]), :] = value

    place(up_scr, dp, 256, 0, mine_ref[...])
    place(up_scr, dp ^ 1, 256, 0, pack_ref[0:256])
    place(up_scr, dp ^ 2, 256, 0, u2_ref[...])
    place(up_scr, dp ^ 2, 256, CUT, u2b_ref[...])
    place(up_scr, dp ^ 3, 256, 0, u3_ref[...])
    place(up_scr, dp ^ 3, 256, CUT, u3b_ref[...])
    place(down_scr, dp & 1, 512, 0, down_ref[...])
    place(down_scr, (dp & 1) ^ 1, 512, 0, pack_ref[256:768])

    def tile(i, carry):
        base = pl.multiple_of(i * 256, 256)
        for p in range(8):
            here = pl.ds(base + p * 32, 16)
            there = pl.ds(base + p * 32 + 16, 16)
            near = near_ref[i * 8 + p]
            x_ref[here, :] = near[0:16]
            g_ref[here, :] = near[16:32]
            across = across_ref[i * 8 + p].astype(F32)
            own = own_ref[i * 8 + p].astype(F32)
            x_ref[there, :] = jnp.concatenate([across[0:8], own[0:8]], axis=0).astype(BF)
            g_ref[there, :] = jnp.concatenate([across[8:16], own[8:16]], axis=0).astype(BF)
        rows = pl.ds(base, 256)
        pre = dot(x_ref[rows, :], up_scr[...])
        act_grad = dot_nt(g_ref[rows, :], down_scr[...])
        sig = 1.0 / (1.0 + jnp.exp(-pre))
        act = (pre * sig).astype(BF)
        act_ref[rows, :] = act
        gate = jnp.sum(act.astype(F32) * act_grad, axis=1, keepdims=True)
        gate_ref[rows, :] = jnp.broadcast_to(gate, (256, 128))
        pg_ref[rows, :] = (act_grad * (sig * (1.0 + pre * (1.0 - sig)))).astype(BF)
        back_ref[rows, :] = dot_nt(pg_ref[rows, :], up_scr[...]).astype(BF)
        return carry

    lax.fori_loop(0, 4, tile, 0)


def experts(dp, near, across, own, mine, pack, up_first, up_second, down):
    big = jax.ShapeDtypeStruct((1024, MODEL), BF)
    ins = [near, across, own, mine, pack, *up_first, *up_second, down]
    return pl.pallas_call(
        experts_kernel,
        out_shape=[big] * 5 + [jax.ShapeDtypeStruct((1024, 128), F32)],
        in_specs=[pl.BlockSpec(memory_space=pltpu.SMEM)]
        + [pl.BlockSpec(memory_space=pltpu.VMEM)] * len(ins),
        out_specs=[pl.BlockSpec(memory_space=pltpu.VMEM)] * 6,
        scratch_shapes=[pltpu.VMEM((1024, MODEL), BF)] * 2,
        compiler_params=pltpu.CompilerParams(vmem_limit_bytes=40 * 1024 * 1024),
        cost_estimate=pl.CostEstimate(
            flops=6 * 10**9, bytes_accessed=20 * 10**6, transcendentals=10**6
        ),
    )(dp.reshape(1), *ins)


def per_device(
    queries, keys, values, out_weight, ffn_input, routes, gates, up_weight, down_weight, out_grad
):
    seq = lax.axis_index("seq")
    dp = lax.axis_index("dp")
    z_hi = (seq // 8) % 2
    tok, model = ffn_input.shape[1:]
    n_seq = lax.axis_size("seq")
    plane = n_seq // 2
    frames = ffn_input[0]
    cotan = out_grad[0]

    with jax.named_scope("meta"):
        chosen = routes[0].T.reshape(1, 2 * tok)
        named = chosen == jnp.arange(n_seq, dtype=jnp.int32)[:, None]
        order = jnp.arange(2 * tok)
        before = (order[:, None] < order[None, :]).astype(BF)
        counts = dot(named.astype(BF), before)
        rank = jnp.sum(jnp.where(named, counts, 0.0), axis=0, keepdims=True)
        note = jnp.concatenate(
            [
                chosen.astype(BF),
                rank.astype(BF),
                gates[0].T.reshape(1, 2 * tok),
                jnp.zeros((1, 2 * tok), BF),
            ],
            axis=1,
        )
        payload = jnp.concatenate([frames, note, jnp.zeros((15, model), BF), cotan], axis=0)
    n_x = tok + 16
    with jax.named_scope("tokens_z"):
        above = along_z(payload, lambda z: z - 2)
        below = along_z(payload, lambda z: z + 2)
        across_x = along_z(above[:n_x], lambda z: z - 2)
        across_g = along_z(below[n_x:], lambda z: z + 2)

    with jax.named_scope("weights_z"):
        half = dp // 2
        up_mine = lax.dynamic_slice(up_weight[0], (0, half * 1024), (256, 1024))
        up_other = lax.dynamic_slice(up_weight[0], (0, (1 - half) * 1024), (256, 1024))
        pack = jnp.concatenate([up_mine, down_weight[0]], axis=0)
        pack, up_other, _, _ = lax.optimization_barrier((pack, up_other, across_x, across_g))
        pack1 = along_z(pack, lambda z: z ^ 1)
        up_first = [along_z(up_other[:CUT], lambda z, j=j: z ^ j) for j in (2, 3)]
        up_second = after(up_other[CUT:], *up_first)
        up_second = [along_z(up_second, lambda z, j=j: z ^ j) for j in (2, 3)]

    def rows_of(note_row, stride, offset):
        expert = note_row[0, : 2 * tok].astype(jnp.int32)
        place = (expert // 16) * 8 + expert % 8
        here = (expert // 8) % 2 == z_hi
        row = place * stride + offset + note_row[0, 2 * tok : 4 * tok].astype(jnp.int32)
        row = jnp.where(here, row, -1).reshape(2, tok)
        return row, note_row[0, 4 * tok : 6 * tok].reshape(2, tok)

    def placing(row, total):
        spots = jnp.arange(total, dtype=jnp.int32)[:, None]
        return [spots == row[t][None, :] for t in range(2)]

    def merged(hits, gate=None):
        if gate is None:
            return (hits[0] | hits[1]).astype(BF)
        zero = jnp.zeros((), BF)
        return jnp.where(hits[0], gate[0][None, :], jnp.where(hits[1], gate[1][None, :], zero))

    class Sets:
        def __init__(self, notes, xs, gs):
            n = len(notes)
            self.n = n
            found = [rows_of(note_row, n * SLOT, k * SLOT) for k, note_row in enumerate(notes)]
            self.hits = placing(jnp.concatenate([f[0] for f in found], axis=1), plane * n * SLOT)
            self.gate = jnp.concatenate([f[1] for f in found], axis=1)
            self.x = xs[0] if n == 1 else jnp.concatenate(xs, axis=0)
            self.g = gs[0] if n == 1 else jnp.concatenate(gs, axis=0)

        def packed(self):
            shape = (plane, self.n * SLOT, model)
            send_x = dot(merged(self.hits), self.x).astype(BF).reshape(shape)
            send_g = dot(merged(self.hits, self.gate), self.g).astype(BF).reshape(shape)
            return jnp.concatenate([send_x, send_g], axis=1)

    with jax.named_scope("out_own"):
        own = Sets([note], [frames], [cotan])
        got_own = plane_exchange(own.packed())
    with jax.named_scope("out_near"):
        near = Sets(
            [above[tok : tok + 1], below[tok : tok + 1]],
            [above[:tok], below[:tok]],
            [above[n_x:], below[n_x:]],
        )
        got_near = plane_exchange(after(near.packed(), got_own, pack, up_other))
    with jax.named_scope("out_across"):
        across = Sets([across_x[tok : tok + 1]], [across_x[:tok]], [across_g])
        got_across = plane_exchange(after(across.packed(), got_near, *up_first))

    with jax.named_scope("attn_fwd"):
        steps = halo_steps(seq)
        kv_own = jnp.concatenate([keys[0], values[0]], axis=1)

    with jax.named_scope("experts"):
        pack1, *up_second = lax.optimization_barrier((pack1, *up_second, got_across))[:3]
        back, x_rows, g_rows, act, pre_grad, gate_wide = experts(
            dp, got_near, got_across, got_own, up_mine, pack1, up_first, up_second,
            down_weight[0],
        )
    with jax.named_scope("back"):
        returned = plane_exchange(back.reshape(plane, 4 * SLOT, model))

    with jax.named_scope("weight_grads"):
        down_term = dot(act, g_rows, ((0,), (0,))).astype(BF)
        up_term = dot(x_rows, pre_grad, ((0,), (0,))).astype(BF)

        def down_part(j):
            return lax.dynamic_slice(down_term, (((dp ^ j) % 2) * 512, 0), (512, model))

        def up_part(j):
            return lax.dynamic_slice(up_term, ((dp ^ j) * 256, 0), (256, 1024))

        down_far = along_z(down_part(1), lambda z: z ^ 1)

    with jax.named_scope("attn_fwd"):
        kv = halo(after(kv_own, down_term))
        shared_own, lse = attn_forward(steps, queries[0], kv)
        shared = halo(shared_own)

    with jax.named_scope("back"):
        found = [
            rows_of(note_row, 4 * SLOT, k * SLOT)
            for k, note_row in enumerate(
                [above[tok : tok + 1], below[tok : tok + 1], across_x[tok : tok + 1], note]
            )
        ]
        all_hits = placing(jnp.concatenate([f[0] for f in found], axis=1), plane * 4 * SLOT)
        all_place = after(merged(all_hits), back)
        sums = dot(all_place, returned.reshape(-1, model), ((0,), (0,)))
        far_sums = sums[: 3 * tok].astype(BF)
        gate_pack = gate_wide[:, 0].reshape(plane, 4 * SLOT).astype(BF)
        far_sums = [far_sums[k * tok : (k + 1) * tok] for k in range(3)]
        *far_sums, gate_pack = lax.optimization_barrier(
            (*far_sums, gate_pack, down_far)
        )[:4]
        from_below = along_z(far_sums[0], lambda z: z + 2)
        from_above = along_z(far_sums[1], lambda z: z - 2)
        from_across = along_z(far_sums[2], lambda z: z + 4)
        total = cotan.astype(F32) + sums[3 * tok :]
        total = total + from_below.astype(F32) + from_above.astype(F32) + from_across.astype(F32)
        input_grad = total.astype(BF)

    with jax.named_scope("gate_back"):
        ret_gate = plane_exchange(gate_pack).astype(F32).reshape(-1, 1)
        gate_sums = jnp.stack([jnp.sum(jnp.where(h, ret_gate, 0.0), axis=0) for h in all_hits])

    with jax.named_scope("weight_grads"):
        up_far = [
            along_z(after(up_part(j), input_grad), lambda z, j=j: z ^ j) for j in (1, 2, 3)
        ]
        same = up_part(0).astype(F32) + up_far[0].astype(F32)
        opposite = up_far[1].astype(F32) + up_far[2].astype(F32)
        first = jnp.where(half == 0, same, opposite).astype(BF)
        second = jnp.where(half == 0, opposite, same).astype(BF)
        up_grad = jnp.concatenate([first, second], axis=1)
        down_grad = (down_part(0).astype(F32) + down_far.astype(F32)).astype(BF)

    with jax.named_scope("attn_bwd"):
        attn_grad = dot_nt(input_grad, out_weight).astype(BF)
        do = halo(after(attn_grad, *shared))
        weight_term = dot(shared_own[:tok, WIDTH:], input_grad, ((0,), (0,))).astype(BF)

    with jax.named_scope("out_weight"):
        rows = WIDTH // plane
        parts = plane_exchange(weight_term.reshape(plane, rows, model))
        part = jnp.sum(parts.astype(F32), axis=0)
        part_b = part.astype(BF)
        part_first = part_b
        for k in (1, 2, 3):
            part = part + along_z(part_b, lambda z, k=k: z ^ k).astype(F32)
        part_b = part.astype(BF)
        part = part_b.astype(F32) + along_z(part_b, lambda z: z + 4).astype(F32)
        whole = jnp.broadcast_to(part.astype(BF)[None], (plane, rows, model))
        out_weight_grad = plane_exchange(whole).reshape(WIDTH, model)

    with jax.named_scope("gate_back"):
        gate_far = after(gate_sums.astype(BF), whole)
        gate_sum = gate_sums[:, 3 * tok :]
        gate_moves = [lambda z: z + 2, lambda z: z - 2, lambda z: z + 4]
        for k, move in enumerate(gate_moves):
            part = along_z(gate_far[:, k * tok : (k + 1) * tok], move)
            gate_sum = gate_sum + part.astype(F32)
        gate_grad = gate_sum.T / gates[0].astype(F32)

    with jax.named_scope("attn_bwd"):
        query_grad = attn_queries(steps, shared_own, lse, attn_grad, kv)
        key_grad, value_grad = attn_keys(steps, after(kv_own, part_first), shared, do)

    return (
        input_grad[None],
        query_grad[None],
        key_grad[None],
        value_grad[None],
        out_weight_grad,
        up_grad[None],
        down_grad[None],
        gate_grad[None],
    )


def solution(mesh):
    rows = P("dp", "seq", None)
    weights = P("seq", "dp", None)
    return jax.shard_map(
        per_device,
        mesh=mesh,
        in_specs=(rows, rows, rows, P(), rows, rows, rows, weights, weights, rows),
        out_specs=(rows, rows, rows, rows, P(), weights, weights, rows),
        check_vma=False,
    )
```

```python
import functools

import jax
import jax.numpy as jnp
from jax import lax
from jax.experimental import pallas as pl
from jax.experimental.pallas import tpu as pltpu
from jax.sharding import PartitionSpec as P

HEADS = 8
HEAD = 64
SLOT = 8
TOK = 128
WIDTH = HEADS * HEAD
MODEL = 1024
SCALE = HEAD ** (-0.5)
LOW = -1e30
BOTH = ("seq", "dp")
BF = jnp.bfloat16
F32 = jnp.float32


def seq_of(x, zh, y, c):
    return ((x % 4 * 2 + zh) * 4 + y % 4) * 2 + c


PLANES = [[seq_of(x, zh, y, c) for x in range(4) for y in range(4) for c in range(2)] for zh in range(2)]


def along_z(array, move):
    pairs = []
    for x in range(4):
        for y in range(4):
            for c in range(2):
                for z in range(8):
                    to = move(z) % 8
                    pairs.append(
                        (seq_of(x, z // 4, y, c) * 4 + z % 4, seq_of(x, to // 4, y, c) * 4 + to % 4)
                    )
    return lax.ppermute(array, BOTH, pairs)


def seq_permute(array, move):
    size = lax.axis_size("seq")
    pairs = [(i, move(i)) for i in range(size) if 0 <= move(i) < size]
    return lax.ppermute(array, "seq", pairs)


def plane_exchange(array):
    return lax.all_to_all(
        array, "seq", split_axis=0, concat_axis=0, tiled=True, axis_index_groups=PLANES
    )


def after(value, *others):
    return lax.optimization_barrier((value, *others))[0]


def halo_near(array):
    swap = seq_permute(array, lambda i: i ^ 1)
    left = seq_permute(array, lambda i: i + 2)
    right = seq_permute(array, lambda i: i - 2)
    far = seq_permute(array, lambda i: i + 3 if i % 2 else i - 3)
    return [array, swap, left, right, far]


def halo_rest(array, swap, left, right, far):
    rows = array.shape[0]
    swapped = seq_permute(jnp.concatenate([left, right], axis=0), lambda i: i ^ 1)
    return [array, swap, left, swapped[:rows], right, swapped[rows:], far]


def halo(array):
    return halo_rest(*halo_near(array))


def halo_steps(seq):
    core = seq % 2
    steps = jnp.stack(
        [
            jnp.int32(0),
            1 - 2 * core,
            jnp.int32(-2),
            -1 - 2 * core,
            jnp.int32(2),
            3 - 2 * core,
            6 * core - 3,
        ]
    ).astype(jnp.int32)
    there = seq + steps
    real = ((there >= 0) & (there < lax.axis_size("seq"))).astype(jnp.int32)
    return jnp.stack([steps, real])


def dot(left, right, dims=((1,), (0,))):
    return lax.dot_general(left, right, (dims, ((), ())), preferred_element_type=F32)


def dot_nt(left, right):
    return dot(left, right, ((1,), (1,)))


def head_lanes(half):
    lane = lax.broadcasted_iota(jnp.int32, (TOK, 2 * HEAD), 1)
    return (lane < HEAD) if half == 0 else (lane >= HEAD)


def within(steps_ref, b, far_axis):
    own = lax.broadcasted_iota(jnp.int32, (TOK, TOK), 1 - far_axis)
    other = lax.broadcasted_iota(jnp.int32, (TOK, TOK), far_axis)
    gap = other + steps_ref[0, b] * TOK - own
    return (jnp.abs(gap) <= 3 * TOK) & (steps_ref[1, b] == 1)


def fwd_kernel(steps_ref, q_ref, *refs):
    kv = refs[:7]
    shared_ref, lse_ref = refs[7:9]
    lane = lax.broadcasted_iota(jnp.int32, (TOK, TOK), 1)
    lse_all = jnp.zeros((TOK, TOK), F32)
    masks = [within(steps_ref, b, 1) for b in range(7)]
    shared_ref[0:TOK, 0:WIDTH] = q_ref[...]
    for pair in range(HEADS // 2):
        cols = slice(pair * 128, pair * 128 + 128)
        vcols = slice(WIDTH + pair * 128, WIDTH + pair * 128 + 128)
        q_pair = q_ref[:, cols]
        outs = []
        for half in range(2):
            q_head = jnp.where(head_lanes(half), q_pair, jnp.zeros((), BF))
            scores = [
                jnp.where(masks[b], dot_nt(q_head, kv[b][:, cols]) * SCALE, LOW) for b in range(7)
            ]
            top = functools.reduce(jnp.maximum, scores)
            top = jnp.max(top, axis=1, keepdims=True)
            exps = [jnp.exp(s - top) for s in scores]
            total = jnp.sum(functools.reduce(jnp.add, exps), axis=1, keepdims=True)
            inv = 1.0 / total
            acc = jnp.zeros((TOK, 128), F32)
            for b in range(7):
                acc = acc + dot((exps[b] * inv).astype(BF), kv[b][:, vcols])
            outs.append(acc)
            lse_all = jnp.where(lane == 2 * pair + half, top + jnp.log(total), lse_all)
        shared_ref[0:TOK, vcols] = jnp.where(head_lanes(0), outs[0], outs[1]).astype(BF)
    lse_ref[...] = lse_all
    rows = jnp.transpose(lse_all)[0:16]
    high = rows.astype(BF)
    rows = rows - high.astype(F32)
    mid = rows.astype(BF)
    low = (rows - mid.astype(F32)).astype(BF)
    shared_ref[TOK : TOK + 16, :] = jnp.concatenate(
        [high, mid, low, jnp.zeros((16, MODEL - 3 * TOK), BF)], axis=1
    )


def query_kernel(steps_ref, shared_ref, lse_ref, do_ref, *refs):
    kv = refs[:7]
    dq_ref = refs[7]
    masks = [within(steps_ref, b, 1) for b in range(7)]
    lse_all = lse_ref[...]
    for pair in range(HEADS // 2):
        cols = slice(pair * 128, pair * 128 + 128)
        vcols = slice(WIDTH + pair * 128, WIDTH + pair * 128 + 128)
        q_pair = shared_ref[0:TOK, cols]
        do_pair = do_ref[:, cols]
        prod = do_pair.astype(F32) * shared_ref[0:TOK, vcols].astype(F32)
        outs = []
        for half in range(2):
            lanes = head_lanes(half)
            q_head = jnp.where(lanes, q_pair, jnp.zeros((), BF))
            do_head = jnp.where(lanes, do_pair, jnp.zeros((), BF))
            delta = jnp.sum(jnp.where(lanes, prod, 0.0), axis=1, keepdims=True)
            lse = lse_all[:, 2 * pair + half : 2 * pair + half + 1]
            acc = jnp.zeros((TOK, 128), F32)
            for b in range(7):
                score = dot_nt(q_head, kv[b][:, cols]) * SCALE - lse
                prob = jnp.exp(jnp.where(masks[b], score, LOW))
                dprob = dot_nt(do_head, kv[b][:, vcols])
                dscore = (prob * (dprob - delta) * SCALE).astype(BF)
                acc = acc + dot(dscore, kv[b][:, cols])
            outs.append(acc)
        dq_ref[:, cols] = jnp.where(head_lanes(0), outs[0], outs[1]).astype(BF)


def key_kernel(steps_ref, kv_ref, *refs):
    shared = refs[:7]
    do = refs[7:14]
    dk_ref, dv_ref, lse_scr, delta_scr = refs[14:18]
    masks = [within(steps_ref, b, 1) for b in range(7)]
    row = lax.broadcasted_iota(jnp.int32, (16, WIDTH), 0)
    col = lax.broadcasted_iota(jnp.int32, (16, WIDTH), 1)
    pick = ((col >= row * HEAD) & (col < row * HEAD + HEAD)).astype(BF)
    for b in range(7):
        tail = shared[b][TOK : TOK + 16, 0 : 3 * TOK].astype(F32)
        lse_scr[b] = tail[:, 0:TOK] + tail[:, TOK : 2 * TOK] + tail[:, 2 * TOK :]
        prod = do[b][...].astype(F32) * shared[b][0:TOK, WIDTH:].astype(F32)
        high = prod.astype(BF)
        prod = prod - high.astype(F32)
        mid = prod.astype(BF)
        low = (prod - mid.astype(F32)).astype(BF)
        delta_scr[b] = dot_nt(pick, high) + dot_nt(pick, mid) + dot_nt(pick, low)
    for pair in range(HEADS // 2):
        cols = slice(pair * 128, pair * 128 + 128)
        vcols = slice(WIDTH + pair * 128, WIDTH + pair * 128 + 128)
        k_pair = kv_ref[:, cols]
        v_pair = kv_ref[:, vcols]
        dks, dvs = [], []
        for half in range(2):
            head = 2 * pair + half
            lanes = head_lanes(half)
            k_head = jnp.where(lanes, k_pair, jnp.zeros((), BF))
            v_head = jnp.where(lanes, v_pair, jnp.zeros((), BF))
            dk = jnp.zeros((TOK, 128), F32)
            dv = jnp.zeros((TOK, 128), F32)
            for b in range(7):
                q_b = shared[b][0:TOK, cols]
                do_b = do[b][:, cols]
                score = dot_nt(k_head, q_b) * SCALE - lse_scr[b, head : head + 1, :]
                prob = jnp.exp(jnp.where(masks[b], score, LOW))
                dprob = dot_nt(v_head, do_b)
                dscore = (prob * (dprob - delta_scr[b, head : head + 1, :]) * SCALE).astype(BF)
                dk = dk + dot(dscore, q_b)
                dv = dv + dot(prob.astype(BF), do_b)
            dks.append(dk)
            dvs.append(dv)
        dk_ref[:, cols] = jnp.where(head_lanes(0), dks[0], dks[1]).astype(BF)
        dv_ref[:, cols] = jnp.where(head_lanes(0), dvs[0], dvs[1]).astype(BF)


def on_chip(body, outs, n_in, scratch=()):
    return pl.pallas_call(
        body,
        out_shape=outs,
        in_specs=[pl.BlockSpec(memory_space=pltpu.SMEM)]
        + [pl.BlockSpec(memory_space=pltpu.VMEM)] * (n_in - 1),
        out_specs=[pl.BlockSpec(memory_space=pltpu.VMEM)] * len(outs),
        scratch_shapes=list(scratch),
        compiler_params=pltpu.CompilerParams(vmem_limit_bytes=24 * 1024 * 1024),
        cost_estimate=pl.CostEstimate(flops=10**6, bytes_accessed=10**5, transcendentals=10**3),
    )


def attn_forward(steps, q, kv):
    outs = [
        jax.ShapeDtypeStruct((TOK + 16, MODEL), BF),
        jax.ShapeDtypeStruct((TOK, TOK), F32),
    ]
    return on_chip(fwd_kernel, outs, 9)(steps, q, *kv)


def attn_queries(steps, shared, lse, do, kv):
    outs = [jax.ShapeDtypeStruct((TOK, WIDTH), BF)]
    return on_chip(query_kernel, outs, 11)(steps, shared, lse, do, *kv)[0]


def attn_keys(steps, kv, shared, do):
    outs = [jax.ShapeDtypeStruct((TOK, WIDTH), BF)] * 2
    scratch = [pltpu.VMEM((7, 16, TOK), F32), pltpu.VMEM((7, 16, TOK), F32)]
    return on_chip(key_kernel, outs, 16, scratch)(steps, kv, *shared, *do)


def experts_kernel(
    dp_ref, near_ref, across_ref, own_ref, mine_ref, pack_ref, u2_ref, u3_ref,
    down_ref, back_ref, x_ref, g_ref, act_ref, pg_ref, gate_ref, up_scr, down_scr,
):
    dp = dp_ref[0]

    def place(scr, block, rows, value):
        scr[pl.ds(pl.multiple_of(block * rows, rows), rows), :] = value

    place(up_scr, dp, 256, mine_ref[...])
    place(up_scr, dp ^ 1, 256, pack_ref[0:256])
    place(up_scr, dp ^ 2, 256, u2_ref[...])
    place(up_scr, dp ^ 3, 256, u3_ref[...])
    place(down_scr, dp & 1, 512, down_ref[...])
    place(down_scr, (dp & 1) ^ 1, 512, pack_ref[256:768])

    def tile(i, carry):
        base = pl.multiple_of(i * 256, 256)
        for p in range(8):
            here = pl.ds(base + p * 32, 16)
            there = pl.ds(base + p * 32 + 16, 16)
            near = near_ref[i * 8 + p]
            x_ref[here, :] = near[0:16]
            g_ref[here, :] = near[16:32]
            across = across_ref[i * 8 + p].astype(F32)
            own = own_ref[i * 8 + p].astype(F32)
            x_ref[there, :] = jnp.concatenate([across[0:8], own[0:8]], axis=0).astype(BF)
            g_ref[there, :] = jnp.concatenate([across[8:16], own[8:16]], axis=0).astype(BF)
        rows = pl.ds(base, 256)
        pre = dot(x_ref[rows, :], up_scr[...])
        act_grad = dot_nt(g_ref[rows, :], down_scr[...])
        sig = 1.0 / (1.0 + jnp.exp(-pre))
        act = (pre * sig).astype(BF)
        act_ref[rows, :] = act
        gate = jnp.sum(act.astype(F32) * act_grad, axis=1, keepdims=True)
        gate_ref[rows, :] = jnp.broadcast_to(gate, (256, 128))
        pg_ref[rows, :] = (act_grad * (sig * (1.0 + pre * (1.0 - sig)))).astype(BF)
        back_ref[rows, :] = dot_nt(pg_ref[rows, :], up_scr[...]).astype(BF)
        return carry

    lax.fori_loop(0, 4, tile, 0)


def experts(dp, near, across, own, mine, pack, up_two, up_three, down):
    big = jax.ShapeDtypeStruct((1024, MODEL), BF)
    ins = [near, across, own, mine, pack, up_two, up_three, down]
    return pl.pallas_call(
        experts_kernel,
        out_shape=[big] * 5 + [jax.ShapeDtypeStruct((1024, 128), F32)],
        in_specs=[pl.BlockSpec(memory_space=pltpu.SMEM)]
        + [pl.BlockSpec(memory_space=pltpu.VMEM)] * len(ins),
        out_specs=[pl.BlockSpec(memory_space=pltpu.VMEM)] * 6,
        scratch_shapes=[pltpu.VMEM((1024, MODEL), BF)] * 2,
        compiler_params=pltpu.CompilerParams(vmem_limit_bytes=40 * 1024 * 1024),
        cost_estimate=pl.CostEstimate(
            flops=6 * 10**9, bytes_accessed=20 * 10**6, transcendentals=10**6
        ),
    )(dp.reshape(1), *ins)


def per_device(
    queries, keys, values, out_weight, ffn_input, routes, gates, up_weight, down_weight, out_grad
):
    seq = lax.axis_index("seq")
    dp = lax.axis_index("dp")
    z_hi = (seq // 8) % 2
    tok, model = ffn_input.shape[1:]
    n_seq = lax.axis_size("seq")
    plane = n_seq // 2
    frames = ffn_input[0]
    cotan = out_grad[0]

    with jax.named_scope("meta"):
        chosen = routes[0].T.reshape(1, 2 * tok)
        named = chosen == jnp.arange(n_seq, dtype=jnp.int32)[:, None]
        order = jnp.arange(2 * tok)
        before = (order[:, None] < order[None, :]).astype(BF)
        counts = dot(named.astype(BF), before)
        rank = jnp.sum(jnp.where(named, counts, 0.0), axis=0, keepdims=True)
        note = jnp.concatenate(
            [
                chosen.astype(BF),
                rank.astype(BF),
                gates[0].T.reshape(1, 2 * tok),
                jnp.zeros((1, 2 * tok), BF),
            ],
            axis=1,
        )
        payload = jnp.concatenate([frames, note, jnp.zeros((15, model), BF), cotan], axis=0)
    n_x = tok + 16
    with jax.named_scope("tokens_z"):
        above = along_z(payload, lambda z: z - 2)
        below = along_z(payload, lambda z: z + 2)
        across_x = along_z(above[:n_x], lambda z: z - 2)
        across_g = along_z(below[n_x:], lambda z: z + 2)

    with jax.named_scope("weights_z"):
        half = dp // 2
        up_mine = lax.dynamic_slice(up_weight[0], (0, half * 1024), (256, 1024))
        up_other = lax.dynamic_slice(up_weight[0], (0, (1 - half) * 1024), (256, 1024))
        pack = jnp.concatenate([up_mine, down_weight[0]], axis=0)
        pack, up_other, _, _ = lax.optimization_barrier((pack, up_other, across_x, across_g))
        pack1 = along_z(pack, lambda z: z ^ 1)
        up_two = along_z(up_other, lambda z: z ^ 2)
        up_three = along_z(up_two, lambda z: z ^ 1)

    def rows_of(note_row, stride, offset):
        expert = note_row[0, : 2 * tok].astype(jnp.int32)
        place = (expert // 16) * 8 + expert % 8
        here = (expert // 8) % 2 == z_hi
        row = place * stride + offset + note_row[0, 2 * tok : 4 * tok].astype(jnp.int32)
        row = jnp.where(here, row, -1).reshape(2, tok)
        return row, note_row[0, 4 * tok : 6 * tok].reshape(2, tok)

    def placing(row, total):
        spots = jnp.arange(total, dtype=jnp.int32)[:, None]
        return [spots == row[t][None, :] for t in range(2)]

    def merged(hits, gate=None):
        if gate is None:
            return (hits[0] | hits[1]).astype(BF)
        zero = jnp.zeros((), BF)
        return jnp.where(hits[0], gate[0][None, :], jnp.where(hits[1], gate[1][None, :], zero))

    class Sets:
        def __init__(self, notes, xs, gs):
            n = len(notes)
            self.n = n
            found = [rows_of(note_row, n * SLOT, k * SLOT) for k, note_row in enumerate(notes)]
            self.hits = placing(jnp.concatenate([f[0] for f in found], axis=1), plane * n * SLOT)
            self.gate = jnp.concatenate([f[1] for f in found], axis=1)
            self.x = xs[0] if n == 1 else jnp.concatenate(xs, axis=0)
            self.g = gs[0] if n == 1 else jnp.concatenate(gs, axis=0)

        def packed(self):
            shape = (plane, self.n * SLOT, model)
            send_x = dot(merged(self.hits), self.x).astype(BF).reshape(shape)
            send_g = dot(merged(self.hits, self.gate), self.g).astype(BF).reshape(shape)
            return jnp.concatenate([send_x, send_g], axis=1)

    with jax.named_scope("out_own"):
        own = Sets([note], [frames], [cotan])
        got_own = plane_exchange(own.packed())
    with jax.named_scope("attn_fwd"):
        steps = halo_steps(seq)
        kv_own = jnp.concatenate([keys[0], values[0]], axis=1)
        kv = halo(after(kv_own, above, below))
        shared_own, lse = attn_forward(steps, queries[0], kv)
        shared_near = halo_near(after(shared_own, up_two))
    with jax.named_scope("out_near"):
        near = Sets(
            [above[tok : tok + 1], below[tok : tok + 1]],
            [above[:tok], below[:tok]],
            [above[n_x:], below[n_x:]],
        )
        got_near = plane_exchange(after(near.packed(), got_own, pack, up_other, *kv[1:]))
    with jax.named_scope("out_across"):
        across = Sets([across_x[tok : tok + 1]], [across_x[:tok]], [across_g])
        got_across = plane_exchange(after(across.packed(), got_near, shared_own))

    with jax.named_scope("experts"):
        pack1, up_three, _ = lax.optimization_barrier((pack1, up_three, got_across))
        back, x_rows, g_rows, act, pre_grad, gate_wide = experts(
            dp, got_near, got_across, got_own, up_mine, pack1, up_two, up_three,
            down_weight[0],
        )
        back = after(back, *shared_near)

    with jax.named_scope("back"):
        returned = plane_exchange(back.reshape(plane, 4 * SLOT, model))

    with jax.named_scope("weight_grads"):
        down_term = dot(act, g_rows, ((0,), (0,))).astype(BF)
        up_term = dot(x_rows, pre_grad, ((0,), (0,))).astype(BF)

        def down_part(j):
            return lax.dynamic_slice(down_term, (((dp ^ j) % 2) * 512, 0), (512, model))

        def up_part(j):
            return lax.dynamic_slice(up_term, ((dp ^ j) * 256, 0), (256, 1024))

        pair_far = along_z(
            jnp.concatenate([down_part(1), up_part(3)], axis=0), lambda z: z ^ 1
        )
        pair_sum = (up_part(2).astype(F32) + pair_far[512:].astype(F32)).astype(BF)

    with jax.named_scope("attn_fwd"):
        shared = halo_rest(*shared_near)

    with jax.named_scope("back"):
        found = [
            rows_of(note_row, 4 * SLOT, k * SLOT)
            for k, note_row in enumerate(
                [above[tok : tok + 1], below[tok : tok + 1], across_x[tok : tok + 1], note]
            )
        ]
        all_hits = placing(jnp.concatenate([f[0] for f in found], axis=1), plane * 4 * SLOT)
        all_place = after(merged(all_hits), back)
        sums = dot(all_place, returned.reshape(-1, model), ((0,), (0,)))
        far_sums = sums[: 3 * tok].astype(BF)
        gate_pack = gate_wide[:, 0].reshape(plane, 4 * SLOT).astype(BF)
        far_sums = [far_sums[k * tok : (k + 1) * tok] for k in range(3)]
        *far_sums, gate_pack = lax.optimization_barrier(
            (*far_sums, gate_pack, pair_far)
        )[:4]
        from_below = along_z(far_sums[0], lambda z: z + 2)
        from_above = along_z(far_sums[1], lambda z: z - 2)
        from_across = along_z(far_sums[2], lambda z: z + 4)
        total = cotan.astype(F32) + sums[3 * tok :]
        total = total + from_below.astype(F32) + from_above.astype(F32) + from_across.astype(F32)
        input_grad = total.astype(BF)

    with jax.named_scope("gate_back"):
        ret_gate = plane_exchange(gate_pack)

    with jax.named_scope("weight_grads"):
        up_near = along_z(after(up_part(1), input_grad), lambda z: z ^ 1)
        up_cross = along_z(after(pair_sum, input_grad), lambda z: z ^ 2)
        same = up_part(0).astype(F32) + up_near.astype(F32)
        opposite = up_cross.astype(F32)
        first = jnp.where(half == 0, same, opposite).astype(BF)
        second = jnp.where(half == 0, opposite, same).astype(BF)
        up_grad = jnp.concatenate([first, second], axis=1)
        down_grad = (down_part(0).astype(F32) + pair_far[:512].astype(F32)).astype(BF)

    with jax.named_scope("attn_bwd"):
        attn_grad = dot_nt(input_grad, out_weight).astype(BF)
        do = halo(after(attn_grad, *shared))
        weight_term = dot(shared_own[:tok, WIDTH:], input_grad, ((0,), (0,))).astype(BF)

    with jax.named_scope("out_weight"):
        rows = WIDTH // plane
        parts = plane_exchange(weight_term.reshape(plane, rows, model))
        parts = after(parts, up_near, up_cross)
        part = jnp.sum(parts.astype(F32), axis=0)
        part_b = part.astype(BF)
        part_first = part_b
        for k in (1, 2, 3):
            part = part + along_z(part_b, lambda z, k=k: z ^ k).astype(F32)
        part_b = part.astype(BF)
        part = part_b.astype(F32) + along_z(part_b, lambda z: z + 4).astype(F32)
        whole = jnp.broadcast_to(part.astype(BF)[None], (plane, rows, model))
        out_weight_grad = plane_exchange(whole).reshape(WIDTH, model)

    with jax.named_scope("gate_back"):
        ret_gate = after(ret_gate, part_first).astype(F32).reshape(-1, 1)
        gate_sums = jnp.stack([jnp.sum(jnp.where(h, ret_gate, 0.0), axis=0) for h in all_hits])
        gate_far = after(gate_sums.astype(BF), whole)
        gate_sum = gate_sums[:, 3 * tok :]
        gate_moves = [lambda z: z + 2, lambda z: z - 2, lambda z: z + 4]
        for k, move in enumerate(gate_moves):
            part = along_z(gate_far[:, k * tok : (k + 1) * tok], move)
            gate_sum = gate_sum + part.astype(F32)
        gate_grad = gate_sum.T / gates[0].astype(F32)

    with jax.named_scope("attn_bwd"):
        query_grad = attn_queries(steps, shared_own, lse, attn_grad, kv)
        key_grad, value_grad = attn_keys(steps, after(kv_own, part_first), shared, do)

    return (
        input_grad[None],
        query_grad[None],
        key_grad[None],
        value_grad[None],
        out_weight_grad,
        up_grad[None],
        down_grad[None],
        gate_grad[None],
    )


def solution(mesh):
    rows = P("dp", "seq", None)
    weights = P("seq", "dp", None)
    return jax.shard_map(
        per_device,
        mesh=mesh,
        in_specs=(rows, rows, rows, P(), rows, rows, rows, weights, weights, rows),
        out_specs=(rows, rows, rows, rows, P(), weights, weights, rows),
        check_vma=False,
    )
```

```python
import functools

import jax
import jax.numpy as jnp
from jax import lax
from jax.experimental import pallas as pl
from jax.experimental.pallas import tpu as pltpu
from jax.sharding import PartitionSpec as P

HEADS = 8
HEAD = 64
SLOT = 8
TOK = 128
WIDTH = HEADS * HEAD
MODEL = 1024
SCALE = HEAD ** (-0.5)
LOW = -1e30
BOTH = ("seq", "dp")
BF = jnp.bfloat16
F32 = jnp.float32


def seq_of(x, zh, y, c):
    return ((x % 4 * 2 + zh) * 4 + y % 4) * 2 + c


PLANES = [[seq_of(x, zh, y, c) for x in range(4) for y in range(4) for c in range(2)] for zh in range(2)]


def along_z(array, move):
    pairs = []
    for x in range(4):
        for y in range(4):
            for c in range(2):
                for z in range(8):
                    to = move(z) % 8
                    pairs.append(
                        (seq_of(x, z // 4, y, c) * 4 + z % 4, seq_of(x, to // 4, y, c) * 4 + to % 4)
                    )
    return lax.ppermute(array, BOTH, pairs)


def seq_permute(array, move):
    size = lax.axis_size("seq")
    pairs = [(i, move(i)) for i in range(size) if 0 <= move(i) < size]
    return lax.ppermute(array, "seq", pairs)


def plane_exchange(array):
    return lax.all_to_all(
        array, "seq", split_axis=0, concat_axis=0, tiled=True, axis_index_groups=PLANES
    )


def after(value, *others):
    return lax.optimization_barrier((value, *others))[0]


def halo_near(array):
    swap = seq_permute(array, lambda i: i ^ 1)
    left = seq_permute(array, lambda i: i + 2)
    right = seq_permute(array, lambda i: i - 2)
    far = seq_permute(array, lambda i: i + 3 if i % 2 else i - 3)
    return [array, swap, left, right, far]


def halo_rest(array, swap, left, right, far):
    rows = array.shape[0]
    swapped = seq_permute(jnp.concatenate([left, right], axis=0), lambda i: i ^ 1)
    return [array, swap, left, swapped[:rows], right, swapped[rows:], far]


def halo(array):
    return halo_rest(*halo_near(array))


def halo_steps(seq):
    core = seq % 2
    steps = jnp.stack(
        [
            jnp.int32(0),
            1 - 2 * core,
            jnp.int32(-2),
            -1 - 2 * core,
            jnp.int32(2),
            3 - 2 * core,
            6 * core - 3,
        ]
    ).astype(jnp.int32)
    there = seq + steps
    real = ((there >= 0) & (there < lax.axis_size("seq"))).astype(jnp.int32)
    return jnp.stack([steps, real])


def dot(left, right, dims=((1,), (0,))):
    return lax.dot_general(left, right, (dims, ((), ())), preferred_element_type=F32)


def dot_nt(left, right):
    return dot(left, right, ((1,), (1,)))


def head_lanes(half):
    lane = lax.broadcasted_iota(jnp.int32, (TOK, 2 * HEAD), 1)
    return (lane < HEAD) if half == 0 else (lane >= HEAD)


def within(steps_ref, b, far_axis):
    own = lax.broadcasted_iota(jnp.int32, (TOK, TOK), 1 - far_axis)
    other = lax.broadcasted_iota(jnp.int32, (TOK, TOK), far_axis)
    gap = other + steps_ref[0, b] * TOK - own
    return (jnp.abs(gap) <= 3 * TOK) & (steps_ref[1, b] == 1)


def fwd_kernel(steps_ref, q_ref, *refs):
    kv = refs[:7]
    shared_ref, lse_ref = refs[7:9]
    lane = lax.broadcasted_iota(jnp.int32, (TOK, TOK), 1)
    lse_all = jnp.zeros((TOK, TOK), F32)
    masks = [within(steps_ref, b, 1) for b in range(7)]
    shared_ref[0:TOK, 0:WIDTH] = q_ref[...]
    for pair in range(HEADS // 2):
        cols = slice(pair * 128, pair * 128 + 128)
        vcols = slice(WIDTH + pair * 128, WIDTH + pair * 128 + 128)
        q_pair = q_ref[:, cols]
        outs = []
        for half in range(2):
            q_head = jnp.where(head_lanes(half), q_pair, jnp.zeros((), BF))
            scores = [
                jnp.where(masks[b], dot_nt(q_head, kv[b][:, cols]) * SCALE, LOW) for b in range(7)
            ]
            top = functools.reduce(jnp.maximum, scores)
            top = jnp.max(top, axis=1, keepdims=True)
            exps = [jnp.exp(s - top) for s in scores]
            total = jnp.sum(functools.reduce(jnp.add, exps), axis=1, keepdims=True)
            inv = 1.0 / total
            acc = jnp.zeros((TOK, 128), F32)
            for b in range(7):
                acc = acc + dot((exps[b] * inv).astype(BF), kv[b][:, vcols])
            outs.append(acc)
            lse_all = jnp.where(lane == 2 * pair + half, top + jnp.log(total), lse_all)
        shared_ref[0:TOK, vcols] = jnp.where(head_lanes(0), outs[0], outs[1]).astype(BF)
    lse_ref[...] = lse_all
    rows = jnp.transpose(lse_all)[0:16]
    high = rows.astype(BF)
    rows = rows - high.astype(F32)
    mid = rows.astype(BF)
    low = (rows - mid.astype(F32)).astype(BF)
    shared_ref[TOK : TOK + 16, :] = jnp.concatenate(
        [high, mid, low, jnp.zeros((16, MODEL - 3 * TOK), BF)], axis=1
    )


def query_kernel(steps_ref, shared_ref, lse_ref, do_ref, *refs):
    kv = refs[:7]
    dq_ref = refs[7]
    masks = [within(steps_ref, b, 1) for b in range(7)]
    lse_all = lse_ref[...]
    for pair in range(HEADS // 2):
        cols = slice(pair * 128, pair * 128 + 128)
        vcols = slice(WIDTH + pair * 128, WIDTH + pair * 128 + 128)
        q_pair = shared_ref[0:TOK, cols]
        do_pair = do_ref[:, cols]
        prod = do_pair.astype(F32) * shared_ref[0:TOK, vcols].astype(F32)
        outs = []
        for half in range(2):
            lanes = head_lanes(half)
            q_head = jnp.where(lanes, q_pair, jnp.zeros((), BF))
            do_head = jnp.where(lanes, do_pair, jnp.zeros((), BF))
            delta = jnp.sum(jnp.where(lanes, prod, 0.0), axis=1, keepdims=True)
            lse = lse_all[:, 2 * pair + half : 2 * pair + half + 1]
            acc = jnp.zeros((TOK, 128), F32)
            for b in range(7):
                score = dot_nt(q_head, kv[b][:, cols]) * SCALE - lse
                prob = jnp.exp(jnp.where(masks[b], score, LOW))
                dprob = dot_nt(do_head, kv[b][:, vcols])
                dscore = (prob * (dprob - delta) * SCALE).astype(BF)
                acc = acc + dot(dscore, kv[b][:, cols])
            outs.append(acc)
        dq_ref[:, cols] = jnp.where(head_lanes(0), outs[0], outs[1]).astype(BF)


def key_kernel(steps_ref, kv_ref, *refs):
    shared = refs[:7]
    do = refs[7:14]
    dk_ref, dv_ref, lse_scr, delta_scr = refs[14:18]
    masks = [within(steps_ref, b, 1) for b in range(7)]
    row = lax.broadcasted_iota(jnp.int32, (16, WIDTH), 0)
    col = lax.broadcasted_iota(jnp.int32, (16, WIDTH), 1)
    pick = ((col >= row * HEAD) & (col < row * HEAD + HEAD)).astype(BF)
    for b in range(7):
        tail = shared[b][TOK : TOK + 16, 0 : 3 * TOK].astype(F32)
        lse_scr[b] = tail[:, 0:TOK] + tail[:, TOK : 2 * TOK] + tail[:, 2 * TOK :]
        prod = do[b][...].astype(F32) * shared[b][0:TOK, WIDTH:].astype(F32)
        high = prod.astype(BF)
        prod = prod - high.astype(F32)
        mid = prod.astype(BF)
        low = (prod - mid.astype(F32)).astype(BF)
        delta_scr[b] = dot_nt(pick, high) + dot_nt(pick, mid) + dot_nt(pick, low)
    for pair in range(HEADS // 2):
        cols = slice(pair * 128, pair * 128 + 128)
        vcols = slice(WIDTH + pair * 128, WIDTH + pair * 128 + 128)
        k_pair = kv_ref[:, cols]
        v_pair = kv_ref[:, vcols]
        dks, dvs = [], []
        for half in range(2):
            head = 2 * pair + half
            lanes = head_lanes(half)
            k_head = jnp.where(lanes, k_pair, jnp.zeros((), BF))
            v_head = jnp.where(lanes, v_pair, jnp.zeros((), BF))
            dk = jnp.zeros((TOK, 128), F32)
            dv = jnp.zeros((TOK, 128), F32)
            for b in range(7):
                q_b = shared[b][0:TOK, cols]
                do_b = do[b][:, cols]
                score = dot_nt(k_head, q_b) * SCALE - lse_scr[b, head : head + 1, :]
                prob = jnp.exp(jnp.where(masks[b], score, LOW))
                dprob = dot_nt(v_head, do_b)
                dscore = (prob * (dprob - delta_scr[b, head : head + 1, :]) * SCALE).astype(BF)
                dk = dk + dot(dscore, q_b)
                dv = dv + dot(prob.astype(BF), do_b)
            dks.append(dk)
            dvs.append(dv)
        dk_ref[:, cols] = jnp.where(head_lanes(0), dks[0], dks[1]).astype(BF)
        dv_ref[:, cols] = jnp.where(head_lanes(0), dvs[0], dvs[1]).astype(BF)


def on_chip(body, outs, n_in, scratch=(), moved=10**5):
    return pl.pallas_call(
        body,
        out_shape=outs,
        in_specs=[pl.BlockSpec(memory_space=pltpu.SMEM)]
        + [pl.BlockSpec(memory_space=pltpu.VMEM)] * (n_in - 1),
        out_specs=[pl.BlockSpec(memory_space=pltpu.VMEM)] * len(outs),
        scratch_shapes=list(scratch),
        compiler_params=pltpu.CompilerParams(vmem_limit_bytes=24 * 1024 * 1024),
        cost_estimate=pl.CostEstimate(flops=10**6, bytes_accessed=moved, transcendentals=10**3),
    )


def attn_forward(steps, q, kv):
    outs = [
        jax.ShapeDtypeStruct((TOK + 16, MODEL), BF),
        jax.ShapeDtypeStruct((TOK, TOK), F32),
    ]
    return on_chip(fwd_kernel, outs, 9)(steps, q, *kv)


def attn_queries(steps, shared, lse, do, kv):
    outs = [jax.ShapeDtypeStruct((TOK, WIDTH), BF)]
    return on_chip(query_kernel, outs, 11, moved=2 * 10**7)(steps, shared, lse, do, *kv)[0]


def attn_keys(steps, kv, shared, do):
    outs = [jax.ShapeDtypeStruct((TOK, WIDTH), BF)] * 2
    scratch = [pltpu.VMEM((7, 16, TOK), F32), pltpu.VMEM((7, 16, TOK), F32)]
    return on_chip(key_kernel, outs, 16, scratch, 2 * 10**7)(steps, kv, *shared, *do)


def experts_kernel(
    dp_ref, near_ref, across_ref, own_ref, mine_ref, pack_ref, u2_ref, u3_ref,
    down_ref, back_ref, x_ref, g_ref, act_ref, pg_ref, gate_ref, up_scr, down_scr,
):
    dp = dp_ref[0]

    def place(scr, block, rows, value):
        scr[pl.ds(pl.multiple_of(block * rows, rows), rows), :] = value

    place(up_scr, dp, 256, mine_ref[...])
    place(up_scr, dp ^ 1, 256, pack_ref[0:256])
    place(up_scr, dp ^ 2, 256, u2_ref[...])
    place(up_scr, dp ^ 3, 256, u3_ref[...])
    place(down_scr, dp & 1, 512, down_ref[...])
    place(down_scr, (dp & 1) ^ 1, 512, pack_ref[256:768])

    def tile(i, carry):
        base = pl.multiple_of(i * 256, 256)
        for p in range(8):
            here = pl.ds(base + p * 32, 16)
            there = pl.ds(base + p * 32 + 16, 16)
            near = near_ref[i * 8 + p]
            x_ref[here, :] = near[0:16]
            g_ref[here, :] = near[16:32]
            across = across_ref[i * 8 + p].astype(F32)
            own = own_ref[i * 8 + p].astype(F32)
            x_ref[there, :] = jnp.concatenate([across[0:8], own[0:8]], axis=0).astype(BF)
            g_ref[there, :] = jnp.concatenate([across[8:16], own[8:16]], axis=0).astype(BF)
        rows = pl.ds(base, 256)
        pre = dot(x_ref[rows, :], up_scr[...])
        act_grad = dot_nt(g_ref[rows, :], down_scr[...])
        sig = 1.0 / (1.0 + jnp.exp(-pre))
        act = (pre * sig).astype(BF)
        act_ref[rows, :] = act
        gate = jnp.sum(act.astype(F32) * act_grad, axis=1, keepdims=True)
        gate_ref[rows, :] = jnp.broadcast_to(gate, (256, 128))
        pg_ref[rows, :] = (act_grad * (sig * (1.0 + pre * (1.0 - sig)))).astype(BF)
        back_ref[rows, :] = dot_nt(pg_ref[rows, :], up_scr[...]).astype(BF)
        return carry

    lax.fori_loop(0, 4, tile, 0)


def experts(dp, near, across, own, mine, pack, up_two, up_three, down):
    big = jax.ShapeDtypeStruct((1024, MODEL), BF)
    ins = [near, across, own, mine, pack, up_two, up_three, down]
    return pl.pallas_call(
        experts_kernel,
        out_shape=[big] * 5 + [jax.ShapeDtypeStruct((1024, 128), F32)],
        in_specs=[pl.BlockSpec(memory_space=pltpu.SMEM)]
        + [pl.BlockSpec(memory_space=pltpu.VMEM)] * len(ins),
        out_specs=[pl.BlockSpec(memory_space=pltpu.VMEM)] * 6,
        scratch_shapes=[pltpu.VMEM((1024, MODEL), BF)] * 2,
        compiler_params=pltpu.CompilerParams(vmem_limit_bytes=40 * 1024 * 1024),
        cost_estimate=pl.CostEstimate(
            flops=6 * 10**9, bytes_accessed=20 * 10**6, transcendentals=10**6
        ),
    )(dp.reshape(1), *ins)


def per_device(
    queries, keys, values, out_weight, ffn_input, routes, gates, up_weight, down_weight, out_grad
):
    seq = lax.axis_index("seq")
    dp = lax.axis_index("dp")
    z_hi = (seq // 8) % 2
    tok, model = ffn_input.shape[1:]
    n_seq = lax.axis_size("seq")
    plane = n_seq // 2
    frames = ffn_input[0]
    cotan = out_grad[0]

    with jax.named_scope("attn_kv"):
        kv_own = jnp.concatenate([keys[0], values[0]], axis=1)
        kv_near = halo_near(kv_own)

    with jax.named_scope("meta"):
        chosen = routes[0].T.reshape(1, 2 * tok)
        named = chosen == jnp.arange(n_seq, dtype=jnp.int32)[:, None]
        order = jnp.arange(2 * tok)
        before = (order[:, None] < order[None, :]).astype(BF)
        counts = dot(named.astype(BF), before)
        rank = jnp.sum(jnp.where(named, counts, 0.0), axis=0, keepdims=True)
        note = jnp.concatenate(
            [
                chosen.astype(BF),
                rank.astype(BF),
                gates[0].T.reshape(1, 2 * tok),
                jnp.zeros((1, 2 * tok), BF),
            ],
            axis=1,
        )
        payload = jnp.concatenate([frames, note, jnp.zeros((15, model), BF), cotan], axis=0)
    n_x = tok + 16
    with jax.named_scope("tokens_z"):
        above = along_z(payload, lambda z: z - 2)
        below = along_z(payload, lambda z: z + 2)
        across_x = along_z(above[:n_x], lambda z: z - 2)
        across_g = along_z(below[n_x:], lambda z: z + 2)

    with jax.named_scope("weights_z"):
        half = dp // 2
        up_mine = lax.dynamic_slice(up_weight[0], (0, half * 1024), (256, 1024))
        up_other = lax.dynamic_slice(up_weight[0], (0, (1 - half) * 1024), (256, 1024))
        pack = jnp.concatenate([up_mine, down_weight[0]], axis=0)
        pack, up_other, _, _ = lax.optimization_barrier((pack, up_other, across_x, across_g))
        pack1 = along_z(pack, lambda z: z ^ 1)
        up_two = along_z(up_other, lambda z: z ^ 2)
        up_three = along_z(up_two, lambda z: z ^ 1)

    def rows_of(note_row, stride, offset):
        expert = note_row[0, : 2 * tok].astype(jnp.int32)
        place = (expert // 16) * 8 + expert % 8
        here = (expert // 8) % 2 == z_hi
        row = place * stride + offset + note_row[0, 2 * tok : 4 * tok].astype(jnp.int32)
        row = jnp.where(here, row, -1).reshape(2, tok)
        return row, note_row[0, 4 * tok : 6 * tok].reshape(2, tok)

    def placing(row, total):
        spots = jnp.arange(total, dtype=jnp.int32)[:, None]
        return [spots == row[t][None, :] for t in range(2)]

    def merged(hits, gate=None):
        if gate is None:
            return (hits[0] | hits[1]).astype(BF)
        zero = jnp.zeros((), BF)
        return jnp.where(hits[0], gate[0][None, :], jnp.where(hits[1], gate[1][None, :], zero))

    class Sets:
        def __init__(self, notes, xs, gs):
            n = len(notes)
            self.n = n
            found = [rows_of(note_row, n * SLOT, k * SLOT) for k, note_row in enumerate(notes)]
            self.hits = placing(jnp.concatenate([f[0] for f in found], axis=1), plane * n * SLOT)
            self.gate = jnp.concatenate([f[1] for f in found], axis=1)
            self.x = xs[0] if n == 1 else jnp.concatenate(xs, axis=0)
            self.g = gs[0] if n == 1 else jnp.concatenate(gs, axis=0)

        def packed(self):
            shape = (plane, self.n * SLOT, model)
            send_x = dot(merged(self.hits), self.x).astype(BF).reshape(shape)
            send_g = dot(merged(self.hits, self.gate), self.g).astype(BF).reshape(shape)
            return jnp.concatenate([send_x, send_g], axis=1)

    with jax.named_scope("out_own"):
        own = Sets([note], [frames], [cotan])
        got_own = plane_exchange(after(own.packed(), *kv_near[2:]))
    with jax.named_scope("out_near"):
        near = Sets(
            [above[tok : tok + 1], below[tok : tok + 1]],
            [above[:tok], below[:tok]],
            [above[n_x:], below[n_x:]],
        )
        got_near = plane_exchange(after(near.packed(), got_own, pack, up_other))
    with jax.named_scope("attn_fwd"):
        steps = halo_steps(seq)
        kv_near = list(lax.optimization_barrier((*kv_near, got_near))[:5])
        kv_near[1] = seq_permute(kv_near[0], lambda i: i ^ 1)
        kv = halo_rest(*kv_near)
        shared_own, lse = attn_forward(steps, queries[0], kv)
        shared_near = halo_near(after(shared_own, up_two))
    with jax.named_scope("out_across"):
        across = Sets([across_x[tok : tok + 1]], [across_x[:tok]], [across_g])
        got_across = plane_exchange(after(across.packed(), got_near))

    with jax.named_scope("experts"):
        pack1, up_three, _ = lax.optimization_barrier((pack1, up_three, got_across))
        back, x_rows, g_rows, act, pre_grad, gate_wide = experts(
            dp, got_near, got_across, got_own, up_mine, pack1, up_two, up_three,
            down_weight[0],
        )
        back = after(back, *shared_near)

    with jax.named_scope("back"):
        returned = plane_exchange(back.reshape(plane, 4 * SLOT, model))

    with jax.named_scope("weight_grads"):
        down_term = dot(act, g_rows, ((0,), (0,))).astype(BF)
        up_term = dot(x_rows, pre_grad, ((0,), (0,))).astype(BF)

        def down_part(j):
            return lax.dynamic_slice(down_term, (((dp ^ j) % 2) * 512, 0), (512, model))

        def up_part(j):
            return lax.dynamic_slice(up_term, ((dp ^ j) * 256, 0), (256, 1024))

        down_far = along_z(down_part(1), lambda z: z ^ 1)

    with jax.named_scope("attn_fwd"):
        shared = halo_rest(*shared_near)

    with jax.named_scope("back"):
        found = [
            rows_of(note_row, 4 * SLOT, k * SLOT)
            for k, note_row in enumerate(
                [above[tok : tok + 1], below[tok : tok + 1], across_x[tok : tok + 1], note]
            )
        ]
        all_hits = placing(jnp.concatenate([f[0] for f in found], axis=1), plane * 4 * SLOT)
        all_place = after(merged(all_hits), back)
        sums = dot(all_place, returned.reshape(-1, model), ((0,), (0,)))
        far_sums = sums[: 3 * tok].astype(BF)
        gate_pack = gate_wide[:, 0].reshape(plane, 4 * SLOT).astype(BF)
        far_sums = [far_sums[k * tok : (k + 1) * tok] for k in range(3)]
        *far_sums, gate_pack = lax.optimization_barrier(
            (*far_sums, gate_pack, down_far)
        )[:4]
        from_below = along_z(far_sums[0], lambda z: z + 2)
        from_above = along_z(far_sums[1], lambda z: z - 2)
        from_across = along_z(far_sums[2], lambda z: z + 4)
        total = cotan.astype(F32) + sums[3 * tok :]
        total = total + from_below.astype(F32) + from_above.astype(F32) + from_across.astype(F32)
        input_grad = total.astype(BF)

    with jax.named_scope("gate_back"):
        ret_gate = plane_exchange(gate_pack)

    with jax.named_scope("weight_grads"):
        pair = jnp.concatenate([up_part(1), up_part(3)], axis=0)
        pair_far = along_z(after(pair, input_grad), lambda z: z ^ 1)
        pair_sum = (up_part(2).astype(F32) + pair_far[256:].astype(F32)).astype(BF)
        up_cross = along_z(pair_sum, lambda z: z ^ 2)
        same = up_part(0).astype(F32) + pair_far[:256].astype(F32)
        opposite = up_cross.astype(F32)
        first = jnp.where(half == 0, same, opposite).astype(BF)
        second = jnp.where(half == 0, opposite, same).astype(BF)
        up_grad = jnp.concatenate([first, second], axis=1)
        down_grad = (down_part(0).astype(F32) + down_far.astype(F32)).astype(BF)

    with jax.named_scope("attn_bwd"):
        attn_grad = dot_nt(input_grad, out_weight).astype(BF)
        do = halo(after(attn_grad, *shared))
        weight_term = dot(shared_own[:tok, WIDTH:], input_grad, ((0,), (0,))).astype(BF)

    with jax.named_scope("out_weight"):
        rows = WIDTH // plane
        parts = plane_exchange(weight_term.reshape(plane, rows, model))
        part = jnp.sum(parts.astype(F32), axis=0)
        part_b = part.astype(BF)
        part_first = part_b
        for k in (1, 2, 3):
            part = part + along_z(part_b, lambda z, k=k: z ^ k).astype(F32)
        part_b = part.astype(BF)
        part = part_b.astype(F32) + along_z(part_b, lambda z: z + 4).astype(F32)
        part = after(part, pair_far)
        whole = jnp.broadcast_to(part.astype(BF)[None], (plane, rows, model))
        out_weight_grad = plane_exchange(whole).reshape(WIDTH, model)

    with jax.named_scope("gate_back"):
        ret_gate = after(ret_gate, part_first).astype(F32).reshape(-1, 1)
        gate_sums = jnp.stack([jnp.sum(jnp.where(h, ret_gate, 0.0), axis=0) for h in all_hits])
        gate_far = after(gate_sums.astype(BF), whole)
        gate_sum = gate_sums[:, 3 * tok :]
        gate_moves = [lambda z: z + 2, lambda z: z - 2, lambda z: z + 4]
        for k, move in enumerate(gate_moves):
            part = along_z(gate_far[:, k * tok : (k + 1) * tok], move)
            gate_sum = gate_sum + part.astype(F32)
        gate_grad = gate_sum.T / gates[0].astype(F32)

    with jax.named_scope("attn_bwd"):
        query_grad = attn_queries(steps, shared_own, lse, attn_grad, kv)
        key_grad, value_grad = attn_keys(steps, after(kv_own, part_first), shared, do)

    return (
        input_grad[None],
        query_grad[None],
        key_grad[None],
        value_grad[None],
        out_weight_grad,
        up_grad[None],
        down_grad[None],
        gate_grad[None],
    )


def solution(mesh):
    rows = P("dp", "seq", None)
    weights = P("seq", "dp", None)
    return jax.shard_map(
        per_device,
        mesh=mesh,
        in_specs=(rows, rows, rows, P(), rows, rows, rows, weights, weights, rows),
        out_specs=(rows, rows, rows, rows, P(), weights, weights, rows),
        check_vma=False,
    )
```

```python
import functools

import jax
import jax.numpy as jnp
from jax import lax
from jax.experimental import pallas as pl
from jax.experimental.pallas import tpu as pltpu
from jax.sharding import PartitionSpec as P

HEADS = 8
HEAD = 64
SLOT = 8
TOK = 128
WIDTH = HEADS * HEAD
MODEL = 1024
SCALE = HEAD ** (-0.5)
LOW = -1e30
BOTH = ("seq", "dp")
BF = jnp.bfloat16
F32 = jnp.float32


def seq_of(x, zh, y, c):
    return ((x % 4 * 2 + zh) * 4 + y % 4) * 2 + c


PLANES = [[seq_of(x, zh, y, c) for x in range(4) for y in range(4) for c in range(2)] for zh in range(2)]


def along_z(array, move):
    pairs = []
    for x in range(4):
        for y in range(4):
            for c in range(2):
                for z in range(8):
                    to = move(z) % 8
                    pairs.append(
                        (seq_of(x, z // 4, y, c) * 4 + z % 4, seq_of(x, to // 4, y, c) * 4 + to % 4)
                    )
    return lax.ppermute(array, BOTH, pairs)


def seq_permute(array, move):
    size = lax.axis_size("seq")
    pairs = [(i, move(i)) for i in range(size) if 0 <= move(i) < size]
    return lax.ppermute(array, "seq", pairs)


def plane_exchange(array):
    return lax.all_to_all(
        array, "seq", split_axis=0, concat_axis=0, tiled=True, axis_index_groups=PLANES
    )


def after(value, *others):
    return lax.optimization_barrier((value, *others))[0]


def halo_across(array):
    far = seq_permute(array, lambda i: i + 3 if i % 2 else i - 3)
    left = seq_permute(array, lambda i: i + 2)
    right = seq_permute(array, lambda i: i - 2)
    return [far, left, right]


def halo(array, far, left, right):
    other = seq_permute(jnp.concatenate([array, left, right], axis=0), lambda i: i ^ 1)
    rows = array.shape[0]
    return [array, far, left, right] + [other[k * rows : (k + 1) * rows] for k in range(3)]


def halo_terms(terms):
    rows = terms.shape[0] // 7
    other = seq_permute(terms[4 * rows :], lambda i: i ^ 1).astype(F32)
    from_far = seq_permute(terms[rows : 2 * rows], lambda i: i - 3 if i % 2 == 0 else i + 3)
    chip = terms[2 * rows : 4 * rows].astype(F32) + other[rows:]
    from_right = seq_permute(chip[:rows].astype(BF), lambda i: i - 2)
    from_left = seq_permute(chip[rows:].astype(BF), lambda i: i + 2)
    return terms[:rows].astype(F32) + other[:rows], from_far, from_right, from_left


def halo_steps(seq):
    core = seq % 2
    steps = jnp.stack(
        [
            jnp.int32(0),
            6 * core - 3,
            jnp.int32(-2),
            jnp.int32(2),
            1 - 2 * core,
            -1 - 2 * core,
            3 - 2 * core,
        ]
    ).astype(jnp.int32)
    there = seq + steps
    real = ((there >= 0) & (there < lax.axis_size("seq"))).astype(jnp.int32)
    return jnp.stack([steps, real])


def dot(left, right, dims=((1,), (0,))):
    return lax.dot_general(left, right, (dims, ((), ())), preferred_element_type=F32)


def dot_nt(left, right):
    return dot(left, right, ((1,), (1,)))


def head_lanes(half):
    lane = lax.broadcasted_iota(jnp.int32, (TOK, 2 * HEAD), 1)
    return (lane < HEAD) if half == 0 else (lane >= HEAD)


def within(steps_ref, b, far_axis):
    own = lax.broadcasted_iota(jnp.int32, (TOK, TOK), 1 - far_axis)
    other = lax.broadcasted_iota(jnp.int32, (TOK, TOK), far_axis)
    gap = other + steps_ref[0, b] * TOK - own
    return (jnp.abs(gap) <= 3 * TOK) & (steps_ref[1, b] == 1)


def fwd_kernel(steps_ref, q_ref, *refs):
    kv = refs[:7]
    out_ref, lse_ref = refs[7:9]
    lane = lax.broadcasted_iota(jnp.int32, (TOK, TOK), 1)
    lse_all = jnp.zeros((TOK, TOK), F32)
    masks = [within(steps_ref, b, 1) for b in range(7)]
    for pair in range(HEADS // 2):
        cols = slice(pair * 128, pair * 128 + 128)
        vcols = slice(WIDTH + pair * 128, WIDTH + pair * 128 + 128)
        q_pair = q_ref[:, cols]
        outs = []
        for half in range(2):
            q_head = jnp.where(head_lanes(half), q_pair, jnp.zeros((), BF))
            scores = [
                jnp.where(masks[b], dot_nt(q_head, kv[b][:, cols]) * SCALE, LOW) for b in range(7)
            ]
            top = functools.reduce(jnp.maximum, scores)
            top = jnp.max(top, axis=1, keepdims=True)
            exps = [jnp.exp(s - top) for s in scores]
            total = jnp.sum(functools.reduce(jnp.add, exps), axis=1, keepdims=True)
            inv = 1.0 / total
            acc = jnp.zeros((TOK, 128), F32)
            for b in range(7):
                acc = acc + dot((exps[b] * inv).astype(BF), kv[b][:, vcols])
            outs.append(acc)
            lse_all = jnp.where(lane == 2 * pair + half, top + jnp.log(total), lse_all)
        out_ref[:, cols] = jnp.where(head_lanes(0), outs[0], outs[1]).astype(BF)
    lse_ref[...] = jnp.transpose(lse_all)[0:16]


def bwd_kernel(steps_ref, q_ref, out_ref, lse_ref, do_ref, *refs):
    kv = refs[:7]
    dq_ref, dkv_ref, delta_scr = refs[7:10]
    masks = [within(steps_ref, b, 0) for b in range(7)]
    row = lax.broadcasted_iota(jnp.int32, (16, WIDTH), 0)
    col = lax.broadcasted_iota(jnp.int32, (16, WIDTH), 1)
    pick = ((col >= row * HEAD) & (col < row * HEAD + HEAD)).astype(BF)
    prod = do_ref[...].astype(F32) * out_ref[...].astype(F32)
    high = prod.astype(BF)
    prod = prod - high.astype(F32)
    mid = prod.astype(BF)
    low = (prod - mid.astype(F32)).astype(BF)
    delta_scr[...] = dot_nt(pick, high) + dot_nt(pick, mid) + dot_nt(pick, low)
    for pair in range(HEADS // 2):
        cols = slice(pair * 128, pair * 128 + 128)
        vcols = slice(WIDTH + pair * 128, WIDTH + pair * 128 + 128)
        q_pair = q_ref[:, cols]
        do_pair = do_ref[:, cols]
        q_heads = [jnp.where(head_lanes(h), q_pair, jnp.zeros((), BF)) for h in range(2)]
        do_heads = [jnp.where(head_lanes(h), do_pair, jnp.zeros((), BF)) for h in range(2)]
        dqs = [jnp.zeros((TOK, 128), F32) for _ in range(2)]
        for b in range(7):
            k_pair = kv[b][:, cols]
            v_pair = kv[b][:, vcols]
            dk = jnp.zeros((TOK, 128), F32)
            dv = jnp.zeros((TOK, 128), F32)
            for half in range(2):
                head = 2 * pair + half
                score = dot_nt(k_pair, q_heads[half]) * SCALE - lse_ref[head : head + 1, :]
                prob = jnp.exp(jnp.where(masks[b], score, LOW))
                dprob = dot_nt(v_pair, do_heads[half])
                dscore = (prob * (dprob - delta_scr[head : head + 1, :]) * SCALE).astype(BF)
                dqs[half] = dqs[half] + dot(dscore, k_pair, ((0,), (0,)))
                dk = dk + dot(dscore, q_heads[half])
                dv = dv + dot(prob.astype(BF), do_heads[half])
            rows = slice(b * TOK, b * TOK + TOK)
            dkv_ref[rows, cols] = dk.astype(BF)
            dkv_ref[rows, vcols] = dv.astype(BF)
        dq_ref[:, cols] = jnp.where(head_lanes(0), dqs[0], dqs[1]).astype(BF)


def on_chip(body, outs, n_in, scratch=(), moved=10**5):
    return pl.pallas_call(
        body,
        out_shape=outs,
        in_specs=[pl.BlockSpec(memory_space=pltpu.SMEM)]
        + [pl.BlockSpec(memory_space=pltpu.VMEM)] * (n_in - 1),
        out_specs=[pl.BlockSpec(memory_space=pltpu.VMEM)] * len(outs),
        scratch_shapes=list(scratch),
        compiler_params=pltpu.CompilerParams(vmem_limit_bytes=24 * 1024 * 1024),
        cost_estimate=pl.CostEstimate(flops=10**6, bytes_accessed=moved, transcendentals=10**3),
    )


def attn_forward(steps, q, kv):
    outs = [
        jax.ShapeDtypeStruct((TOK, WIDTH), BF),
        jax.ShapeDtypeStruct((16, TOK), F32),
    ]
    return on_chip(fwd_kernel, outs, 9)(steps, q, *kv)


def attn_backward(steps, q, out, lse, do, kv):
    outs = [
        jax.ShapeDtypeStruct((TOK, WIDTH), BF),
        jax.ShapeDtypeStruct((7 * TOK, 2 * WIDTH), BF),
    ]
    scratch = [pltpu.VMEM((16, TOK), F32)]
    return on_chip(bwd_kernel, outs, 12, scratch)(steps, q, out, lse, do, *kv)


def experts_kernel(
    dp_ref, near_ref, across_ref, own_ref, mine_ref, pack_ref, u2_ref, u3_ref,
    down_ref, back_ref, x_ref, g_ref, act_ref, pg_ref, gate_ref, up_scr, down_scr,
):
    dp = dp_ref[0]

    def place(scr, block, rows, value):
        scr[pl.ds(pl.multiple_of(block * rows, rows), rows), :] = value

    place(up_scr, dp, 256, mine_ref[...])
    place(up_scr, dp ^ 1, 256, pack_ref[0:256])
    place(up_scr, dp ^ 2, 256, u2_ref[...])
    place(up_scr, dp ^ 3, 256, u3_ref[...])
    place(down_scr, dp & 1, 512, down_ref[...])
    place(down_scr, (dp & 1) ^ 1, 512, pack_ref[256:768])

    def tile(i, carry):
        base = pl.multiple_of(i * 256, 256)
        for p in range(8):
            here = pl.ds(base + p * 32, 16)
            there = pl.ds(base + p * 32 + 16, 16)
            near = near_ref[i * 8 + p]
            x_ref[here, :] = near[0:16]
            g_ref[here, :] = near[16:32]
            across = across_ref[i * 8 + p].astype(F32)
            own = own_ref[i * 8 + p].astype(F32)
            x_ref[there, :] = jnp.concatenate([across[0:8], own[0:8]], axis=0).astype(BF)
            g_ref[there, :] = jnp.concatenate([across[8:16], own[8:16]], axis=0).astype(BF)
        rows = pl.ds(base, 256)
        pre = dot(x_ref[rows, :], up_scr[...])
        act_grad = dot_nt(g_ref[rows, :], down_scr[...])
        sig = 1.0 / (1.0 + jnp.exp(-pre))
        act = (pre * sig).astype(BF)
        act_ref[rows, :] = act
        gate = jnp.sum(act.astype(F32) * act_grad, axis=1, keepdims=True)
        gate_ref[rows, :] = jnp.broadcast_to(gate, (256, 128))
        pg_ref[rows, :] = (act_grad * (sig * (1.0 + pre * (1.0 - sig)))).astype(BF)
        back_ref[rows, :] = dot_nt(pg_ref[rows, :], up_scr[...]).astype(BF)
        return carry

    lax.fori_loop(0, 4, tile, 0)


def experts(dp, near, across, own, mine, pack, up_two, up_three, down):
    big = jax.ShapeDtypeStruct((1024, MODEL), BF)
    ins = [near, across, own, mine, pack, up_two, up_three, down]
    return pl.pallas_call(
        experts_kernel,
        out_shape=[big] * 5 + [jax.ShapeDtypeStruct((1024, 128), F32)],
        in_specs=[pl.BlockSpec(memory_space=pltpu.SMEM)]
        + [pl.BlockSpec(memory_space=pltpu.VMEM)] * len(ins),
        out_specs=[pl.BlockSpec(memory_space=pltpu.VMEM)] * 6,
        scratch_shapes=[pltpu.VMEM((1024, MODEL), BF)] * 2,
        compiler_params=pltpu.CompilerParams(vmem_limit_bytes=40 * 1024 * 1024),
        cost_estimate=pl.CostEstimate(
            flops=6 * 10**9, bytes_accessed=20 * 10**6, transcendentals=10**6
        ),
    )(dp.reshape(1), *ins)


def per_device(
    queries, keys, values, out_weight, ffn_input, routes, gates, up_weight, down_weight, out_grad
):
    seq = lax.axis_index("seq")
    dp = lax.axis_index("dp")
    z_hi = (seq // 8) % 2
    tok, model = ffn_input.shape[1:]
    n_seq = lax.axis_size("seq")
    plane = n_seq // 2
    frames = ffn_input[0]
    cotan = out_grad[0]

    with jax.named_scope("attn_kv"):
        kv_own = jnp.concatenate([keys[0], values[0]], axis=1)
        kv_near = halo_across(kv_own)

    with jax.named_scope("meta"):
        chosen = routes[0].T.reshape(1, 2 * tok)
        named = chosen == jnp.arange(n_seq, dtype=jnp.int32)[:, None]
        order = jnp.arange(2 * tok)
        before = (order[:, None] < order[None, :]).astype(BF)
        counts = dot(named.astype(BF), before)
        rank = jnp.sum(jnp.where(named, counts, 0.0), axis=0, keepdims=True)
        note = jnp.concatenate(
            [
                chosen.astype(BF),
                rank.astype(BF),
                gates[0].T.reshape(1, 2 * tok),
                jnp.zeros((1, 2 * tok), BF),
            ],
            axis=1,
        )
        payload = jnp.concatenate([frames, note, jnp.zeros((15, model), BF), cotan], axis=0)
    n_x = tok + 16
    with jax.named_scope("tokens_z"):
        above = along_z(payload, lambda z: z - 2)
        below = along_z(payload, lambda z: z + 2)
        across_x = along_z(above[:n_x], lambda z: z - 2)
        across_g = along_z(below[n_x:], lambda z: z + 2)

    with jax.named_scope("weights_z"):
        half = dp // 2
        up_mine = lax.dynamic_slice(up_weight[0], (0, half * 1024), (256, 1024))
        up_other = lax.dynamic_slice(up_weight[0], (0, (1 - half) * 1024), (256, 1024))
        pack = jnp.concatenate([up_mine, down_weight[0]], axis=0)
        pack, up_other, _, _ = lax.optimization_barrier((pack, up_other, across_x, across_g))
        pack1 = along_z(pack, lambda z: z ^ 1)
        up_two = along_z(up_other, lambda z: z ^ 2)
        up_three = along_z(up_two, lambda z: z ^ 1)

    def rows_of(note_row, stride, offset):
        expert = note_row[0, : 2 * tok].astype(jnp.int32)
        place = (expert // 16) * 8 + expert % 8
        here = (expert // 8) % 2 == z_hi
        row = place * stride + offset + note_row[0, 2 * tok : 4 * tok].astype(jnp.int32)
        row = jnp.where(here, row, -1).reshape(2, tok)
        return row, note_row[0, 4 * tok : 6 * tok].reshape(2, tok)

    def placing(row, total):
        spots = jnp.arange(total, dtype=jnp.int32)[:, None]
        return [spots == row[t][None, :] for t in range(2)]

    def merged(hits, gate=None):
        if gate is None:
            return (hits[0] | hits[1]).astype(BF)
        zero = jnp.zeros((), BF)
        return jnp.where(hits[0], gate[0][None, :], jnp.where(hits[1], gate[1][None, :], zero))

    class Sets:
        def __init__(self, notes, xs, gs):
            n = len(notes)
            self.n = n
            found = [rows_of(note_row, n * SLOT, k * SLOT) for k, note_row in enumerate(notes)]
            self.hits = placing(jnp.concatenate([f[0] for f in found], axis=1), plane * n * SLOT)
            self.gate = jnp.concatenate([f[1] for f in found], axis=1)
            self.x = xs[0] if n == 1 else jnp.concatenate(xs, axis=0)
            self.g = gs[0] if n == 1 else jnp.concatenate(gs, axis=0)

        def packed(self):
            shape = (plane, self.n * SLOT, model)
            send_x = dot(merged(self.hits), self.x).astype(BF).reshape(shape)
            send_g = dot(merged(self.hits, self.gate), self.g).astype(BF).reshape(shape)
            return jnp.concatenate([send_x, send_g], axis=1)

    with jax.named_scope("out_own"):
        own = Sets([note], [frames], [cotan])
        got_own = plane_exchange(own.packed())
    with jax.named_scope("out_near"):
        near = Sets(
            [above[tok : tok + 1], below[tok : tok + 1]],
            [above[:tok], below[:tok]],
            [above[n_x:], below[n_x:]],
        )
        got_near = plane_exchange(after(near.packed(), got_own, pack, up_other, *kv_near))
    with jax.named_scope("attn_fwd"):
        steps = halo_steps(seq)
        kv = halo(after(kv_own, got_near), *kv_near)
        attn_out, lse = attn_forward(steps, queries[0], kv)
    with jax.named_scope("out_across"):
        across = Sets([across_x[tok : tok + 1]], [across_x[:tok]], [across_g])
        got_across = plane_exchange(after(across.packed(), got_near))

    with jax.named_scope("experts"):
        pack1, up_three, _ = lax.optimization_barrier((pack1, up_three, got_across))
        back, x_rows, g_rows, act, pre_grad, gate_wide = experts(
            dp, got_near, got_across, got_own, up_mine, pack1, up_two, up_three,
            down_weight[0],
        )

    with jax.named_scope("back"):
        returned = plane_exchange(back.reshape(plane, 4 * SLOT, model))

    with jax.named_scope("weight_grads"):
        down_term = dot(act, g_rows, ((0,), (0,))).astype(BF)
        up_term = dot(x_rows, pre_grad, ((0,), (0,))).astype(BF)

        def down_part(j):
            return lax.dynamic_slice(down_term, (((dp ^ j) % 2) * 512, 0), (512, model))

        def up_part(j):
            return lax.dynamic_slice(up_term, ((dp ^ j) * 256, 0), (256, 1024))

        down_far = along_z(down_part(1), lambda z: z ^ 1)

    with jax.named_scope("back"):
        found = [
            rows_of(note_row, 4 * SLOT, k * SLOT)
            for k, note_row in enumerate(
                [above[tok : tok + 1], below[tok : tok + 1], across_x[tok : tok + 1], note]
            )
        ]
        all_hits = placing(jnp.concatenate([f[0] for f in found], axis=1), plane * 4 * SLOT)
        all_place = after(merged(all_hits), back)
        sums = dot(all_place, returned.reshape(-1, model), ((0,), (0,)))
        far_sums = sums[: 3 * tok].astype(BF)
        gate_pack = gate_wide[:, 0].reshape(plane, 4 * SLOT).astype(BF)
        far_sums = [far_sums[k * tok : (k + 1) * tok] for k in range(3)]
        *far_sums, gate_pack = lax.optimization_barrier(
            (*far_sums, gate_pack, down_far)
        )[:4]
        from_below = along_z(far_sums[0], lambda z: z + 2)
        from_above = along_z(far_sums[1], lambda z: z - 2)
        from_across = along_z(far_sums[2], lambda z: z + 4)
        ret_gate = plane_exchange(gate_pack)
        total = cotan.astype(F32) + after(sums[3 * tok :], ret_gate)
        total = total + from_below.astype(F32) + from_above.astype(F32) + from_across.astype(F32)
        input_grad = total.astype(BF)


    with jax.named_scope("weight_grads"):
        pair = jnp.concatenate([up_part(1), up_part(3)], axis=0)
        pair_far = along_z(after(pair, input_grad), lambda z: z ^ 1)
        pair_sum = (up_part(2).astype(F32) + pair_far[256:].astype(F32)).astype(BF)
        up_cross = along_z(pair_sum, lambda z: z ^ 2)
        same = up_part(0).astype(F32) + pair_far[:256].astype(F32)
        opposite = up_cross.astype(F32)
        first = jnp.where(half == 0, same, opposite).astype(BF)
        second = jnp.where(half == 0, opposite, same).astype(BF)
        up_grad = jnp.concatenate([first, second], axis=1)
        down_own = down_part(0).astype(F32)

    with jax.named_scope("attn_bwd"):
        attn_grad = dot_nt(input_grad, out_weight).astype(BF)
        query_grad, terms = attn_backward(steps, queries[0], attn_out, lse, attn_grad, kv)
        key_value_terms = halo_terms(terms)
        weight_term = dot(attn_out, input_grad, ((0,), (0,))).astype(BF)

    with jax.named_scope("out_weight"):
        rows = WIDTH // plane
        parts = plane_exchange(weight_term.reshape(plane, rows, model))
        part = jnp.sum(parts.astype(F32), axis=0)
        part_b = part.astype(BF)
        part_first = part_b
        for k in (1, 2, 3):
            part = part + along_z(part_b, lambda z, k=k: z ^ k).astype(F32)
        part_b = part.astype(BF)
        part = part_b.astype(F32) + along_z(part_b, lambda z: z + 4).astype(F32)
        part = after(part, pair_far)
        whole = jnp.broadcast_to(part.astype(BF)[None], (plane, rows, model))
        out_weight_grad = plane_exchange(whole).reshape(WIDTH, model)
        key_value_terms = lax.optimization_barrier((*key_value_terms, whole))[:4]
        key_value_grad = sum(term.astype(F32) for term in key_value_terms).astype(BF)

    with jax.named_scope("gate_back"):
        ret_gate = after(ret_gate, part_first).astype(F32).reshape(-1, 1)
        gate_sums = jnp.stack([jnp.sum(jnp.where(h, ret_gate, 0.0), axis=0) for h in all_hits])
        gate_far = after(gate_sums.astype(BF), whole)
        gate_sum = gate_sums[:, 3 * tok :]
        gate_moves = [lambda z: z + 2, lambda z: z - 2, lambda z: z + 4]
        for k, move in enumerate(gate_moves):
            part = along_z(gate_far[:, k * tok : (k + 1) * tok], move)
            gate_sum = gate_sum + part.astype(F32)
        down_grad = (after(down_own, part_first) + down_far.astype(F32)).astype(BF)
        gate_grad = gate_sum.T / gates[0].astype(F32)

    return (
        input_grad[None],
        query_grad[None],
        key_value_grad[None, :, :WIDTH],
        key_value_grad[None, :, WIDTH:],
        out_weight_grad,
        up_grad[None],
        down_grad[None],
        gate_grad[None],
    )


def solution(mesh):
    rows = P("dp", "seq", None)
    weights = P("seq", "dp", None)
    return jax.shard_map(
        per_device,
        mesh=mesh,
        in_specs=(rows, rows, rows, P(), rows, rows, rows, weights, weights, rows),
        out_specs=(rows, rows, rows, rows, P(), weights, weights, rows),
        check_vma=False,
    )
```

```python
import functools

import jax
import jax.numpy as jnp
from jax import lax
from jax.experimental import pallas as pl
from jax.experimental.pallas import tpu as pltpu
from jax.sharding import PartitionSpec as P

HEADS = 8
HEAD = 64
SLOT = 8
TOK = 128
WIDTH = HEADS * HEAD
MODEL = 1024
SCALE = HEAD ** (-0.5)
LOW = -1e30
BOTH = ("seq", "dp")
BF = jnp.bfloat16
F32 = jnp.float32


def seq_of(x, zh, y, c):
    return ((x % 4 * 2 + zh) * 4 + y % 4) * 2 + c


PLANES = [[seq_of(x, zh, y, c) for x in range(4) for y in range(4) for c in range(2)] for zh in range(2)]


def along_z(array, move):
    pairs = []
    for x in range(4):
        for y in range(4):
            for c in range(2):
                for z in range(8):
                    to = move(z) % 8
                    pairs.append(
                        (seq_of(x, z // 4, y, c) * 4 + z % 4, seq_of(x, to // 4, y, c) * 4 + to % 4)
                    )
    return lax.ppermute(array, BOTH, pairs)


def seq_permute(array, move):
    size = lax.axis_size("seq")
    pairs = [(i, move(i)) for i in range(size) if 0 <= move(i) < size]
    return lax.ppermute(array, "seq", pairs)


def plane_exchange(array):
    return lax.all_to_all(
        array, "seq", split_axis=0, concat_axis=0, tiled=True, axis_index_groups=PLANES
    )


def after(value, *others):
    return lax.optimization_barrier((value, *others))[0]


def halo_across(array):
    far = seq_permute(array, lambda i: i + 3 if i % 2 else i - 3)
    left = seq_permute(array, lambda i: i + 2)
    right = seq_permute(array, lambda i: i - 2)
    return [far, left, right]


def halo(array, far, left, right):
    other = seq_permute(jnp.concatenate([array, left, right], axis=0), lambda i: i ^ 1)
    rows = array.shape[0]
    return [array, far, left, right] + [other[k * rows : (k + 1) * rows] for k in range(3)]


def halo_terms(terms):
    rows = terms.shape[0] // 7
    other = seq_permute(terms[4 * rows :], lambda i: i ^ 1).astype(F32)
    from_far = seq_permute(terms[rows : 2 * rows], lambda i: i - 3 if i % 2 == 0 else i + 3)
    chip = terms[2 * rows : 4 * rows].astype(F32) + other[rows:]
    return terms[:rows].astype(F32) + other[:rows], from_far, chip.astype(BF)


def halo_steps(seq):
    core = seq % 2
    steps = jnp.stack(
        [
            jnp.int32(0),
            6 * core - 3,
            jnp.int32(-2),
            jnp.int32(2),
            1 - 2 * core,
            -1 - 2 * core,
            3 - 2 * core,
        ]
    ).astype(jnp.int32)
    there = seq + steps
    real = ((there >= 0) & (there < lax.axis_size("seq"))).astype(jnp.int32)
    return jnp.stack([steps, real])


def dot(left, right, dims=((1,), (0,))):
    return lax.dot_general(left, right, (dims, ((), ())), preferred_element_type=F32)


def dot_nt(left, right):
    return dot(left, right, ((1,), (1,)))


def head_lanes(half):
    lane = lax.broadcasted_iota(jnp.int32, (TOK, 2 * HEAD), 1)
    return (lane < HEAD) if half == 0 else (lane >= HEAD)


def within(steps_ref, b, far_axis):
    own = lax.broadcasted_iota(jnp.int32, (TOK, TOK), 1 - far_axis)
    other = lax.broadcasted_iota(jnp.int32, (TOK, TOK), far_axis)
    gap = other + steps_ref[0, b] * TOK - own
    return (jnp.abs(gap) <= 3 * TOK) & (steps_ref[1, b] == 1)


def fwd_kernel(steps_ref, q_ref, *refs):
    kv = refs[:7]
    out_ref, lse_ref = refs[7:9]
    lane = lax.broadcasted_iota(jnp.int32, (TOK, TOK), 1)
    lse_all = jnp.zeros((TOK, TOK), F32)
    masks = [within(steps_ref, b, 1) for b in range(7)]
    for pair in range(HEADS // 2):
        cols = slice(pair * 128, pair * 128 + 128)
        vcols = slice(WIDTH + pair * 128, WIDTH + pair * 128 + 128)
        q_pair = q_ref[:, cols]
        outs = []
        for half in range(2):
            q_head = jnp.where(head_lanes(half), q_pair, jnp.zeros((), BF))
            scores = [
                jnp.where(masks[b], dot_nt(q_head, kv[b][:, cols]) * SCALE, LOW) for b in range(7)
            ]
            top = functools.reduce(jnp.maximum, scores)
            top = jnp.max(top, axis=1, keepdims=True)
            exps = [jnp.exp(s - top) for s in scores]
            total = jnp.sum(functools.reduce(jnp.add, exps), axis=1, keepdims=True)
            inv = 1.0 / total
            acc = jnp.zeros((TOK, 128), F32)
            for b in range(7):
                acc = acc + dot((exps[b] * inv).astype(BF), kv[b][:, vcols])
            outs.append(acc)
            lse_all = jnp.where(lane == 2 * pair + half, top + jnp.log(total), lse_all)
        out_ref[:, cols] = jnp.where(head_lanes(0), outs[0], outs[1]).astype(BF)
    lse_ref[...] = jnp.transpose(lse_all)[0:16]


def bwd_kernel(steps_ref, q_ref, out_ref, lse_ref, do_ref, *refs):
    kv = refs[:7]
    dq_ref, dkv_ref, delta_scr = refs[7:10]
    masks = [within(steps_ref, b, 0) for b in range(7)]
    row = lax.broadcasted_iota(jnp.int32, (16, WIDTH), 0)
    col = lax.broadcasted_iota(jnp.int32, (16, WIDTH), 1)
    pick = ((col >= row * HEAD) & (col < row * HEAD + HEAD)).astype(BF)
    prod = do_ref[...].astype(F32) * out_ref[...].astype(F32)
    high = prod.astype(BF)
    prod = prod - high.astype(F32)
    mid = prod.astype(BF)
    low = (prod - mid.astype(F32)).astype(BF)
    delta_scr[...] = dot_nt(pick, high) + dot_nt(pick, mid) + dot_nt(pick, low)
    for pair in range(HEADS // 2):
        cols = slice(pair * 128, pair * 128 + 128)
        vcols = slice(WIDTH + pair * 128, WIDTH + pair * 128 + 128)
        q_pair = q_ref[:, cols]
        do_pair = do_ref[:, cols]
        q_heads = [jnp.where(head_lanes(h), q_pair, jnp.zeros((), BF)) for h in range(2)]
        do_heads = [jnp.where(head_lanes(h), do_pair, jnp.zeros((), BF)) for h in range(2)]
        dqs = [jnp.zeros((TOK, 128), F32) for _ in range(2)]
        for b in range(7):
            k_pair = kv[b][:, cols]
            v_pair = kv[b][:, vcols]
            dk = jnp.zeros((TOK, 128), F32)
            dv = jnp.zeros((TOK, 128), F32)
            for half in range(2):
                head = 2 * pair + half
                score = dot_nt(k_pair, q_heads[half]) * SCALE - lse_ref[head : head + 1, :]
                prob = jnp.exp(jnp.where(masks[b], score, LOW))
                dprob = dot_nt(v_pair, do_heads[half])
                dscore = (prob * (dprob - delta_scr[head : head + 1, :]) * SCALE).astype(BF)
                dqs[half] = dqs[half] + dot(dscore, k_pair, ((0,), (0,)))
                dk = dk + dot(dscore, q_heads[half])
                dv = dv + dot(prob.astype(BF), do_heads[half])
            rows = slice(b * TOK, b * TOK + TOK)
            dkv_ref[rows, cols] = dk.astype(BF)
            dkv_ref[rows, vcols] = dv.astype(BF)
        dq_ref[:, cols] = jnp.where(head_lanes(0), dqs[0], dqs[1]).astype(BF)


def on_chip(body, outs, n_in, scratch=(), moved=10**5):
    return pl.pallas_call(
        body,
        out_shape=outs,
        in_specs=[pl.BlockSpec(memory_space=pltpu.SMEM)]
        + [pl.BlockSpec(memory_space=pltpu.VMEM)] * (n_in - 1),
        out_specs=[pl.BlockSpec(memory_space=pltpu.VMEM)] * len(outs),
        scratch_shapes=list(scratch),
        compiler_params=pltpu.CompilerParams(vmem_limit_bytes=24 * 1024 * 1024),
        cost_estimate=pl.CostEstimate(flops=10**6, bytes_accessed=moved, transcendentals=10**3),
    )


def attn_forward(steps, q, kv):
    outs = [
        jax.ShapeDtypeStruct((TOK, WIDTH), BF),
        jax.ShapeDtypeStruct((16, TOK), F32),
    ]
    return on_chip(fwd_kernel, outs, 9)(steps, q, *kv)


def attn_backward(steps, q, out, lse, do, kv):
    outs = [
        jax.ShapeDtypeStruct((TOK, WIDTH), BF),
        jax.ShapeDtypeStruct((7 * TOK, 2 * WIDTH), BF),
    ]
    scratch = [pltpu.VMEM((16, TOK), F32)]
    return on_chip(bwd_kernel, outs, 12, scratch)(steps, q, out, lse, do, *kv)


def experts_kernel(
    dp_ref, near_ref, across_ref, own_ref, mine_ref, pack_ref, u2_ref, u3_ref,
    down_ref, back_ref, x_ref, g_ref, act_ref, pg_ref, gate_ref, up_scr, down_scr,
):
    dp = dp_ref[0]

    def place(scr, block, rows, value):
        scr[pl.ds(pl.multiple_of(block * rows, rows), rows), :] = value

    place(up_scr, dp, 256, mine_ref[...])
    place(up_scr, dp ^ 1, 256, pack_ref[0:256])
    place(up_scr, dp ^ 2, 256, u2_ref[...])
    place(up_scr, dp ^ 3, 256, u3_ref[...])
    place(down_scr, dp & 1, 512, down_ref[...])
    place(down_scr, (dp & 1) ^ 1, 512, pack_ref[256:768])

    def tile(i, carry):
        base = pl.multiple_of(i * 256, 256)
        for p in range(8):
            here = pl.ds(base + p * 32, 16)
            there = pl.ds(base + p * 32 + 16, 16)
            near = near_ref[i * 8 + p]
            x_ref[here, :] = near[0:16]
            g_ref[here, :] = near[16:32]
            across = across_ref[i * 8 + p].astype(F32)
            own = own_ref[i * 8 + p].astype(F32)
            x_ref[there, :] = jnp.concatenate([across[0:8], own[0:8]], axis=0).astype(BF)
            g_ref[there, :] = jnp.concatenate([across[8:16], own[8:16]], axis=0).astype(BF)
        rows = pl.ds(base, 256)
        pre = dot(x_ref[rows, :], up_scr[...])
        act_grad = dot_nt(g_ref[rows, :], down_scr[...])
        sig = 1.0 / (1.0 + jnp.exp(-pre))
        act = (pre * sig).astype(BF)
        act_ref[rows, :] = act
        gate = jnp.sum(act.astype(F32) * act_grad, axis=1, keepdims=True)
        gate_ref[rows, :] = jnp.broadcast_to(gate, (256, 128))
        pg_ref[rows, :] = (act_grad * (sig * (1.0 + pre * (1.0 - sig)))).astype(BF)
        back_ref[rows, :] = dot_nt(pg_ref[rows, :], up_scr[...]).astype(BF)
        return carry

    lax.fori_loop(0, 4, tile, 0)


def experts(dp, near, across, own, mine, pack, up_two, up_three, down):
    big = jax.ShapeDtypeStruct((1024, MODEL), BF)
    ins = [near, across, own, mine, pack, up_two, up_three, down]
    return pl.pallas_call(
        experts_kernel,
        out_shape=[big] * 5 + [jax.ShapeDtypeStruct((1024, 128), F32)],
        in_specs=[pl.BlockSpec(memory_space=pltpu.SMEM)]
        + [pl.BlockSpec(memory_space=pltpu.VMEM)] * len(ins),
        out_specs=[pl.BlockSpec(memory_space=pltpu.VMEM)] * 6,
        scratch_shapes=[pltpu.VMEM((1024, MODEL), BF)] * 2,
        compiler_params=pltpu.CompilerParams(vmem_limit_bytes=40 * 1024 * 1024),
        cost_estimate=pl.CostEstimate(
            flops=6 * 10**9, bytes_accessed=20 * 10**6, transcendentals=10**6
        ),
    )(dp.reshape(1), *ins)


def per_device(
    queries, keys, values, out_weight, ffn_input, routes, gates, up_weight, down_weight, out_grad
):
    seq = lax.axis_index("seq")
    dp = lax.axis_index("dp")
    z_hi = (seq // 8) % 2
    tok, model = ffn_input.shape[1:]
    n_seq = lax.axis_size("seq")
    plane = n_seq // 2
    frames = ffn_input[0]
    cotan = out_grad[0]

    with jax.named_scope("attn_kv"):
        kv_own = jnp.concatenate([keys[0], values[0]], axis=1)

    with jax.named_scope("meta"):
        chosen = routes[0].T.reshape(1, 2 * tok)
        named = chosen == jnp.arange(n_seq, dtype=jnp.int32)[:, None]
        order = jnp.arange(2 * tok)
        before = (order[:, None] < order[None, :]).astype(BF)
        counts = dot(named.astype(BF), before)
        rank = jnp.sum(jnp.where(named, counts, 0.0), axis=0, keepdims=True)
        note = jnp.concatenate(
            [
                chosen.astype(BF),
                rank.astype(BF),
                gates[0].T.reshape(1, 2 * tok),
                jnp.zeros((1, 2 * tok), BF),
            ],
            axis=1,
        )
        payload = jnp.concatenate([frames, note, jnp.zeros((15, model), BF), cotan], axis=0)
    n_x = tok + 16
    with jax.named_scope("tokens_z"):
        above = along_z(payload, lambda z: z - 2)
        below = along_z(payload, lambda z: z + 2)
        across_x = along_z(above[:n_x], lambda z: z - 2)
        across_g = along_z(below[n_x:], lambda z: z + 2)

    with jax.named_scope("weights_z"):
        half = dp // 2
        up_mine = lax.dynamic_slice(up_weight[0], (0, half * 1024), (256, 1024))
        up_other = lax.dynamic_slice(up_weight[0], (0, (1 - half) * 1024), (256, 1024))
        pack = jnp.concatenate([up_mine, down_weight[0]], axis=0)
        pack, up_other, _, _ = lax.optimization_barrier((pack, up_other, across_x, across_g))
        pack1 = along_z(pack, lambda z: z ^ 1)
        up_two = along_z(up_other, lambda z: z ^ 2)
        up_three = along_z(up_two, lambda z: z ^ 1)

    def rows_of(note_row, stride, offset):
        expert = note_row[0, : 2 * tok].astype(jnp.int32)
        place = (expert // 16) * 8 + expert % 8
        here = (expert // 8) % 2 == z_hi
        row = place * stride + offset + note_row[0, 2 * tok : 4 * tok].astype(jnp.int32)
        row = jnp.where(here, row, -1).reshape(2, tok)
        return row, note_row[0, 4 * tok : 6 * tok].reshape(2, tok)

    def placing(row, total):
        spots = jnp.arange(total, dtype=jnp.int32)[:, None]
        return [spots == row[t][None, :] for t in range(2)]

    def merged(hits, gate=None):
        if gate is None:
            return (hits[0] | hits[1]).astype(BF)
        zero = jnp.zeros((), BF)
        return jnp.where(hits[0], gate[0][None, :], jnp.where(hits[1], gate[1][None, :], zero))

    class Sets:
        def __init__(self, notes, xs, gs):
            n = len(notes)
            self.n = n
            found = [rows_of(note_row, n * SLOT, k * SLOT) for k, note_row in enumerate(notes)]
            self.hits = placing(jnp.concatenate([f[0] for f in found], axis=1), plane * n * SLOT)
            self.gate = jnp.concatenate([f[1] for f in found], axis=1)
            self.x = xs[0] if n == 1 else jnp.concatenate(xs, axis=0)
            self.g = gs[0] if n == 1 else jnp.concatenate(gs, axis=0)

        def packed(self):
            shape = (plane, self.n * SLOT, model)
            send_x = dot(merged(self.hits), self.x).astype(BF).reshape(shape)
            send_g = dot(merged(self.hits, self.gate), self.g).astype(BF).reshape(shape)
            return jnp.concatenate([send_x, send_g], axis=1)

    with jax.named_scope("out_own"):
        own = Sets([note], [frames], [cotan])
        got_own = plane_exchange(own.packed())
    with jax.named_scope("out_near"):
        near = Sets(
            [above[tok : tok + 1], below[tok : tok + 1]],
            [above[:tok], below[:tok]],
            [above[n_x:], below[n_x:]],
        )
        got_near = plane_exchange(after(near.packed(), got_own, pack, up_other))
    with jax.named_scope("attn_fwd"):
        steps = halo_steps(seq)
        kv_near = halo_across(after(kv_own, up_two))
        kv = halo(kv_own, *kv_near)
        attn_out, lse = attn_forward(steps, queries[0], kv)
    with jax.named_scope("out_across"):
        across = Sets([across_x[tok : tok + 1]], [across_x[:tok]], [across_g])
        got_across = plane_exchange(after(across.packed(), got_near))

    with jax.named_scope("experts"):
        pack1, up_three, _ = lax.optimization_barrier((pack1, up_three, got_across))
        back, x_rows, g_rows, act, pre_grad, gate_wide = experts(
            dp, got_near, got_across, got_own, up_mine, pack1, up_two, up_three,
            down_weight[0],
        )

        back = after(back, *kv_near)

    with jax.named_scope("back"):
        returned = plane_exchange(back.reshape(plane, 4 * SLOT, model))

    with jax.named_scope("weight_grads"):
        down_term = dot(act, g_rows, ((0,), (0,))).astype(BF)
        up_term = dot(x_rows, pre_grad, ((0,), (0,))).astype(BF)

        def down_part(j):
            return lax.dynamic_slice(down_term, (((dp ^ j) % 2) * 512, 0), (512, model))

        def up_part(j):
            return lax.dynamic_slice(up_term, ((dp ^ j) * 256, 0), (256, 1024))

        down_far = along_z(down_part(1), lambda z: z ^ 1)
        pair = jnp.concatenate([up_part(1), up_part(3)], axis=0)

    with jax.named_scope("back"):
        found = [
            rows_of(note_row, 4 * SLOT, k * SLOT)
            for k, note_row in enumerate(
                [above[tok : tok + 1], below[tok : tok + 1], across_x[tok : tok + 1], note]
            )
        ]
        all_hits = placing(jnp.concatenate([f[0] for f in found], axis=1), plane * 4 * SLOT)
        all_place = after(merged(all_hits), back)
        sums = dot(all_place, returned.reshape(-1, model), ((0,), (0,)))
        far_sums = sums[: 3 * tok].astype(BF)
        gate_pack = gate_wide[:, 0].reshape(plane, 4 * SLOT).astype(BF)
        far_sums = [far_sums[k * tok : (k + 1) * tok] for k in range(3)]
        *far_sums, gate_pack, pair = lax.optimization_barrier(
            (*far_sums, gate_pack, pair, down_far)
        )[:5]
        from_below = along_z(far_sums[0], lambda z: z + 2)
        from_above = along_z(far_sums[1], lambda z: z - 2)
        from_across = along_z(far_sums[2], lambda z: z + 4)
        ret_gate = plane_exchange(gate_pack)
        total = cotan.astype(F32) + after(sums[3 * tok :], ret_gate)
        total = total + from_below.astype(F32) + from_above.astype(F32) + from_across.astype(F32)
        input_grad = total.astype(BF)


    with jax.named_scope("weight_grads"):
        pair_far = along_z(after(pair, input_grad), lambda z: z ^ 1)
        pair_sum = (up_part(2).astype(F32) + pair_far[256:].astype(F32)).astype(BF)
        up_cross = along_z(pair_sum, lambda z: z ^ 2)
        same = up_part(0).astype(F32) + pair_far[:256].astype(F32)
        opposite = up_cross.astype(F32)
        first = jnp.where(half == 0, same, opposite).astype(BF)
        second = jnp.where(half == 0, opposite, same).astype(BF)
        up_grad = jnp.concatenate([first, second], axis=1)
        down_own = down_part(0).astype(F32)

    with jax.named_scope("attn_bwd"):
        weight_term = dot(attn_out, input_grad, ((0,), (0,))).astype(BF)
        do = dot_nt(after(input_grad, weight_term), out_weight).astype(BF)

    with jax.named_scope("out_weight"):
        rows = WIDTH // plane
        parts = plane_exchange(weight_term.reshape(plane, rows, model))
        part = jnp.sum(parts.astype(F32), axis=0)
        part_b = part.astype(BF)
        part_first = part_b
        do = after(do, part_first)
        query_grad, terms = attn_backward(steps, queries[0], attn_out, lse, do, kv)
        key_value_terms = halo_terms(terms)
        for k in (1, 2, 3):
            part = part + along_z(part_b, lambda z, k=k: z ^ k).astype(F32)
        part_b = part.astype(BF)
        part = part_b.astype(F32) + along_z(part_b, lambda z: z + 4).astype(F32)
        part = after(part, pair_far)
        whole = jnp.broadcast_to(part.astype(BF)[None], (plane, rows, model))
        out_weight_grad = plane_exchange(whole).reshape(WIDTH, model)
        own_terms, from_far, chip_terms = lax.optimization_barrier((*key_value_terms, whole))[:3]
        from_right = seq_permute(chip_terms[:tok], lambda i: i - 2)
        from_left = seq_permute(chip_terms[tok:], lambda i: i + 2)
        key_value_grad = own_terms + from_far.astype(F32)
        key_value_grad = key_value_grad + from_right.astype(F32) + from_left.astype(F32)
        key_value_grad = key_value_grad.astype(BF)

    with jax.named_scope("gate_back"):
        ret_gate = after(ret_gate, part_first).astype(F32).reshape(-1, 1)
        gate_sums = jnp.stack([jnp.sum(jnp.where(h, ret_gate, 0.0), axis=0) for h in all_hits])
        gate_far = after(gate_sums.astype(BF), from_far)
        gate_sum = gate_sums[:, 3 * tok :]
        gate_moves = [lambda z: z + 2, lambda z: z - 2, lambda z: z + 4]
        for k, move in enumerate(gate_moves):
            part = along_z(gate_far[:, k * tok : (k + 1) * tok], move)
            gate_sum = gate_sum + part.astype(F32)
        down_grad = (after(down_own, part_first) + down_far.astype(F32)).astype(BF)
        gate_grad = gate_sum.T / gates[0].astype(F32)

    return (
        input_grad[None],
        query_grad[None],
        key_value_grad[None, :, :WIDTH],
        key_value_grad[None, :, WIDTH:],
        out_weight_grad,
        up_grad[None],
        down_grad[None],
        gate_grad[None],
    )


def solution(mesh):
    rows = P("dp", "seq", None)
    weights = P("seq", "dp", None)
    return jax.shard_map(
        per_device,
        mesh=mesh,
        in_specs=(rows, rows, rows, P(), rows, rows, rows, weights, weights, rows),
        out_specs=(rows, rows, rows, rows, P(), weights, weights, rows),
        check_vma=False,
    )
```

```python
import functools

import jax
import jax.numpy as jnp
from jax import lax
from jax.experimental import pallas as pl
from jax.experimental.pallas import tpu as pltpu
from jax.sharding import PartitionSpec as P

HEADS = 8
HEAD = 64
SLOT = 8
TOK = 128
WIDTH = HEADS * HEAD
MODEL = 1024
SCALE = HEAD ** (-0.5)
LOW = -1e30
BOTH = ("seq", "dp")
BF = jnp.bfloat16
F32 = jnp.float32


def seq_of(x, zh, y, c):
    return ((x % 4 * 2 + zh) * 4 + y % 4) * 2 + c


PLANES = [[seq_of(x, zh, y, c) for x in range(4) for y in range(4) for c in range(2)] for zh in range(2)]


def along_z(array, move):
    pairs = []
    for x in range(4):
        for y in range(4):
            for c in range(2):
                for z in range(8):
                    to = move(z) % 8
                    pairs.append(
                        (seq_of(x, z // 4, y, c) * 4 + z % 4, seq_of(x, to // 4, y, c) * 4 + to % 4)
                    )
    return lax.ppermute(array, BOTH, pairs)


def seq_permute(array, move):
    size = lax.axis_size("seq")
    pairs = [(i, move(i)) for i in range(size) if 0 <= move(i) < size]
    return lax.ppermute(array, "seq", pairs)


def plane_exchange(array):
    return lax.all_to_all(
        array, "seq", split_axis=0, concat_axis=0, tiled=True, axis_index_groups=PLANES
    )


def after(value, *others):
    return lax.optimization_barrier((value, *others))[0]


def halo_across(array):
    far = seq_permute(array, lambda i: i + 3 if i % 2 else i - 3)
    left = seq_permute(array, lambda i: i + 2)
    right = seq_permute(array, lambda i: i - 2)
    return [far, left, right]


def halo(array, far, left, right):
    other = seq_permute(jnp.concatenate([array, left, right], axis=0), lambda i: i ^ 1)
    rows = array.shape[0]
    return [array, far, left, right] + [other[k * rows : (k + 1) * rows] for k in range(3)]


def halo_terms(terms):
    rows = terms.shape[0] // 7
    other = seq_permute(terms[4 * rows :], lambda i: i ^ 1).astype(F32)
    from_far = seq_permute(terms[rows : 2 * rows], lambda i: i - 3 if i % 2 == 0 else i + 3)
    chip = terms[2 * rows : 4 * rows].astype(F32) + other[rows:]
    return terms[:rows].astype(F32) + other[:rows], from_far, chip.astype(BF)


def halo_steps(seq):
    core = seq % 2
    steps = jnp.stack(
        [
            jnp.int32(0),
            6 * core - 3,
            jnp.int32(-2),
            jnp.int32(2),
            1 - 2 * core,
            -1 - 2 * core,
            3 - 2 * core,
        ]
    ).astype(jnp.int32)
    there = seq + steps
    real = ((there >= 0) & (there < lax.axis_size("seq"))).astype(jnp.int32)
    return jnp.stack([steps, real])


def dot(left, right, dims=((1,), (0,))):
    return lax.dot_general(left, right, (dims, ((), ())), preferred_element_type=F32)


def dot_nt(left, right):
    return dot(left, right, ((1,), (1,)))


def head_lanes(half):
    lane = lax.broadcasted_iota(jnp.int32, (TOK, 2 * HEAD), 1)
    return (lane < HEAD) if half == 0 else (lane >= HEAD)


def within(steps_ref, b, far_axis):
    own = lax.broadcasted_iota(jnp.int32, (TOK, TOK), 1 - far_axis)
    other = lax.broadcasted_iota(jnp.int32, (TOK, TOK), far_axis)
    gap = other + steps_ref[0, b] * TOK - own
    return (jnp.abs(gap) <= 3 * TOK) & (steps_ref[1, b] == 1)


def fwd_kernel(steps_ref, q_ref, *refs):
    kv = refs[:7]
    out_ref, lse_ref = refs[7:9]
    lane = lax.broadcasted_iota(jnp.int32, (TOK, TOK), 1)
    lse_all = jnp.zeros((TOK, TOK), F32)
    masks = [within(steps_ref, b, 1) for b in range(7)]
    for pair in range(HEADS // 2):
        cols = slice(pair * 128, pair * 128 + 128)
        vcols = slice(WIDTH + pair * 128, WIDTH + pair * 128 + 128)
        q_pair = q_ref[:, cols]
        outs = []
        for half in range(2):
            q_head = jnp.where(head_lanes(half), q_pair, jnp.zeros((), BF))
            scores = [
                jnp.where(masks[b], dot_nt(q_head, kv[b][:, cols]) * SCALE, LOW) for b in range(7)
            ]
            top = functools.reduce(jnp.maximum, scores)
            top = jnp.max(top, axis=1, keepdims=True)
            exps = [jnp.exp(s - top) for s in scores]
            total = jnp.sum(functools.reduce(jnp.add, exps), axis=1, keepdims=True)
            inv = 1.0 / total
            acc = jnp.zeros((TOK, 128), F32)
            for b in range(7):
                acc = acc + dot((exps[b] * inv).astype(BF), kv[b][:, vcols])
            outs.append(acc)
            lse_all = jnp.where(lane == 2 * pair + half, top + jnp.log(total), lse_all)
        out_ref[:, cols] = jnp.where(head_lanes(0), outs[0], outs[1]).astype(BF)
    lse_ref[...] = jnp.transpose(lse_all)[0:16]


def bwd_kernel(steps_ref, q_ref, out_ref, lse_ref, do_ref, *refs):
    kv = refs[:7]
    dq_ref, dkv_ref, delta_scr = refs[7:10]
    masks = [within(steps_ref, b, 0) for b in range(7)]
    row = lax.broadcasted_iota(jnp.int32, (16, WIDTH), 0)
    col = lax.broadcasted_iota(jnp.int32, (16, WIDTH), 1)
    pick = ((col >= row * HEAD) & (col < row * HEAD + HEAD)).astype(BF)
    prod = do_ref[...].astype(F32) * out_ref[...].astype(F32)
    high = prod.astype(BF)
    prod = prod - high.astype(F32)
    mid = prod.astype(BF)
    low = (prod - mid.astype(F32)).astype(BF)
    delta_scr[...] = dot_nt(pick, high) + dot_nt(pick, mid) + dot_nt(pick, low)
    for pair in range(HEADS // 2):
        cols = slice(pair * 128, pair * 128 + 128)
        vcols = slice(WIDTH + pair * 128, WIDTH + pair * 128 + 128)
        q_pair = q_ref[:, cols]
        do_pair = do_ref[:, cols]
        q_heads = [jnp.where(head_lanes(h), q_pair, jnp.zeros((), BF)) for h in range(2)]
        do_heads = [jnp.where(head_lanes(h), do_pair, jnp.zeros((), BF)) for h in range(2)]
        dqs = [jnp.zeros((TOK, 128), F32) for _ in range(2)]
        for b in range(7):
            k_pair = kv[b][:, cols]
            v_pair = kv[b][:, vcols]
            dk = jnp.zeros((TOK, 128), F32)
            dv = jnp.zeros((TOK, 128), F32)
            for half in range(2):
                head = 2 * pair + half
                score = dot_nt(k_pair, q_heads[half]) * SCALE - lse_ref[head : head + 1, :]
                prob = jnp.exp(jnp.where(masks[b], score, LOW))
                dprob = dot_nt(v_pair, do_heads[half])
                dscore = (prob * (dprob - delta_scr[head : head + 1, :]) * SCALE).astype(BF)
                dqs[half] = dqs[half] + dot(dscore, k_pair, ((0,), (0,)))
                dk = dk + dot(dscore, q_heads[half])
                dv = dv + dot(prob.astype(BF), do_heads[half])
            rows = slice(b * TOK, b * TOK + TOK)
            dkv_ref[rows, cols] = dk.astype(BF)
            dkv_ref[rows, vcols] = dv.astype(BF)
        dq_ref[:, cols] = jnp.where(head_lanes(0), dqs[0], dqs[1]).astype(BF)


def on_chip(body, outs, n_in, scratch=(), moved=10**5):
    return pl.pallas_call(
        body,
        out_shape=outs,
        in_specs=[pl.BlockSpec(memory_space=pltpu.SMEM)]
        + [pl.BlockSpec(memory_space=pltpu.VMEM)] * (n_in - 1),
        out_specs=[pl.BlockSpec(memory_space=pltpu.VMEM)] * len(outs),
        scratch_shapes=list(scratch),
        compiler_params=pltpu.CompilerParams(vmem_limit_bytes=24 * 1024 * 1024),
        cost_estimate=pl.CostEstimate(flops=10**6, bytes_accessed=moved, transcendentals=10**3),
    )


def attn_forward(steps, q, kv):
    outs = [
        jax.ShapeDtypeStruct((TOK, WIDTH), BF),
        jax.ShapeDtypeStruct((16, TOK), F32),
    ]
    return on_chip(fwd_kernel, outs, 9)(steps, q, *kv)


def attn_backward(steps, q, out, lse, do, kv):
    outs = [
        jax.ShapeDtypeStruct((TOK, WIDTH), BF),
        jax.ShapeDtypeStruct((7 * TOK, 2 * WIDTH), BF),
    ]
    scratch = [pltpu.VMEM((16, TOK), F32)]
    return on_chip(bwd_kernel, outs, 12, scratch)(steps, q, out, lse, do, *kv)


def experts_kernel(
    dp_ref, near_ref, across_ref, own_ref, mine_ref, pack_ref, u2_ref, u3_ref,
    down_ref, back_ref, x_ref, g_ref, act_ref, pg_ref, gate_ref, up_scr, down_scr,
):
    dp = dp_ref[0]

    def place(scr, block, rows, value):
        scr[pl.ds(pl.multiple_of(block * rows, rows), rows), :] = value

    place(up_scr, dp, 256, mine_ref[...])
    place(up_scr, dp ^ 1, 256, pack_ref[0:256])
    place(up_scr, dp ^ 2, 256, u2_ref[...])
    place(up_scr, dp ^ 3, 256, u3_ref[...])
    place(down_scr, dp & 1, 512, down_ref[...])
    place(down_scr, (dp & 1) ^ 1, 512, pack_ref[256:768])

    def tile(i, carry):
        base = pl.multiple_of(i * 256, 256)
        for p in range(8):
            here = pl.ds(base + p * 32, 16)
            there = pl.ds(base + p * 32 + 16, 16)
            near = near_ref[i * 8 + p]
            x_ref[here, :] = near[0:16]
            g_ref[here, :] = near[16:32]
            across = across_ref[i * 8 + p].astype(F32)
            own = own_ref[i * 8 + p].astype(F32)
            x_ref[there, :] = jnp.concatenate([across[0:8], own[0:8]], axis=0).astype(BF)
            g_ref[there, :] = jnp.concatenate([across[8:16], own[8:16]], axis=0).astype(BF)
        rows = pl.ds(base, 256)
        pre = dot(x_ref[rows, :], up_scr[...])
        act_grad = dot_nt(g_ref[rows, :], down_scr[...])
        sig = 1.0 / (1.0 + jnp.exp(-pre))
        act = (pre * sig).astype(BF)
        act_ref[rows, :] = act
        gate = jnp.sum(act.astype(F32) * act_grad, axis=1, keepdims=True)
        gate_ref[rows, :] = jnp.broadcast_to(gate, (256, 128))
        pg_ref[rows, :] = (act_grad * (sig * (1.0 + pre * (1.0 - sig)))).astype(BF)
        back_ref[rows, :] = dot_nt(pg_ref[rows, :], up_scr[...]).astype(BF)
        return carry

    lax.fori_loop(0, 4, tile, 0)


def experts(dp, near, across, own, mine, pack, up_two, up_three, down):
    big = jax.ShapeDtypeStruct((1024, MODEL), BF)
    ins = [near, across, own, mine, pack, up_two, up_three, down]
    return pl.pallas_call(
        experts_kernel,
        out_shape=[big] * 5 + [jax.ShapeDtypeStruct((1024, 128), F32)],
        in_specs=[pl.BlockSpec(memory_space=pltpu.SMEM)]
        + [pl.BlockSpec(memory_space=pltpu.VMEM)] * len(ins),
        out_specs=[pl.BlockSpec(memory_space=pltpu.VMEM)] * 6,
        scratch_shapes=[pltpu.VMEM((1024, MODEL), BF)] * 2,
        compiler_params=pltpu.CompilerParams(vmem_limit_bytes=40 * 1024 * 1024),
        cost_estimate=pl.CostEstimate(
            flops=6 * 10**9, bytes_accessed=20 * 10**6, transcendentals=10**6
        ),
    )(dp.reshape(1), *ins)


def per_device(
    queries, keys, values, out_weight, ffn_input, routes, gates, up_weight, down_weight, out_grad
):
    seq = lax.axis_index("seq")
    dp = lax.axis_index("dp")
    z_hi = (seq // 8) % 2
    tok, model = ffn_input.shape[1:]
    n_seq = lax.axis_size("seq")
    plane = n_seq // 2
    frames = ffn_input[0]
    cotan = out_grad[0]

    with jax.named_scope("attn_kv"):
        kv_own = jnp.concatenate([keys[0], values[0]], axis=1)

    with jax.named_scope("meta"):
        chosen = routes[0].T.reshape(1, 2 * tok)
        named = chosen == jnp.arange(n_seq, dtype=jnp.int32)[:, None]
        order = jnp.arange(2 * tok)
        before = (order[:, None] < order[None, :]).astype(BF)
        counts = dot(named.astype(BF), before)
        rank = jnp.sum(jnp.where(named, counts, 0.0), axis=0, keepdims=True)
        note = jnp.concatenate(
            [
                chosen.astype(BF),
                rank.astype(BF),
                gates[0].T.reshape(1, 2 * tok),
                jnp.zeros((1, 2 * tok), BF),
            ],
            axis=1,
        )
        payload = jnp.concatenate([frames, note, jnp.zeros((15, model), BF), cotan], axis=0)
    n_x = tok + 16
    with jax.named_scope("tokens_z"):
        above = along_z(payload, lambda z: z - 2)
        below = along_z(payload, lambda z: z + 2)
        across_x = along_z(above[:n_x], lambda z: z - 2)
        across_g = along_z(below[n_x:], lambda z: z + 2)

    with jax.named_scope("weights_z"):
        half = dp // 2
        up_mine = lax.dynamic_slice(up_weight[0], (0, half * 1024), (256, 1024))
        up_other = lax.dynamic_slice(up_weight[0], (0, (1 - half) * 1024), (256, 1024))
        pack = jnp.concatenate([up_mine, down_weight[0]], axis=0)
        pack, up_other, _, _ = lax.optimization_barrier((pack, up_other, across_x, across_g))
        pack1 = along_z(pack, lambda z: z ^ 1)
        up_two = along_z(up_other, lambda z: z ^ 2)
        up_three = along_z(up_two, lambda z: z ^ 1)

    def rows_of(note_row, stride, offset):
        expert = note_row[0, : 2 * tok].astype(jnp.int32)
        place = (expert // 16) * 8 + expert % 8
        here = (expert // 8) % 2 == z_hi
        row = place * stride + offset + note_row[0, 2 * tok : 4 * tok].astype(jnp.int32)
        row = jnp.where(here, row, -1).reshape(2, tok)
        return row, note_row[0, 4 * tok : 6 * tok].reshape(2, tok)

    def placing(row, total):
        spots = jnp.arange(total, dtype=jnp.int32)[:, None]
        return [spots == row[t][None, :] for t in range(2)]

    def merged(hits, gate=None):
        if gate is None:
            return (hits[0] | hits[1]).astype(BF)
        zero = jnp.zeros((), BF)
        return jnp.where(hits[0], gate[0][None, :], jnp.where(hits[1], gate[1][None, :], zero))

    class Sets:
        def __init__(self, notes, xs, gs):
            n = len(notes)
            self.n = n
            found = [rows_of(note_row, n * SLOT, k * SLOT) for k, note_row in enumerate(notes)]
            self.hits = placing(jnp.concatenate([f[0] for f in found], axis=1), plane * n * SLOT)
            self.gate = jnp.concatenate([f[1] for f in found], axis=1)
            self.x = xs[0] if n == 1 else jnp.concatenate(xs, axis=0)
            self.g = gs[0] if n == 1 else jnp.concatenate(gs, axis=0)

        def packed(self):
            shape = (plane, self.n * SLOT, model)
            send_x = dot(merged(self.hits), self.x).astype(BF).reshape(shape)
            send_g = dot(merged(self.hits, self.gate), self.g).astype(BF).reshape(shape)
            return jnp.concatenate([send_x, send_g], axis=1)

    with jax.named_scope("out_own"):
        own = Sets([note], [frames], [cotan])
        got_own = plane_exchange(own.packed())
    with jax.named_scope("out_near"):
        near = Sets(
            [above[tok : tok + 1], below[tok : tok + 1]],
            [above[:tok], below[:tok]],
            [above[n_x:], below[n_x:]],
        )
        got_near = plane_exchange(after(near.packed(), got_own, pack, up_other))
    with jax.named_scope("attn_fwd"):
        steps = halo_steps(seq)
        kv_near = halo_across(after(kv_own, up_two))
        kv = halo(kv_own, *kv_near)
        attn_out, lse = attn_forward(steps, queries[0], kv)
    with jax.named_scope("out_across"):
        across = Sets([across_x[tok : tok + 1]], [across_x[:tok]], [across_g])
        got_across = plane_exchange(after(across.packed(), got_near))

    with jax.named_scope("experts"):
        pack1, up_three, _ = lax.optimization_barrier((pack1, up_three, got_across))
        back, x_rows, g_rows, act, pre_grad, gate_wide = experts(
            dp, got_near, got_across, got_own, up_mine, pack1, up_two, up_three,
            down_weight[0],
        )

        back = after(back, *kv_near)

    with jax.named_scope("back"):
        returned = plane_exchange(back.reshape(plane, 4 * SLOT, model))

    with jax.named_scope("weight_grads"):
        down_term = dot(act, g_rows, ((0,), (0,))).astype(BF)
        up_term = dot(x_rows, pre_grad, ((0,), (0,))).astype(BF)

        def down_part(j):
            return lax.dynamic_slice(down_term, (((dp ^ j) % 2) * 512, 0), (512, model))

        def up_part(j):
            return lax.dynamic_slice(up_term, ((dp ^ j) * 256, 0), (256, 1024))

        down_far = along_z(down_part(1), lambda z: z ^ 1)
        pair = jnp.concatenate([up_part(1), up_part(3)], axis=0)

    with jax.named_scope("back"):
        found = [
            rows_of(note_row, 4 * SLOT, k * SLOT)
            for k, note_row in enumerate(
                [above[tok : tok + 1], below[tok : tok + 1], across_x[tok : tok + 1], note]
            )
        ]
        all_hits = placing(jnp.concatenate([f[0] for f in found], axis=1), plane * 4 * SLOT)
        all_place = after(merged(all_hits), back)
        sums = dot(all_place, returned.reshape(-1, model), ((0,), (0,)))
        far_sums = sums[: 3 * tok].astype(BF)
        gate_pack = gate_wide[:, 0].reshape(plane, 4 * SLOT).astype(BF)
        far_sums = [far_sums[k * tok : (k + 1) * tok] for k in range(3)]
        *far_sums, gate_pack, pair = lax.optimization_barrier(
            (*far_sums, gate_pack, pair, down_far)
        )[:5]
        from_below = along_z(far_sums[0], lambda z: z + 2)
        from_above = along_z(far_sums[1], lambda z: z - 2)
        from_across = along_z(far_sums[2], lambda z: z + 4)
        ret_gate = plane_exchange(gate_pack)
        total = cotan.astype(F32) + after(sums[3 * tok :], ret_gate)
        total = total + from_below.astype(F32) + from_above.astype(F32) + from_across.astype(F32)
        input_grad = total.astype(BF)


    with jax.named_scope("weight_grads"):
        pair_far = along_z(after(pair, input_grad), lambda z: z ^ 1)
        pair_sum = (up_part(2).astype(F32) + pair_far[256:].astype(F32)).astype(BF)

    with jax.named_scope("attn_bwd"):
        weight_term = dot(attn_out, input_grad, ((0,), (0,))).astype(BF)
        do = dot_nt(after(input_grad, weight_term), out_weight).astype(BF)
        query_grad, terms = attn_backward(steps, queries[0], attn_out, lse, do, kv)

    with jax.named_scope("out_weight"):
        rows = WIDTH // plane
        parts = plane_exchange(weight_term.reshape(plane, rows, model))
        parts, terms = lax.optimization_barrier((parts, terms))
        part = jnp.sum(parts.astype(F32), axis=0)
        part_b = part.astype(BF)
        part_first = part_b
        key_value_terms = halo_terms(terms)
        for k in (1, 2, 3):
            part = part + along_z(part_b, lambda z, k=k: z ^ k).astype(F32)
        part_b = part.astype(BF)
        part = part_b.astype(F32) + along_z(part_b, lambda z: z + 4).astype(F32)
        part = after(part, pair_far)
        whole = jnp.broadcast_to(part.astype(BF)[None], (plane, rows, model))
        out_weight_grad = plane_exchange(whole).reshape(WIDTH, model)
        own_terms, from_far, chip_terms = lax.optimization_barrier((*key_value_terms, whole))[:3]
        from_right = seq_permute(chip_terms[:tok], lambda i: i - 2)
        from_left = seq_permute(chip_terms[tok:], lambda i: i + 2)
        key_value_grad = own_terms + from_far.astype(F32)
        key_value_grad = key_value_grad + from_right.astype(F32) + from_left.astype(F32)
        key_value_grad = key_value_grad.astype(BF)

    with jax.named_scope("last"):
        up_cross = along_z(after(pair_sum, whole), lambda z: z ^ 2)
        same = up_part(0).astype(F32) + pair_far[:256].astype(F32)
        opposite = up_cross.astype(F32)
        first = jnp.where(half == 0, same, opposite).astype(BF)
        second = jnp.where(half == 0, opposite, same).astype(BF)
        up_grad = jnp.concatenate([first, second], axis=1)
        down_own = down_part(0).astype(F32)
        ret_gate = after(ret_gate, part_first).astype(F32).reshape(-1, 1)
        gate_sums = jnp.stack([jnp.sum(jnp.where(h, ret_gate, 0.0), axis=0) for h in all_hits])
        gate_far = after(gate_sums.astype(BF), from_far)
        gate_moves = [lambda z: z + 2, lambda z: z - 2, lambda z: z + 4]
        gate_parts = [
            along_z(gate_far[:, k * tok : (k + 1) * tok], move) for k, move in enumerate(gate_moves)
        ]
        gate_sum = gate_sums[:, 3 * tok :]
        for gate_part in gate_parts:
            gate_sum = gate_sum + gate_part.astype(F32)
        down_grad = (after(down_own, part_first) + down_far.astype(F32)).astype(BF)
        gate_grad = gate_sum.T / gates[0].astype(F32)

    return (
        input_grad[None],
        query_grad[None],
        key_value_grad[None, :, :WIDTH],
        key_value_grad[None, :, WIDTH:],
        out_weight_grad,
        up_grad[None],
        down_grad[None],
        gate_grad[None],
    )


def solution(mesh):
    rows = P("dp", "seq", None)
    weights = P("seq", "dp", None)
    return jax.shard_map(
        per_device,
        mesh=mesh,
        in_specs=(rows, rows, rows, P(), rows, rows, rows, weights, weights, rows),
        out_specs=(rows, rows, rows, rows, P(), weights, weights, rows),
        check_vma=False,
    )
```

```python
import functools

import jax
import jax.numpy as jnp
from jax import lax
from jax.experimental import pallas as pl
from jax.experimental.pallas import tpu as pltpu
from jax.sharding import PartitionSpec as P

HEADS = 8
HEAD = 64
SLOT = 8
TOK = 128
WIDTH = HEADS * HEAD
MODEL = 1024
SCALE = HEAD ** (-0.5)
LOW = -1e30
BOTH = ("seq", "dp")
BF = jnp.bfloat16
F32 = jnp.float32


def seq_of(x, zh, y, c):
    return ((x % 4 * 2 + zh) * 4 + y % 4) * 2 + c


PLANES = [[seq_of(x, zh, y, c) for x in range(4) for y in range(4) for c in range(2)] for zh in range(2)]


def along_z(array, move):
    pairs = []
    for x in range(4):
        for y in range(4):
            for c in range(2):
                for z in range(8):
                    to = move(z) % 8
                    pairs.append(
                        (seq_of(x, z // 4, y, c) * 4 + z % 4, seq_of(x, to // 4, y, c) * 4 + to % 4)
                    )
    return lax.ppermute(array, BOTH, pairs)


def seq_permute(array, move):
    size = lax.axis_size("seq")
    pairs = [(i, move(i)) for i in range(size) if 0 <= move(i) < size]
    return lax.ppermute(array, "seq", pairs)


def plane_exchange(array):
    return lax.all_to_all(
        array, "seq", split_axis=0, concat_axis=0, tiled=True, axis_index_groups=PLANES
    )


def after(value, *others):
    return lax.optimization_barrier((value, *others))[0]


def halo_across(array):
    left = seq_permute(array, lambda i: i + 2)
    right = seq_permute(array, lambda i: i - 2)
    return [left, right]


def halo(array, far, left, right):
    other = seq_permute(jnp.concatenate([array, left, right], axis=0), lambda i: i ^ 1)
    rows = array.shape[0]
    return [array, far, left, right] + [other[k * rows : (k + 1) * rows] for k in range(3)]


def halo_terms(terms):
    rows = terms.shape[0] // 7
    other = seq_permute(terms[4 * rows :], lambda i: i ^ 1).astype(F32)
    from_far = seq_permute(terms[rows : 2 * rows], lambda i: i - 3 if i % 2 == 0 else i + 3)
    chip = terms[2 * rows : 4 * rows].astype(F32) + other[rows:]
    return terms[:rows].astype(F32) + other[:rows], from_far, chip.astype(BF)


def halo_steps(seq):
    core = seq % 2
    steps = jnp.stack(
        [
            jnp.int32(0),
            6 * core - 3,
            jnp.int32(-2),
            jnp.int32(2),
            1 - 2 * core,
            -1 - 2 * core,
            3 - 2 * core,
        ]
    ).astype(jnp.int32)
    there = seq + steps
    real = ((there >= 0) & (there < lax.axis_size("seq"))).astype(jnp.int32)
    return jnp.stack([steps, real])


def dot(left, right, dims=((1,), (0,))):
    return lax.dot_general(left, right, (dims, ((), ())), preferred_element_type=F32)


def dot_nt(left, right):
    return dot(left, right, ((1,), (1,)))


def head_lanes(half):
    lane = lax.broadcasted_iota(jnp.int32, (TOK, 2 * HEAD), 1)
    return (lane < HEAD) if half == 0 else (lane >= HEAD)


def within(steps_ref, b, far_axis):
    own = lax.broadcasted_iota(jnp.int32, (TOK, TOK), 1 - far_axis)
    other = lax.broadcasted_iota(jnp.int32, (TOK, TOK), far_axis)
    gap = other + steps_ref[0, b] * TOK - own
    return (jnp.abs(gap) <= 3 * TOK) & (steps_ref[1, b] == 1)


def fwd_kernel(steps_ref, q_ref, *refs):
    kv = refs[:7]
    out_ref, lse_ref = refs[7:9]
    lane = lax.broadcasted_iota(jnp.int32, (TOK, TOK), 1)
    lse_all = jnp.zeros((TOK, TOK), F32)
    masks = [within(steps_ref, b, 1) for b in range(7)]
    for pair in range(HEADS // 2):
        cols = slice(pair * 128, pair * 128 + 128)
        vcols = slice(WIDTH + pair * 128, WIDTH + pair * 128 + 128)
        q_pair = q_ref[:, cols]
        outs = []
        for half in range(2):
            q_head = jnp.where(head_lanes(half), q_pair, jnp.zeros((), BF))
            scores = [
                jnp.where(masks[b], dot_nt(q_head, kv[b][:, cols]) * SCALE, LOW) for b in range(7)
            ]
            top = functools.reduce(jnp.maximum, scores)
            top = jnp.max(top, axis=1, keepdims=True)
            exps = [jnp.exp(s - top) for s in scores]
            total = jnp.sum(functools.reduce(jnp.add, exps), axis=1, keepdims=True)
            inv = 1.0 / total
            acc = jnp.zeros((TOK, 128), F32)
            for b in range(7):
                acc = acc + dot((exps[b] * inv).astype(BF), kv[b][:, vcols])
            outs.append(acc)
            lse_all = jnp.where(lane == 2 * pair + half, top + jnp.log(total), lse_all)
        out_ref[:, cols] = jnp.where(head_lanes(0), outs[0], outs[1]).astype(BF)
    lse_ref[...] = jnp.transpose(lse_all)[0:16]


def bwd_kernel(steps_ref, q_ref, out_ref, lse_ref, do_ref, *refs):
    kv = refs[:7]
    dq_ref, dkv_ref, delta_scr = refs[7:10]
    masks = [within(steps_ref, b, 0) for b in range(7)]
    row = lax.broadcasted_iota(jnp.int32, (16, WIDTH), 0)
    col = lax.broadcasted_iota(jnp.int32, (16, WIDTH), 1)
    pick = ((col >= row * HEAD) & (col < row * HEAD + HEAD)).astype(BF)
    prod = do_ref[...].astype(F32) * out_ref[...].astype(F32)
    high = prod.astype(BF)
    prod = prod - high.astype(F32)
    mid = prod.astype(BF)
    low = (prod - mid.astype(F32)).astype(BF)
    delta_scr[...] = dot_nt(pick, high) + dot_nt(pick, mid) + dot_nt(pick, low)
    for pair in range(HEADS // 2):
        cols = slice(pair * 128, pair * 128 + 128)
        vcols = slice(WIDTH + pair * 128, WIDTH + pair * 128 + 128)
        q_pair = q_ref[:, cols]
        do_pair = do_ref[:, cols]
        q_heads = [jnp.where(head_lanes(h), q_pair, jnp.zeros((), BF)) for h in range(2)]
        do_heads = [jnp.where(head_lanes(h), do_pair, jnp.zeros((), BF)) for h in range(2)]
        dqs = [jnp.zeros((TOK, 128), F32) for _ in range(2)]
        for b in range(7):
            k_pair = kv[b][:, cols]
            v_pair = kv[b][:, vcols]
            dk = jnp.zeros((TOK, 128), F32)
            dv = jnp.zeros((TOK, 128), F32)
            for half in range(2):
                head = 2 * pair + half
                score = dot_nt(k_pair, q_heads[half]) * SCALE - lse_ref[head : head + 1, :]
                prob = jnp.exp(jnp.where(masks[b], score, LOW))
                dprob = dot_nt(v_pair, do_heads[half])
                dscore = (prob * (dprob - delta_scr[head : head + 1, :]) * SCALE).astype(BF)
                dqs[half] = dqs[half] + dot(dscore, k_pair, ((0,), (0,)))
                dk = dk + dot(dscore, q_heads[half])
                dv = dv + dot(prob.astype(BF), do_heads[half])
            rows = slice(b * TOK, b * TOK + TOK)
            dkv_ref[rows, cols] = dk.astype(BF)
            dkv_ref[rows, vcols] = dv.astype(BF)
        dq_ref[:, cols] = jnp.where(head_lanes(0), dqs[0], dqs[1]).astype(BF)


def on_chip(body, outs, n_in, scratch=(), moved=10**5):
    return pl.pallas_call(
        body,
        out_shape=outs,
        in_specs=[pl.BlockSpec(memory_space=pltpu.SMEM)]
        + [pl.BlockSpec(memory_space=pltpu.VMEM)] * (n_in - 1),
        out_specs=[pl.BlockSpec(memory_space=pltpu.VMEM)] * len(outs),
        scratch_shapes=list(scratch),
        compiler_params=pltpu.CompilerParams(vmem_limit_bytes=24 * 1024 * 1024),
        cost_estimate=pl.CostEstimate(flops=10**6, bytes_accessed=moved, transcendentals=10**3),
    )


def attn_forward(steps, q, kv):
    outs = [
        jax.ShapeDtypeStruct((TOK, WIDTH), BF),
        jax.ShapeDtypeStruct((16, TOK), F32),
    ]
    return on_chip(fwd_kernel, outs, 9)(steps, q, *kv)


def attn_backward(steps, q, out, lse, do, kv):
    outs = [
        jax.ShapeDtypeStruct((TOK, WIDTH), BF),
        jax.ShapeDtypeStruct((7 * TOK, 2 * WIDTH), BF),
    ]
    scratch = [pltpu.VMEM((16, TOK), F32)]
    return on_chip(bwd_kernel, outs, 12, scratch)(steps, q, out, lse, do, *kv)


def experts_kernel(
    dp_ref, near_ref, across_ref, own_ref, mine_ref, pack_ref, u2_ref, u3_ref,
    down_ref, back_ref, x_ref, g_ref, act_ref, pg_ref, gate_ref, up_scr, down_scr,
):
    dp = dp_ref[0]

    def place(scr, block, rows, value):
        scr[pl.ds(pl.multiple_of(block * rows, rows), rows), :] = value

    place(up_scr, dp, 256, mine_ref[...])
    place(up_scr, dp ^ 1, 256, pack_ref[0:256])
    place(up_scr, dp ^ 2, 256, u2_ref[...])
    place(up_scr, dp ^ 3, 256, u3_ref[...])
    place(down_scr, dp & 1, 512, down_ref[...])
    place(down_scr, (dp & 1) ^ 1, 512, pack_ref[256:768])

    def tile(i, carry):
        base = pl.multiple_of(i * 256, 256)
        for p in range(8):
            here = pl.ds(base + p * 32, 16)
            there = pl.ds(base + p * 32 + 16, 16)
            near = near_ref[i * 8 + p]
            x_ref[here, :] = near[0:16]
            g_ref[here, :] = near[16:32]
            across = across_ref[i * 8 + p].astype(F32)
            own = own_ref[i * 8 + p].astype(F32)
            x_ref[there, :] = jnp.concatenate([across[0:8], own[0:8]], axis=0).astype(BF)
            g_ref[there, :] = jnp.concatenate([across[8:16], own[8:16]], axis=0).astype(BF)
        rows = pl.ds(base, 256)
        pre = dot(x_ref[rows, :], up_scr[...])
        act_grad = dot_nt(g_ref[rows, :], down_scr[...])
        sig = 1.0 / (1.0 + jnp.exp(-pre))
        act = (pre * sig).astype(BF)
        act_ref[rows, :] = act
        gate = jnp.sum(act.astype(F32) * act_grad, axis=1, keepdims=True)
        gate_ref[rows, :] = jnp.broadcast_to(gate, (256, 128))
        pg_ref[rows, :] = (act_grad * (sig * (1.0 + pre * (1.0 - sig)))).astype(BF)
        back_ref[rows, :] = dot_nt(pg_ref[rows, :], up_scr[...]).astype(BF)
        return carry

    lax.fori_loop(0, 4, tile, 0)


def experts(dp, near, across, own, mine, pack, up_two, up_three, down):
    big = jax.ShapeDtypeStruct((1024, MODEL), BF)
    ins = [near, across, own, mine, pack, up_two, up_three, down]
    return pl.pallas_call(
        experts_kernel,
        out_shape=[big] * 5 + [jax.ShapeDtypeStruct((1024, 128), F32)],
        in_specs=[pl.BlockSpec(memory_space=pltpu.SMEM)]
        + [pl.BlockSpec(memory_space=pltpu.VMEM)] * len(ins),
        out_specs=[pl.BlockSpec(memory_space=pltpu.VMEM)] * 6,
        scratch_shapes=[pltpu.VMEM((1024, MODEL), BF)] * 2,
        compiler_params=pltpu.CompilerParams(vmem_limit_bytes=40 * 1024 * 1024),
        cost_estimate=pl.CostEstimate(
            flops=6 * 10**9, bytes_accessed=20 * 10**6, transcendentals=10**6
        ),
    )(dp.reshape(1), *ins)


def per_device(
    queries, keys, values, out_weight, ffn_input, routes, gates, up_weight, down_weight, out_grad
):
    seq = lax.axis_index("seq")
    dp = lax.axis_index("dp")
    z_hi = (seq // 8) % 2
    tok, model = ffn_input.shape[1:]
    n_seq = lax.axis_size("seq")
    plane = n_seq // 2
    frames = ffn_input[0]
    cotan = out_grad[0]

    with jax.named_scope("attn_kv"):
        kv_own = jnp.concatenate([keys[0], values[0]], axis=1)

    with jax.named_scope("meta"):
        chosen = routes[0].T.reshape(1, 2 * tok)
        named = chosen == jnp.arange(n_seq, dtype=jnp.int32)[:, None]
        order = jnp.arange(2 * tok)
        before = (order[:, None] < order[None, :]).astype(BF)
        counts = dot(named.astype(BF), before)
        rank = jnp.sum(jnp.where(named, counts, 0.0), axis=0, keepdims=True)
        note = jnp.concatenate(
            [
                chosen.astype(BF),
                rank.astype(BF),
                gates[0].T.reshape(1, 2 * tok),
                jnp.zeros((1, 2 * tok), BF),
            ],
            axis=1,
        )
        payload = jnp.concatenate([frames, note, jnp.zeros((15, model), BF), cotan], axis=0)
    n_x = tok + 16
    with jax.named_scope("tokens_z"):
        above = along_z(payload, lambda z: z - 2)
        below = along_z(payload, lambda z: z + 2)
        across_x = along_z(above[:n_x], lambda z: z - 2)
        across_g = along_z(below[n_x:], lambda z: z + 2)

    with jax.named_scope("weights_z"):
        half = dp // 2
        up_mine = lax.dynamic_slice(up_weight[0], (0, half * 1024), (256, 1024))
        up_other = lax.dynamic_slice(up_weight[0], (0, (1 - half) * 1024), (256, 1024))
        pack = jnp.concatenate([up_mine, down_weight[0]], axis=0)
        pack, up_other, _, _ = lax.optimization_barrier((pack, up_other, across_x, across_g))
        pack1 = along_z(pack, lambda z: z ^ 1)
        up_two = along_z(up_other, lambda z: z ^ 2)
        up_three = along_z(up_two, lambda z: z ^ 1)

    def rows_of(note_row, stride, offset):
        expert = note_row[0, : 2 * tok].astype(jnp.int32)
        place = (expert // 16) * 8 + expert % 8
        here = (expert // 8) % 2 == z_hi
        row = place * stride + offset + note_row[0, 2 * tok : 4 * tok].astype(jnp.int32)
        row = jnp.where(here, row, -1).reshape(2, tok)
        return row, note_row[0, 4 * tok : 6 * tok].reshape(2, tok)

    def placing(row, total):
        spots = jnp.arange(total, dtype=jnp.int32)[:, None]
        return [spots == row[t][None, :] for t in range(2)]

    def merged(hits, gate=None):
        if gate is None:
            return (hits[0] | hits[1]).astype(BF)
        zero = jnp.zeros((), BF)
        return jnp.where(hits[0], gate[0][None, :], jnp.where(hits[1], gate[1][None, :], zero))

    class Sets:
        def __init__(self, notes, xs, gs):
            n = len(notes)
            self.n = n
            found = [rows_of(note_row, n * SLOT, k * SLOT) for k, note_row in enumerate(notes)]
            self.hits = placing(jnp.concatenate([f[0] for f in found], axis=1), plane * n * SLOT)
            self.gate = jnp.concatenate([f[1] for f in found], axis=1)
            self.x = xs[0] if n == 1 else jnp.concatenate(xs, axis=0)
            self.g = gs[0] if n == 1 else jnp.concatenate(gs, axis=0)

        def packed(self):
            shape = (plane, self.n * SLOT, model)
            send_x = dot(merged(self.hits), self.x).astype(BF).reshape(shape)
            send_g = dot(merged(self.hits, self.gate), self.g).astype(BF).reshape(shape)
            return jnp.concatenate([send_x, send_g], axis=1)

    with jax.named_scope("out_own"):
        own = Sets([note], [frames], [cotan])
        got_own = plane_exchange(own.packed())
    with jax.named_scope("out_near"):
        near = Sets(
            [above[tok : tok + 1], below[tok : tok + 1]],
            [above[:tok], below[:tok]],
            [above[n_x:], below[n_x:]],
        )
        got_near = plane_exchange(after(near.packed(), got_own, pack, up_other))
    with jax.named_scope("attn_fwd"):
        steps = halo_steps(seq)
        kv_near = halo_across(after(kv_own, up_two))
    with jax.named_scope("out_across"):
        across = Sets([across_x[tok : tok + 1]], [across_x[:tok]], [across_g])
        got_across = plane_exchange(after(across.packed(), got_near))

    with jax.named_scope("experts"):
        pack1, up_three, _ = lax.optimization_barrier((pack1, up_three, got_across))
        back, x_rows, g_rows, act, pre_grad, gate_wide = experts(
            dp, got_near, got_across, got_own, up_mine, pack1, up_two, up_three,
            down_weight[0],
        )

        back = after(back, *kv_near)

    with jax.named_scope("back"):
        returned = plane_exchange(back.reshape(plane, 4 * SLOT, model))

    with jax.named_scope("weight_grads"):
        down_term = dot(act, g_rows, ((0,), (0,))).astype(BF)
        up_term = dot(x_rows, pre_grad, ((0,), (0,))).astype(BF)

        def down_part(j):
            return lax.dynamic_slice(down_term, (((dp ^ j) % 2) * 512, 0), (512, model))

        def up_part(j):
            return lax.dynamic_slice(up_term, ((dp ^ j) * 256, 0), (256, 1024))

        down_far = along_z(down_part(1), lambda z: z ^ 1)
        far_kv = seq_permute(after(kv_own, down_term), lambda i: i + 3 if i % 2 else i - 3)
        kv = halo(kv_own, far_kv, *kv_near)
        attn_out, lse = attn_forward(steps, queries[0], kv)
        pair = jnp.concatenate([up_part(1), up_part(3)], axis=0)

    with jax.named_scope("back"):
        found = [
            rows_of(note_row, 4 * SLOT, k * SLOT)
            for k, note_row in enumerate(
                [above[tok : tok + 1], below[tok : tok + 1], across_x[tok : tok + 1], note]
            )
        ]
        all_hits = placing(jnp.concatenate([f[0] for f in found], axis=1), plane * 4 * SLOT)
        all_place = after(merged(all_hits), back)
        sums = dot(all_place, returned.reshape(-1, model), ((0,), (0,)))
        far_sums = sums[: 3 * tok].astype(BF)
        gate_pack = gate_wide[:, 0].reshape(plane, 4 * SLOT).astype(BF)
        far_sums = [far_sums[k * tok : (k + 1) * tok] for k in range(3)]
        *far_sums, gate_pack, pair = lax.optimization_barrier(
            (*far_sums, gate_pack, pair, down_far)
        )[:5]
        from_below = along_z(far_sums[0], lambda z: z + 2)
        from_above = along_z(far_sums[1], lambda z: z - 2)
        from_across = along_z(far_sums[2], lambda z: z + 4)
        ret_gate = plane_exchange(gate_pack)
        total = cotan.astype(F32) + after(sums[3 * tok :], ret_gate)
        total = total + from_below.astype(F32) + from_above.astype(F32) + from_across.astype(F32)
        input_grad = total.astype(BF)


    with jax.named_scope("weight_grads"):
        pair_far = along_z(after(pair, input_grad), lambda z: z ^ 1)
        pair_sum = (up_part(2).astype(F32) + pair_far[256:].astype(F32)).astype(BF)

    with jax.named_scope("attn_bwd"):
        weight_term = dot(attn_out, input_grad, ((0,), (0,))).astype(BF)
        do = dot_nt(after(input_grad, weight_term), out_weight).astype(BF)
        query_grad, terms = attn_backward(steps, queries[0], attn_out, lse, do, kv)

    with jax.named_scope("out_weight"):
        rows = WIDTH // plane
        parts = plane_exchange(weight_term.reshape(plane, rows, model))
        parts, terms = lax.optimization_barrier((parts, terms))
        part = jnp.sum(parts.astype(F32), axis=0)
        part_b = part.astype(BF)
        part_first = part_b
        key_value_terms = halo_terms(terms)
        for k in (1, 2, 3):
            part = part + along_z(part_b, lambda z, k=k: z ^ k).astype(F32)
        part_b = part.astype(BF)
        part = part_b.astype(F32) + along_z(part_b, lambda z: z + 4).astype(F32)
        part = after(part, pair_far)
        whole = jnp.broadcast_to(part.astype(BF)[None], (plane, rows, model))
        out_weight_grad = plane_exchange(whole).reshape(WIDTH, model)
        own_terms, from_far, chip_terms = key_value_terms
        chip_terms = after(chip_terms, part_b)
        from_right = seq_permute(chip_terms[:tok], lambda i: i - 2)
        from_left = seq_permute(chip_terms[tok:], lambda i: i + 2)
        key_value_grad = own_terms + from_far.astype(F32)
        key_value_grad = key_value_grad + from_right.astype(F32) + from_left.astype(F32)
        key_value_grad = key_value_grad.astype(BF)

    with jax.named_scope("last"):
        up_cross = along_z(after(pair_sum, whole), lambda z: z ^ 2)
        same = up_part(0).astype(F32) + pair_far[:256].astype(F32)
        opposite = up_cross.astype(F32)
        first = jnp.where(half == 0, same, opposite).astype(BF)
        second = jnp.where(half == 0, opposite, same).astype(BF)
        up_grad = jnp.concatenate([first, second], axis=1)
        down_own = down_part(0).astype(F32)
        ret_gate = after(ret_gate, part_first).astype(F32).reshape(-1, 1)
        gate_sums = jnp.stack([jnp.sum(jnp.where(h, ret_gate, 0.0), axis=0) for h in all_hits])
        gate_far = after(gate_sums.astype(BF), from_far, from_left, from_right)
        gate_moves = [lambda z: z + 2, lambda z: z - 2, lambda z: z + 4]
        gate_parts = [
            along_z(gate_far[:, k * tok : (k + 1) * tok], move) for k, move in enumerate(gate_moves)
        ]
        gate_sum = gate_sums[:, 3 * tok :]
        for gate_part in gate_parts:
            gate_sum = gate_sum + gate_part.astype(F32)
        down_grad = (after(down_own, part_first) + down_far.astype(F32)).astype(BF)
        gate_grad = gate_sum.T / gates[0].astype(F32)

    return (
        input_grad[None],
        query_grad[None],
        key_value_grad[None, :, :WIDTH],
        key_value_grad[None, :, WIDTH:],
        out_weight_grad,
        up_grad[None],
        down_grad[None],
        gate_grad[None],
    )


def solution(mesh):
    rows = P("dp", "seq", None)
    weights = P("seq", "dp", None)
    return jax.shard_map(
        per_device,
        mesh=mesh,
        in_specs=(rows, rows, rows, P(), rows, rows, rows, weights, weights, rows),
        out_specs=(rows, rows, rows, rows, P(), weights, weights, rows),
        check_vma=False,
    )
```

```python
import functools

import jax
import jax.numpy as jnp
from jax import lax
from jax.experimental import pallas as pl
from jax.experimental.pallas import tpu as pltpu
from jax.sharding import PartitionSpec as P

HEADS = 8
HEAD = 64
SLOT = 8
TOK = 128
WIDTH = HEADS * HEAD
MODEL = 1024
SCALE = HEAD ** (-0.5)
LOW = -1e30
BOTH = ("seq", "dp")
BF = jnp.bfloat16
F32 = jnp.float32


def seq_of(x, zh, y, c):
    return ((x % 4 * 2 + zh) * 4 + y % 4) * 2 + c


PLANES = [[seq_of(x, zh, y, c) for x in range(4) for y in range(4) for c in range(2)] for zh in range(2)]


def along_z(array, move):
    pairs = []
    for x in range(4):
        for y in range(4):
            for c in range(2):
                for z in range(8):
                    to = move(z) % 8
                    pairs.append(
                        (seq_of(x, z // 4, y, c) * 4 + z % 4, seq_of(x, to // 4, y, c) * 4 + to % 4)
                    )
    return lax.ppermute(array, BOTH, pairs)


def seq_permute(array, move):
    size = lax.axis_size("seq")
    pairs = [(i, move(i)) for i in range(size) if 0 <= move(i) < size]
    return lax.ppermute(array, "seq", pairs)


def plane_exchange(array):
    return lax.all_to_all(
        array, "seq", split_axis=0, concat_axis=0, tiled=True, axis_index_groups=PLANES
    )


def after(value, *others):
    return lax.optimization_barrier((value, *others))[0]


def halo_across(array):
    far = seq_permute(array, lambda i: i + 3 if i % 2 else i - 3)
    left = seq_permute(array, lambda i: i + 2)
    right = seq_permute(array, lambda i: i - 2)
    return [far, left, right]


def halo(array, far, left, right):
    other = seq_permute(jnp.concatenate([array, left, right], axis=0), lambda i: i ^ 1)
    rows = array.shape[0]
    return [array, far, left, right] + [other[k * rows : (k + 1) * rows] for k in range(3)]


def halo_terms(terms):
    rows = terms.shape[0] // 7
    other = seq_permute(terms[4 * rows :], lambda i: i ^ 1).astype(F32)
    from_far = seq_permute(terms[rows : 2 * rows], lambda i: i - 3 if i % 2 == 0 else i + 3)
    chip = terms[2 * rows : 4 * rows].astype(F32) + other[rows:]
    return terms[:rows].astype(F32) + other[:rows], from_far, chip.astype(BF)


def halo_steps(seq):
    core = seq % 2
    steps = jnp.stack(
        [
            jnp.int32(0),
            6 * core - 3,
            jnp.int32(-2),
            jnp.int32(2),
            1 - 2 * core,
            -1 - 2 * core,
            3 - 2 * core,
        ]
    ).astype(jnp.int32)
    there = seq + steps
    real = ((there >= 0) & (there < lax.axis_size("seq"))).astype(jnp.int32)
    return jnp.stack([steps, real])


def dot(left, right, dims=((1,), (0,))):
    return lax.dot_general(left, right, (dims, ((), ())), preferred_element_type=F32)


def dot_nt(left, right):
    return dot(left, right, ((1,), (1,)))


def head_lanes(half):
    lane = lax.broadcasted_iota(jnp.int32, (TOK, 2 * HEAD), 1)
    return (lane < HEAD) if half == 0 else (lane >= HEAD)


def within(steps_ref, b, far_axis):
    own = lax.broadcasted_iota(jnp.int32, (TOK, TOK), 1 - far_axis)
    other = lax.broadcasted_iota(jnp.int32, (TOK, TOK), far_axis)
    gap = other + steps_ref[0, b] * TOK - own
    return (jnp.abs(gap) <= 3 * TOK) & (steps_ref[1, b] == 1)


def fwd_kernel(steps_ref, q_ref, *refs):
    kv = refs[:7]
    out_ref, lse_ref = refs[7:9]
    lane = lax.broadcasted_iota(jnp.int32, (TOK, TOK), 1)
    lse_all = jnp.zeros((TOK, TOK), F32)
    masks = [within(steps_ref, b, 1) for b in range(7)]
    for pair in range(HEADS // 2):
        cols = slice(pair * 128, pair * 128 + 128)
        vcols = slice(WIDTH + pair * 128, WIDTH + pair * 128 + 128)
        q_pair = q_ref[:, cols]
        outs = []
        for half in range(2):
            q_head = jnp.where(head_lanes(half), q_pair, jnp.zeros((), BF))
            scores = [
                jnp.where(masks[b], dot_nt(q_head, kv[b][:, cols]) * SCALE, LOW) for b in range(7)
            ]
            top = functools.reduce(jnp.maximum, scores)
            top = jnp.max(top, axis=1, keepdims=True)
            exps = [jnp.exp(s - top) for s in scores]
            total = jnp.sum(functools.reduce(jnp.add, exps), axis=1, keepdims=True)
            inv = 1.0 / total
            acc = jnp.zeros((TOK, 128), F32)
            for b in range(7):
                acc = acc + dot((exps[b] * inv).astype(BF), kv[b][:, vcols])
            outs.append(acc)
            lse_all = jnp.where(lane == 2 * pair + half, top + jnp.log(total), lse_all)
        out_ref[:, cols] = jnp.where(head_lanes(0), outs[0], outs[1]).astype(BF)
    lse_ref[...] = jnp.transpose(lse_all)[0:16]


def bwd_kernel(steps_ref, q_ref, out_ref, lse_ref, do_ref, *refs):
    kv = refs[:7]
    dq_ref, dkv_ref, delta_scr = refs[7:10]
    masks = [within(steps_ref, b, 0) for b in range(7)]
    row = lax.broadcasted_iota(jnp.int32, (16, WIDTH), 0)
    col = lax.broadcasted_iota(jnp.int32, (16, WIDTH), 1)
    pick = ((col >= row * HEAD) & (col < row * HEAD + HEAD)).astype(BF)
    prod = do_ref[...].astype(F32) * out_ref[...].astype(F32)
    high = prod.astype(BF)
    prod = prod - high.astype(F32)
    mid = prod.astype(BF)
    low = (prod - mid.astype(F32)).astype(BF)
    delta_scr[...] = dot_nt(pick, high) + dot_nt(pick, mid) + dot_nt(pick, low)
    for pair in range(HEADS // 2):
        cols = slice(pair * 128, pair * 128 + 128)
        vcols = slice(WIDTH + pair * 128, WIDTH + pair * 128 + 128)
        q_pair = q_ref[:, cols]
        do_pair = do_ref[:, cols]
        q_heads = [jnp.where(head_lanes(h), q_pair, jnp.zeros((), BF)) for h in range(2)]
        do_heads = [jnp.where(head_lanes(h), do_pair, jnp.zeros((), BF)) for h in range(2)]
        dqs = [jnp.zeros((TOK, 128), F32) for _ in range(2)]
        for b in range(7):
            k_pair = kv[b][:, cols]
            v_pair = kv[b][:, vcols]
            dk = jnp.zeros((TOK, 128), F32)
            dv = jnp.zeros((TOK, 128), F32)
            for half in range(2):
                head = 2 * pair + half
                score = dot_nt(k_pair, q_heads[half]) * SCALE - lse_ref[head : head + 1, :]
                prob = jnp.exp(jnp.where(masks[b], score, LOW))
                dprob = dot_nt(v_pair, do_heads[half])
                dscore = (prob * (dprob - delta_scr[head : head + 1, :]) * SCALE).astype(BF)
                dqs[half] = dqs[half] + dot(dscore, k_pair, ((0,), (0,)))
                dk = dk + dot(dscore, q_heads[half])
                dv = dv + dot(prob.astype(BF), do_heads[half])
            rows = slice(b * TOK, b * TOK + TOK)
            dkv_ref[rows, cols] = dk.astype(BF)
            dkv_ref[rows, vcols] = dv.astype(BF)
        dq_ref[:, cols] = jnp.where(head_lanes(0), dqs[0], dqs[1]).astype(BF)


def on_chip(body, outs, n_in, scratch=(), moved=10**5):
    return pl.pallas_call(
        body,
        out_shape=outs,
        in_specs=[pl.BlockSpec(memory_space=pltpu.SMEM)]
        + [pl.BlockSpec(memory_space=pltpu.VMEM)] * (n_in - 1),
        out_specs=[pl.BlockSpec(memory_space=pltpu.VMEM)] * len(outs),
        scratch_shapes=list(scratch),
        compiler_params=pltpu.CompilerParams(vmem_limit_bytes=24 * 1024 * 1024),
        cost_estimate=pl.CostEstimate(flops=10**6, bytes_accessed=moved, transcendentals=10**3),
    )


def attn_forward(steps, q, kv):
    outs = [
        jax.ShapeDtypeStruct((TOK, WIDTH), BF),
        jax.ShapeDtypeStruct((16, TOK), F32),
    ]
    return on_chip(fwd_kernel, outs, 9)(steps, q, *kv)


def attn_backward(steps, q, out, lse, do, kv):
    outs = [
        jax.ShapeDtypeStruct((TOK, WIDTH), BF),
        jax.ShapeDtypeStruct((7 * TOK, 2 * WIDTH), BF),
    ]
    scratch = [pltpu.VMEM((16, TOK), F32)]
    return on_chip(bwd_kernel, outs, 12, scratch)(steps, q, out, lse, do, *kv)


def experts_kernel(
    dp_ref, near_ref, across_ref, own_ref, mine_ref, pack_ref, u2_ref, u3_ref,
    down_ref, back_ref, x_ref, g_ref, act_ref, pg_ref, gate_ref, up_scr, down_scr,
):
    dp = dp_ref[0]

    def place(scr, block, rows, value):
        scr[pl.ds(pl.multiple_of(block * rows, rows), rows), :] = value

    place(up_scr, dp, 256, mine_ref[...])
    place(up_scr, dp ^ 1, 256, pack_ref[0:256])
    place(up_scr, dp ^ 2, 256, u2_ref[...])
    place(up_scr, dp ^ 3, 256, u3_ref[...])
    place(down_scr, dp & 1, 512, down_ref[...])
    place(down_scr, (dp & 1) ^ 1, 512, pack_ref[256:768])

    def tile(i, carry):
        base = pl.multiple_of(i * 256, 256)
        for p in range(8):
            here = pl.ds(base + p * 32, 16)
            there = pl.ds(base + p * 32 + 16, 16)
            near = near_ref[i * 8 + p]
            x_ref[here, :] = near[0:16]
            g_ref[here, :] = near[16:32]
            across = across_ref[i * 8 + p].astype(F32)
            own = own_ref[i * 8 + p].astype(F32)
            x_ref[there, :] = jnp.concatenate([across[0:8], own[0:8]], axis=0).astype(BF)
            g_ref[there, :] = jnp.concatenate([across[8:16], own[8:16]], axis=0).astype(BF)
        rows = pl.ds(base, 256)
        pre = dot(x_ref[rows, :], up_scr[...])
        act_grad = dot_nt(g_ref[rows, :], down_scr[...])
        sig = 1.0 / (1.0 + jnp.exp(-pre))
        act = (pre * sig).astype(BF)
        act_ref[rows, :] = act
        gate = jnp.sum(act.astype(F32) * act_grad, axis=1, keepdims=True)
        gate_ref[rows, :] = jnp.broadcast_to(gate, (256, 128))
        pg_ref[rows, :] = (act_grad * (sig * (1.0 + pre * (1.0 - sig)))).astype(BF)
        back_ref[rows, :] = dot_nt(pg_ref[rows, :], up_scr[...]).astype(BF)
        return carry

    lax.fori_loop(0, 4, tile, 0)


def experts(dp, near, across, own, mine, pack, up_two, up_three, down):
    big = jax.ShapeDtypeStruct((1024, MODEL), BF)
    ins = [near, across, own, mine, pack, up_two, up_three, down]
    return pl.pallas_call(
        experts_kernel,
        out_shape=[big] * 5 + [jax.ShapeDtypeStruct((1024, 128), F32)],
        in_specs=[pl.BlockSpec(memory_space=pltpu.SMEM)]
        + [pl.BlockSpec(memory_space=pltpu.VMEM)] * len(ins),
        out_specs=[pl.BlockSpec(memory_space=pltpu.VMEM)] * 6,
        scratch_shapes=[pltpu.VMEM((1024, MODEL), BF)] * 2,
        compiler_params=pltpu.CompilerParams(vmem_limit_bytes=40 * 1024 * 1024),
        cost_estimate=pl.CostEstimate(
            flops=6 * 10**9, bytes_accessed=20 * 10**6, transcendentals=10**6
        ),
    )(dp.reshape(1), *ins)


def per_device(
    queries, keys, values, out_weight, ffn_input, routes, gates, up_weight, down_weight, out_grad
):
    seq = lax.axis_index("seq")
    dp = lax.axis_index("dp")
    z_hi = (seq // 8) % 2
    tok, model = ffn_input.shape[1:]
    n_seq = lax.axis_size("seq")
    plane = n_seq // 2
    frames = ffn_input[0]
    cotan = out_grad[0]

    with jax.named_scope("attn_kv"):
        kv_own = jnp.concatenate([keys[0], values[0]], axis=1)

    with jax.named_scope("meta"):
        chosen = routes[0].T.reshape(1, 2 * tok)
        named = chosen == jnp.arange(n_seq, dtype=jnp.int32)[:, None]
        order = jnp.arange(2 * tok)
        before = (order[:, None] < order[None, :]).astype(BF)
        counts = dot(named.astype(BF), before)
        rank = jnp.sum(jnp.where(named, counts, 0.0), axis=0, keepdims=True)
        note = jnp.concatenate(
            [
                chosen.astype(BF),
                rank.astype(BF),
                gates[0].T.reshape(1, 2 * tok),
                jnp.zeros((1, 2 * tok), BF),
            ],
            axis=1,
        )
        payload = jnp.concatenate([frames, note, jnp.zeros((15, model), BF), cotan], axis=0)
    n_x = tok + 16
    with jax.named_scope("tokens_z"):
        above = along_z(payload, lambda z: z - 2)
        below = along_z(payload, lambda z: z + 2)
        across_x = along_z(above[:n_x], lambda z: z - 2)
        across_g = along_z(below[n_x:], lambda z: z + 2)

    with jax.named_scope("weights_z"):
        half = dp // 2
        up_mine = lax.dynamic_slice(up_weight[0], (0, half * 1024), (256, 1024))
        up_other = lax.dynamic_slice(up_weight[0], (0, (1 - half) * 1024), (256, 1024))
        pack = jnp.concatenate([up_mine, down_weight[0]], axis=0)
        pack, up_other, _, _ = lax.optimization_barrier((pack, up_other, across_x, across_g))
        pack1 = along_z(pack, lambda z: z ^ 1)
        up_two = along_z(up_other, lambda z: z ^ 2)
        up_three = along_z(up_two, lambda z: z ^ 1)

    def rows_of(note_row, stride, offset):
        expert = note_row[0, : 2 * tok].astype(jnp.int32)
        place = (expert // 16) * 8 + expert % 8
        here = (expert // 8) % 2 == z_hi
        row = place * stride + offset + note_row[0, 2 * tok : 4 * tok].astype(jnp.int32)
        row = jnp.where(here, row, -1).reshape(2, tok)
        return row, note_row[0, 4 * tok : 6 * tok].reshape(2, tok)

    def placing(row, total):
        spots = jnp.arange(total, dtype=jnp.int32)[:, None]
        return [spots == row[t][None, :] for t in range(2)]

    def merged(hits, gate=None):
        if gate is None:
            return (hits[0] | hits[1]).astype(BF)
        zero = jnp.zeros((), BF)
        return jnp.where(hits[0], gate[0][None, :], jnp.where(hits[1], gate[1][None, :], zero))

    class Sets:
        def __init__(self, notes, xs, gs):
            n = len(notes)
            self.n = n
            found = [rows_of(note_row, n * SLOT, k * SLOT) for k, note_row in enumerate(notes)]
            self.hits = placing(jnp.concatenate([f[0] for f in found], axis=1), plane * n * SLOT)
            self.gate = jnp.concatenate([f[1] for f in found], axis=1)
            self.x = xs[0] if n == 1 else jnp.concatenate(xs, axis=0)
            self.g = gs[0] if n == 1 else jnp.concatenate(gs, axis=0)

        def packed(self):
            shape = (plane, self.n * SLOT, model)
            send_x = dot(merged(self.hits), self.x).astype(BF).reshape(shape)
            send_g = dot(merged(self.hits, self.gate), self.g).astype(BF).reshape(shape)
            return jnp.concatenate([send_x, send_g], axis=1)

    with jax.named_scope("out_own"):
        own = Sets([note], [frames], [cotan])
        got_own = plane_exchange(own.packed())
    with jax.named_scope("out_near"):
        near = Sets(
            [above[tok : tok + 1], below[tok : tok + 1]],
            [above[:tok], below[:tok]],
            [above[n_x:], below[n_x:]],
        )
        got_near = plane_exchange(after(near.packed(), got_own, pack, up_other))
    with jax.named_scope("attn_fwd"):
        steps = halo_steps(seq)
        kv_near = halo_across(after(kv_own, up_two))
        kv = halo(kv_own, *kv_near)
        attn_out, lse = attn_forward(steps, queries[0], kv)
    with jax.named_scope("out_across"):
        across = Sets([across_x[tok : tok + 1]], [across_x[:tok]], [across_g])
        got_across = plane_exchange(after(across.packed(), got_near))

    with jax.named_scope("experts"):
        pack1, up_three, _ = lax.optimization_barrier((pack1, up_three, got_across))
        back, x_rows, g_rows, act, pre_grad, gate_wide = experts(
            dp, got_near, got_across, got_own, up_mine, pack1, up_two, up_three,
            down_weight[0],
        )

        back = after(back, *kv_near)

    with jax.named_scope("back"):
        returned = plane_exchange(back.reshape(plane, 4 * SLOT, model))

    with jax.named_scope("weight_grads"):
        down_term = dot(act, g_rows, ((0,), (0,))).astype(BF)
        up_term = dot(x_rows, pre_grad, ((0,), (0,))).astype(BF)

        def down_part(j):
            return lax.dynamic_slice(down_term, (((dp ^ j) % 2) * 512, 0), (512, model))

        def up_part(j):
            return lax.dynamic_slice(up_term, ((dp ^ j) * 256, 0), (256, 1024))

        down_far = along_z(down_part(1), lambda z: z ^ 1)
        pair = jnp.concatenate([up_part(1), up_part(3)], axis=0)

    with jax.named_scope("back"):
        found = [
            rows_of(note_row, 4 * SLOT, k * SLOT)
            for k, note_row in enumerate(
                [above[tok : tok + 1], below[tok : tok + 1], across_x[tok : tok + 1], note]
            )
        ]
        all_hits = placing(jnp.concatenate([f[0] for f in found], axis=1), plane * 4 * SLOT)
        all_place = after(merged(all_hits), back)
        sums = dot(all_place, returned.reshape(-1, model), ((0,), (0,)))
        far_sums = sums[: 3 * tok].astype(BF)
        gate_pack = gate_wide[:, 0].reshape(plane, 4 * SLOT).astype(BF)
        far_sums = [far_sums[k * tok : (k + 1) * tok] for k in range(3)]
        *far_sums, gate_pack, pair = lax.optimization_barrier(
            (*far_sums, gate_pack, pair, down_far)
        )[:5]
        from_below = along_z(far_sums[0], lambda z: z + 2)
        from_above = along_z(far_sums[1], lambda z: z - 2)
        from_across = along_z(far_sums[2], lambda z: z + 4)
        ret_gate = plane_exchange(gate_pack)
        total = cotan.astype(F32) + after(sums[3 * tok :], ret_gate)
        total = total + from_below.astype(F32) + from_above.astype(F32) + from_across.astype(F32)
        input_grad = total.astype(BF)


    with jax.named_scope("weight_grads"):
        pair_far = along_z(after(pair, input_grad), lambda z: z ^ 1)
        pair_sum = (up_part(2).astype(F32) + pair_far[256:].astype(F32)).astype(BF)

    with jax.named_scope("attn_bwd"):
        weight_term = dot(attn_out, input_grad, ((0,), (0,))).astype(BF)
        do = dot_nt(after(input_grad, weight_term), out_weight).astype(BF)
        query_grad, terms = attn_backward(steps, queries[0], attn_out, lse, do, kv)

    with jax.named_scope("out_weight"):
        rows = WIDTH // plane
        parts = plane_exchange(weight_term.reshape(plane, rows, model))
        parts, terms = lax.optimization_barrier((parts, terms))
        part = jnp.sum(parts.astype(F32), axis=0)
        part_b = part.astype(BF)
        part_first = part_b
        key_value_terms = halo_terms(terms)
        for k in (1, 2, 3):
            part = part + along_z(part_b, lambda z, k=k: z ^ k).astype(F32)
        part_b = part.astype(BF)
        part = part_b.astype(F32) + along_z(part_b, lambda z: z + 4).astype(F32)
        part = after(part, pair_far)
        whole = jnp.broadcast_to(part.astype(BF)[None], (plane, rows, model))
        out_weight_grad = plane_exchange(whole).reshape(WIDTH, model)
        own_terms, from_far, chip_terms = key_value_terms
        chip_terms = after(chip_terms, part_b)
        from_right = seq_permute(chip_terms[:tok], lambda i: i - 2)
        from_left = seq_permute(chip_terms[tok:], lambda i: i + 2)
        key_value_grad = own_terms + from_far.astype(F32)
        key_value_grad = key_value_grad + from_right.astype(F32) + from_left.astype(F32)
        key_value_grad = key_value_grad.astype(BF)

    with jax.named_scope("last"):
        up_cross = along_z(after(pair_sum, whole), lambda z: z ^ 2)
        same = up_part(0).astype(F32) + pair_far[:256].astype(F32)
        opposite = up_cross.astype(F32)
        first = jnp.where(half == 0, same, opposite).astype(BF)
        second = jnp.where(half == 0, opposite, same).astype(BF)
        up_grad = jnp.concatenate([first, second], axis=1)
        down_own = down_part(0).astype(F32)
        ret_gate = after(ret_gate, part_first).astype(F32).reshape(-1, 1)
        gate_sums = jnp.stack([jnp.sum(jnp.where(h, ret_gate, 0.0), axis=0) for h in all_hits])
        gate_far = after(gate_sums.astype(BF), whole)
        gate_moves = [lambda z: z + 2, lambda z: z - 2, lambda z: z + 4]
        gate_parts = [
            along_z(gate_far[:, k * tok : (k + 1) * tok], move) for k, move in enumerate(gate_moves)
        ]
        gate_sum = gate_sums[:, 3 * tok :]
        for gate_part in gate_parts:
            gate_sum = gate_sum + gate_part.astype(F32)
        down_grad = (after(down_own, part_first) + down_far.astype(F32)).astype(BF)
        gate_grad = gate_sum.T / gates[0].astype(F32)

    return (
        input_grad[None],
        query_grad[None],
        key_value_grad[None, :, :WIDTH],
        key_value_grad[None, :, WIDTH:],
        out_weight_grad,
        up_grad[None],
        down_grad[None],
        gate_grad[None],
    )


def solution(mesh):
    rows = P("dp", "seq", None)
    weights = P("seq", "dp", None)
    return jax.shard_map(
        per_device,
        mesh=mesh,
        in_specs=(rows, rows, rows, P(), rows, rows, rows, weights, weights, rows),
        out_specs=(rows, rows, rows, rows, P(), weights, weights, rows),
        check_vma=False,
    )
```
